32 devices in a mesh: dp: 8 (over y, x, core), expert: 4 (over z).
Axes of the slice: x: 2, y: 2, z: 4, core: 2. Of those that a mesh axis runs over, the one named last changes fastest.
Arguments:
- tokens: bfloat16 [24576, 1152], P(('dp', 'expert')), may hold values from -6 to 6
- cotangent: bfloat16 [24576, 1152], P(('dp', 'expert')), may hold values from -6 to 6
- routes: int32 [24576, 1], P(('dp', 'expert')), may hold values from 0 to 3; in each aligned block of 768 rows (0 to 767, 768 to 1535, ...) at most 480 rows name the same one
- starts: int32 [24576], P(('dp', 'expert')), may hold values from 0 to 1, as said below
- input_proj: bfloat16 [1152, 4608], P(None, 'dp'), may hold values from -0.1875 to 0.1875
- conv_kernel: bfloat16 [4, 2304], P(None, 'dp'), may hold values from -3 to 3
- conv_bias: bfloat16 [2304], P('dp'), may hold values from -3 to 3
- select_proj: bfloat16 [2304, 104], P('dp'), may hold values from -0.125 to 0.125
- step_proj: bfloat16 [72, 2304], P(None, 'dp'), may hold values from -0.75 to 0.75
- step_bias: bfloat16 [2304], P('dp'), may hold values from -9 to -2.5
- decay_log: bfloat16 [2304, 16], P('dp'), may hold values from -1.1953125 to 2.796875
- skip_gain: bfloat16 [2304], P('dp'), may hold values from 0.5 to 1.5
- output_proj: bfloat16 [2304, 1152], P('dp'), may hold values from -0.375 to 0.375
- norm_gain: bfloat16 [1152], P('dp'), may hold values from 0.5 to 1.5
- ffn_gain: bfloat16 [1152], P('dp'), may hold values from 0.5 to 1.5
- router: bfloat16 [1152, 4], P('dp'), may hold values from -0.19921875 to 0.19921875
- expert_up: bfloat16 [4, 1152, 3072], P('expert', None, 'dp'), may hold values from -0.1875 to 0.1875
- expert_down: bfloat16 [4, 3072, 1152], P('expert', 'dp'), may hold values from -0.875 to 0.875
Outputs:
- output: bfloat16 [24576, 1152], P(('dp', 'expert'))
- grad_tokens: bfloat16 [24576, 1152], P(('dp', 'expert'))
- grad_input_proj: float32 [1152, 4608], P(None, 'dp')
- grad_conv_kernel: float32 [4, 2304], P(None, 'dp')
- grad_conv_bias: float32 [2304], P('dp')
- grad_select_proj: float32 [2304, 104], P('dp')
- grad_step_proj: float32 [72, 2304], P(None, 'dp')
- grad_step_bias: float32 [2304], P('dp')
- grad_decay_log: float32 [2304, 16], P('dp')
- grad_skip_gain: float32 [2304], P('dp')
- grad_output_proj: float32 [2304, 1152], P('dp')
- grad_norm_gain: float32 [1152], P('dp')
- grad_ffn_gain: float32 [1152], P('dp')
- grad_router: float32 [1152, 4], P('dp')
- grad_expert_up: float32 [4, 1152, 3072], P('expert', None, 'dp')
- grad_expert_down: float32 [4, 3072, 1152], P('expert', 'dp')
The draws below stay inside these ranges and needn't reach their ends.
Inputs may be any that keep to these rules, and one draw needn't show every extreme that they name: `routes`: in the 768 rows of one device no expert is named more than 480 times, and in every draw some device names some expert exactly 480 times, more than its 384 slots. The first token of every aligned run of 3072 tokens has starts = 1. In each such run one sequence begins within its first 384 tokens and ends within its last 384 tokens; the others are short.
All inputs are finite; a program needn't handle non-finite values.
Results may differ from the reference program's by a relative error of at most 0.02.
Values may be sent and summed in bfloat16 or wider, within the bound.
A program may use at most 320 MiB of HBM per device.

```python
import math
from functools import partial
import jax
import jax.numpy as jnp
import numpy as np
from jax import lax

D = 1152
E = 2304
RANK = 72
STATE = 16
KERNEL = 4
FF = 3072
BLK = 32
TOK_DEV = 768
EXPERTS = 4
GROUP = 3072
TOKENS = 24576
CAP = 384
MOST = 480
N_DP = 8
N_EXPERT = 4


def draw_starts(key, part):
    first, second, third = jax.random.split(key, 3)
    half = max(TOK_DEV // 2, 2)
    runs = TOKENS // GROUP
    head = jax.random.randint(first, (runs,), 1, half)
    tail = jax.random.randint(second, (runs,), 1, half)
    extra = jax.random.randint(third, (TOKENS,), 0, 48) == 0
    index = jnp.arange(TOKENS, dtype=jnp.int32)
    place = index % GROUP
    owner = index // GROUP
    head_at = head[owner]
    tail_at = GROUP - tail[owner]
    inside = (place < head_at) | (place > tail_at)
    flags = (place == 0) | (place == head_at) | (place == tail_at) | extra & inside
    return flags.astype(jnp.int32)


def levels(stream_key, extent, cuts, least, largest):
    loudness, own = 1.0, jax.random.fold_in(stream_key, 6)
    for dim, blocks in cuts:
        steps = jnp.exp(jax.random.uniform(jax.random.fold_in(own, dim), (blocks,), jnp.float32, least / len(cuts), largest / len(cuts)))
        loudness = loudness * jnp.repeat(steps, extent[dim] // blocks).reshape([-1 if axis == dim else 1 for axis in range(len(extent))])
    return loudness


def shared_out(own_key, own, number, rows, count, top, bound, skew):
    sequence = jax.random.permutation(own_key, count)
    packed, usual = shares(count, rows * top, bound, skew, True), shares(count, rows * top, bound, skew, False)
    places = jnp.arange(count)

    def named(sizes, rotation):
        used = int((sizes > 0).sum())
        fixed = max(1, used // 4)
        passed = fixed + (places - fixed + rotation * (used - fixed)) % max(1, count - fixed)
        return jnp.zeros((count,), jnp.int32).at[sequence[jnp.where(places < fixed, places, passed)]].set(jnp.asarray(sizes, jnp.int32))

    sizes = jnp.where(number % 4 == 0, named(packed, number // 4), named(usual, number - number // 4 - 1))
    mixed = jax.random.permutation(jax.random.fold_in(own, 3), count)
    source_of, taker = mixed[0:count // 2 * 2:2], mixed[1:count // 2 * 2:2]
    room = jnp.minimum(sizes[source_of] - 1, bound - sizes[taker]) // 2
    room = jnp.where((source_of == sequence[0]) | (taker == sequence[0]) | (sizes[taker] == 0), 0, jnp.maximum(room, 0))
    passed = jax.random.randint(jax.random.fold_in(own, 4), (count // 2,), 0, 1 << 20) % (room + 1)
    sizes = sizes.at[source_of].add(-passed).at[taker].add(passed)
    members = jnp.searchsorted(jnp.cumsum(sizes), jnp.arange(rows * top), side="right").astype(jnp.int32)
    grid = members.reshape(top, rows).T
    grid = grid[jax.random.permutation(jax.random.fold_in(own, 1), rows)]
    rotation = jax.random.randint(jax.random.fold_in(own, 2), (rows, 1), 0, top)
    return jnp.take_along_axis(grid, (jnp.arange(top)[None, :] + rotation) % top, axis=1)


def shares(amount, total, bound, skew, full):
    loads = [(1 << 20) // math.isqrt(rank ** skew) + 1 for rank in range(1, amount + 1)]
    largest = bound if full else min(bound, max(-(-total // amount), total * loads[0] // sum(loads)))
    least = 1 if total - largest >= amount - 1 else 0
    given, surplus = [largest] + [least] * (amount - 1), total - largest - least * (amount - 1)
    while surplus > 0:
        movable = [i for i in range(1, amount) if given[i] < largest] or [i for i in range(1, amount) if given[i] < bound]
        mass, remaining = sum([loads[i] for i in movable]), surplus
        for i in movable:
            more = min(bound - given[i], max(1, remaining * loads[i] // mass), surplus)
            given[i] = given[i] + more
            surplus = surplus - more
    return np.array(given)


def normal_values(own_key, dims, spread, bound, cuts=(), held_as=jnp.bfloat16):
    array = spread * jax.random.normal(own_key, dims, jnp.float32)
    if cuts:
        array = array * levels(own_key, dims, cuts, -0.22, 0.18)
    return jnp.clip(array, -bound, bound).astype(held_as)


def setup_inputs(seed: int = 0) -> dict:
    keys = jax.random.split(jax.random.key(seed), 19)
    tokens = normal_values(keys[0], (TOKENS, D), 1.0, 6.0, ((0, 32),))
    cotangent = normal_values(keys[1], (TOKENS, D), 1.0, 6.0, ((0, 32),))
    routes_keys = jax.random.split(jax.random.fold_in(keys[2], 1), TOKENS // TOK_DEV)
    routes_turns = jax.random.permutation(jax.random.fold_in(keys[2], 3), TOKENS // TOK_DEV)
    routes = jax.vmap(lambda own, number: shared_out(jax.random.fold_in(keys[2], 2), own, number, TOK_DEV, EXPERTS, 1, MOST, 2))(routes_keys, routes_turns).reshape((TOKENS, 1))
    starts = draw_starts(jax.random.fold_in(keys[18], 71), 0)
    input_proj = normal_values(keys[4], (D, 2 * E), D ** -0.5, 0.1875, ((1, 8),))
    conv_kernel = normal_values(keys[5], (KERNEL, E), 0.5, 3.0, ((1, 8),))
    conv_bias = normal_values(keys[6], (E,), 0.3, 3.0, ((0, 8),))
    select_proj = normal_values(keys[7], (E, RANK + 2 * STATE), E ** -0.5, 0.125, ((0, 8),))
    step_proj = normal_values(keys[8], (RANK, E), RANK ** -0.5, 0.75, ((1, 8),))
    step_bias = jnp.clip(-9.0 + 6.5 * jax.random.uniform(keys[9], (E,), jnp.float32) ** levels(keys[9], (E,), ((0, 8),), -0.2, 0.2), -9.0, -2.5).astype(jnp.bfloat16)
    decay_log = jnp.clip(-1.1953125 + 3.9921875 * jax.random.uniform(keys[10], (E, STATE), jnp.float32) ** levels(keys[10], (E, STATE), ((0, 8),), -0.2, 0.2), -1.1953125, 2.796875).astype(jnp.bfloat16)
    skip_gain = jnp.clip(0.5 + 1.0 * jax.random.uniform(keys[11], (E,), jnp.float32) ** levels(keys[11], (E,), ((0, 8),), -0.2, 0.2), 0.5, 1.5).astype(jnp.bfloat16)
    output_proj = normal_values(keys[12], (E, D), (E // 8) ** -0.5, 0.375, ((0, 8),))
    norm_gain = jnp.clip(1.0 + 0.1 * jax.random.normal(keys[13], (D,), jnp.float32), 0.5, 1.5).astype(jnp.bfloat16)
    ffn_gain = jnp.clip(1.0 + 0.1 * jax.random.normal(keys[14], (D,), jnp.float32), 0.5, 1.5).astype(jnp.bfloat16)
    router = normal_values(keys[15], (D, EXPERTS), (0.7 / D ** 0.5), 0.19921875, ((0, 8),))
    expert_up = normal_values(keys[16], (EXPERTS, D, FF), D ** -0.5, 0.1875, ((0, 4), (2, 8)))
    expert_down = normal_values(keys[17], (EXPERTS, FF, D), (FF // 64) ** -0.5, 0.875, ((0, 4), (1, 8)))
    return {"tokens": tokens, "cotangent": cotangent, "routes": routes, "starts": starts, "input_proj": input_proj, "conv_kernel": conv_kernel, "conv_bias": conv_bias, "select_proj": select_proj, "step_proj": step_proj, "step_bias": step_bias, "decay_log": decay_log, "skip_gain": skip_gain, "output_proj": output_proj, "norm_gain": norm_gain, "ffn_gain": ffn_gain, "router": router, "expert_up": expert_up, "expert_down": expert_down}


@jax.custom_vjp
def low(v):
    return lax.optimization_barrier(v.astype(jnp.bfloat16)).astype(jnp.float32)

@jax.custom_vjp
def low_back(v):
    return v

def low_keep(v):
    return (low(v), None)

def low_pass(kept, grad):
    return (grad,)

def back_keep(v):
    return (v, None)

def back_low(kept, grad):
    return (low(grad),)
low.defvjp(low_keep, low_pass)
low_back.defvjp(back_keep, back_low)
epsilon = 1e-05

def multiply(left, right):
    return jnp.dot(left, right, precision=lax.Precision.HIGHEST, preferred_element_type=jnp.float32)

def rms_norm(values, gain):
    return values * lax.rsqrt(lax.optimization_barrier(jnp.mean(values * values, axis=-1, keepdims=True)) + epsilon) * gain

def gate_probs(normed, weights, chosen):
    logits = jnp.dot(normed, weights, precision=lax.Precision.HIGHEST, preferred_element_type=jnp.float32)
    probs = jax.nn.softmax(logits, axis=-1)
    return lax.optimization_barrier(jnp.sum(probs * chosen, axis=-1))

def scan_block(rate, state, block):
    delta, values, b_coeff, c_coeff, keep = block
    outputs = []
    for step in range(delta.shape[0]):
        decay = jnp.exp(delta[step][:, None] * rate) * keep[step]
        state = decay * state + (delta[step] * values[step])[:, None] * b_coeff[step][None, :]
        outputs.append(lax.optimization_barrier(jnp.sum(state * c_coeff[step][None, :], axis=1)))
    return (state, jnp.stack(outputs))

def run_scan(rate, state, delta, values, b_coeff, c_coeff, keep, width):
    count = delta.shape[0] // width
    blocks = (delta.reshape(count, width, -1), values.reshape(count, width, -1), b_coeff.reshape(count, width, -1), c_coeff.reshape(count, width, -1), keep.reshape(count, width))
    state, outputs = lax.scan(jax.checkpoint(partial(scan_block, rate)), state, blocks)
    return (state, outputs.reshape(delta.shape))

def layer_group(weights, piece):
    input_proj, conv_kernel, conv_bias, select_proj, step_proj, step_bias, decay_log, skip_gain, output_proj, norm_gain, ffn_gain, router, expert_up, expert_down = weights
    hidden, route, start = piece
    normed = low(rms_norm(hidden, norm_gain))
    mixed = low_back(low(multiply(normed, input_proj)))
    conv_in = mixed[:, :E]
    gate_in = mixed[:, E:]
    counts = jnp.cumsum(start).astype(jnp.int32)
    conv_sum = jnp.broadcast_to(conv_bias, (GROUP, E))
    for lag in range(KERNEL):
        if lag == 0:
            conv_sum = conv_sum + conv_kernel[KERNEL - 1] * conv_in
        else:
            earlier = jnp.concatenate([jnp.zeros((lag,), jnp.int32), counts[:GROUP - lag]], 0)
            valid = (counts == earlier).astype(jnp.float32)
            shifted = jnp.concatenate([jnp.zeros((lag, E), jnp.float32), conv_in[:GROUP - lag]], 0)
            conv_sum = conv_sum + valid[:, None] * conv_kernel[KERNEL - 1 - lag] * shifted
    inner = low(jax.nn.silu(conv_sum))
    selected = low_back(multiply(inner, select_proj))
    step_low = low(selected[:, :RANK])
    b_coeff = selected[:, RANK:RANK + STATE]
    c_coeff = selected[:, RANK + STATE:]
    delta = jax.nn.softplus(low_back(multiply(step_low, step_proj) + step_bias))
    rate = -jnp.exp(decay_log)
    keep = 1.0 - start.astype(jnp.float32)
    _, scan_out = run_scan(rate, jnp.zeros((E, STATE), jnp.float32), delta, inner, b_coeff, c_coeff, keep, BLK)
    gated = low((scan_out + skip_gain * inner) * jax.nn.silu(gate_in))
    hidden_one = hidden + low_back(multiply(gated, output_proj))
    norm_two = rms_norm(hidden_one, ffn_gain)
    chosen_int = (route[:, None] == jnp.arange(EXPERTS, dtype=jnp.int32)[None, :]).astype(jnp.int32)
    ranks = jnp.cumsum(chosen_int.reshape(N_EXPERT, TOK_DEV, EXPERTS), axis=1).astype(jnp.int32).reshape(GROUP, EXPERTS) - chosen_int
    slot = lax.optimization_barrier(jnp.sum(ranks * chosen_int, axis=1)).astype(jnp.int32)
    source = (jnp.arange(GROUP, dtype=jnp.int32) // TOK_DEV).astype(jnp.int32)
    target = jnp.where(slot < CAP, route * (N_EXPERT * CAP) + source * CAP + slot, EXPERTS * N_EXPERT * CAP).astype(jnp.int32)
    sending = low_back(low(norm_two))
    buffer = jnp.zeros((EXPERTS * N_EXPERT * CAP + 1, D), jnp.float32).at[target].set(sending)
    rows = buffer[:-1].reshape(EXPERTS, N_EXPERT * CAP, D)
    up_pre = low_back(jnp.einsum('erd,edf->erf', rows, expert_up, precision=lax.Precision.HIGHEST))
    up_act = low(jax.nn.gelu(up_pre))
    expert_out = low_back(low(jnp.einsum('erf,efd->erd', up_act, expert_down, precision=lax.Precision.HIGHEST)))
    padded = jnp.concatenate([expert_out.reshape(EXPERTS * N_EXPERT * CAP, D), jnp.zeros((1, D), jnp.float32)], 0)
    picked = padded[target]
    gate_value = gate_probs(norm_two, router, chosen_int.astype(jnp.float32))
    return hidden_one + gate_value[:, None] * picked

def reference(tokens, cotangent, routes, starts, input_proj, conv_kernel, conv_bias, select_proj, step_proj, step_bias, decay_log, skip_gain, output_proj, norm_gain, ffn_gain, router, expert_up, expert_down):
    weights = tuple((item.astype(jnp.float32) for item in (input_proj, conv_kernel, conv_bias, select_proj, step_proj, step_bias, decay_log, skip_gain, output_proj, norm_gain, ffn_gain, router, expert_up, expert_down)))
    route_pieces = routes[:, 0].reshape(N_DP, GROUP)
    start_pieces = starts.reshape(N_DP, GROUP)

    def forward(hidden, params):

        def group_step(carry, piece):
            return (carry, layer_group(params, piece))
        _, outputs = lax.scan(jax.checkpoint(group_step), jnp.zeros((), jnp.float32), (hidden.reshape(N_DP, GROUP, D), route_pieces, start_pieces))
        return outputs.reshape(N_DP * GROUP, D)
    result, backward = jax.vjp(forward, tokens.astype(jnp.float32), weights)
    grad_tokens, grads = backward(cotangent.astype(jnp.float32))
    return (result.astype(jnp.bfloat16), grad_tokens.astype(jnp.bfloat16), grads[0], grads[1], grads[2], grads[3], grads[4], grads[5], grads[6], grads[7], grads[8], grads[9], grads[10], grads[11], grads[12], grads[13])
```

```python
from functools import partial

import jax
import jax.numpy as jnp
from jax import lax
from jax.experimental import pallas as pl
from jax.experimental.pallas import tpu as pltpu
from jax.sharding import PartitionSpec as P

TC = 16
ROWS = 64
FAR = 1e4
LOG2E = 1.4426950408889634
LN2 = 0.6931471805599453
F32 = jnp.float32
BF16 = jnp.bfloat16


def tiled(x, n):
    return jnp.concatenate([x] * n, axis=1) if n > 1 else x


def folded(x):
    n = x.shape[1] // 128
    out = x[:, :128]
    for i in range(1, n):
        out = out + x[:, i * 128 : (i + 1) * 128]
    return out


def dot(a, b):
    return jnp.dot(a, b, preferred_element_type=F32)


def prepare(s_ref, w_ref, b_ref, st_ref, u_ref, dk_ref, dv_ref, pre_ref=None):
    def block(i, carry):
        r = pl.ds(pl.multiple_of(i * ROWS, ROWS), ROWS)
        pre = dot(s_ref[r, :], w_ref[...]) + b_ref[...].astype(F32)
        delta = jnp.maximum(pre, 0.0) + jnp.log1p(jnp.exp(-jnp.abs(pre)))
        dk = jnp.where(st_ref[r, :] > 0.0, FAR, delta)
        dk_ref[r, :] = dk
        if u_ref is not None:
            dv_ref[r, :] = delta * u_ref[r, :].astype(F32)
        if pre_ref is not None:
            pre_ref[r, :] = pre
        return carry + jnp.sum(dk, axis=0, keepdims=True)

    return lax.fori_loop(
        0, s_ref.shape[0] // ROWS, block, jnp.zeros((1, w_ref.shape[1]), F32)
    )


def end_kernel(s_ref, w_ref, b_ref, st_ref, u_ref, a_ref, bb_ref, end_ref, sum_ref, dk_ref, dv_ref):
    reps = w_ref.shape[1] // 128
    sum_ref[...] = prepare(s_ref, w_ref, b_ref, st_ref, u_ref, dk_ref, dv_ref)
    a = a_ref[...]

    def chunk(c, h):
        t0 = pl.multiple_of(c * TC, TC)
        for i in range(TC):
            f = jnp.exp2(a * dk_ref[pl.ds(t0 + i, 1), :])
            h = f * h + dv_ref[pl.ds(t0 + i, 1), :] * tiled(bb_ref[t0 + i], reps)
        return h

    end_ref[...] = lax.fori_loop(0, s_ref.shape[0] // TC, chunk, jnp.zeros_like(a))


def forward_kernel(
    s_ref, w_ref, b_ref, st_ref, u_ref, z_ref, a_ref, skip_ref, bb_ref, cm_ref, h0_ref,
    g_ref, y_ref, ck_ref, dk_ref, dv_ref, ys_ref, hb0, hb1,
):
    reps = w_ref.shape[1] // 128
    states = a_ref.shape[0]
    chunks = s_ref.shape[0] // TC
    prepare(s_ref, w_ref, b_ref, st_ref, u_ref, dk_ref, dv_ref)
    a = a_ref[...]
    hb1[...] = jnp.zeros_like(hb1)

    def scan(c, h, hb):
        t0 = pl.multiple_of(c * TC, TC)
        ck_ref[c] = h
        for i in range(TC):
            f = jnp.exp2(a * dk_ref[pl.ds(t0 + i, 1), :])
            h = f * h + dv_ref[pl.ds(t0 + i, 1), :] * tiled(bb_ref[t0 + i], reps)
            hb[pl.ds(i * states, states), :] = h.astype(BF16)
        return h

    def emit(c, hb):
        t0 = pl.multiple_of(c * TC, TC)
        ys_ref[pl.ds(t0, TC), :] = dot(cm_ref[c], hb[...])

    def pair(c, h):
        emit(jnp.maximum(2 * c - 1, 0), hb1)
        h = scan(2 * c, h, hb0)
        emit(2 * c, hb0)
        return scan(2 * c + 1, h, hb1)

    lax.fori_loop(0, chunks // 2, pair, h0_ref[...])
    emit(chunks - 1, hb1)

    def finish(i, carry):
        r = pl.ds(pl.multiple_of(i * ROWS, ROWS), ROWS)
        y = ys_ref[r, :] + skip_ref[...].astype(F32) * u_ref[r, :].astype(F32)
        z = z_ref[r, :].astype(F32)
        y_ref[r, :] = y.astype(BF16)
        g_ref[r, :] = (y * (z / (1.0 + jnp.exp(-z)))).astype(BF16)
        return carry

    lax.fori_loop(0, s_ref.shape[0] // ROWS, finish, 0)


def start_kernel(s_ref, w_ref, b_ref, st_ref, dg_ref, z_ref, a_ref, cb_ref, out_ref, dk_ref, dy_ref):
    reps = w_ref.shape[1] // 128
    chunks = s_ref.shape[0] // TC
    prepare(s_ref, w_ref, b_ref, st_ref, None, dk_ref, None)

    def gate(i, carry):
        r = pl.ds(pl.multiple_of(i * ROWS, ROWS), ROWS)
        z = z_ref[r, :].astype(F32)
        dy_ref[r, :] = dg_ref[r, :].astype(F32) * (z / (1.0 + jnp.exp(-z)))
        return carry

    lax.fori_loop(0, s_ref.shape[0] // ROWS, gate, 0)
    a = a_ref[...]

    def chunk(j, grad):
        t0 = pl.multiple_of((chunks - 1 - j) * TC, TC)
        for i in range(TC - 1, -1, -1):
            f = jnp.exp2(a * dk_ref[pl.ds(t0 + i, 1), :])
            lam = grad + dy_ref[pl.ds(t0 + i, 1), :] * tiled(cb_ref[t0 + i], reps)
            grad = f * lam
        return grad

    out_ref[...] = lax.fori_loop(0, chunks, chunk, jnp.zeros_like(a))


def backward_kernel(
    s_ref, w_ref, b_ref, st_ref, u_ref, z_ref, y_ref, dg_ref, a_ref, skip_ref,
    bb_ref, cb_ref, bm_ref, om_ref, ck_ref, g0_ref,
    dz_ref, ds_ref, du_ref, da_ref, dskip_ref, dbc_ref,
    pre_ref, dk_ref, dv_ref, dy_ref, q_ref, p_ref, f_ref, fh_ref, lb_ref, wb_ref, accb_ref, accc_ref,
):
    step = pl.program_id(0)
    reps = w_ref.shape[1] // 128
    states = a_ref.shape[0]
    rows = s_ref.shape[0]
    chunks = rows // TC
    prepare(s_ref, w_ref, b_ref, st_ref, u_ref, dk_ref, dv_ref, pre_ref)

    @pl.when(step == 0)
    def _():
        accb_ref[...] = jnp.zeros_like(accb_ref)
        accc_ref[...] = jnp.zeros_like(accc_ref)

    def gate(i, carry):
        r = pl.ds(pl.multiple_of(i * ROWS, ROWS), ROWS)
        z = z_ref[r, :].astype(F32)
        dg = dg_ref[r, :].astype(F32)
        sig = 1.0 / (1.0 + jnp.exp(-z))
        dy = dg * (z * sig)
        dy_ref[r, :] = dy
        dz_ref[r, :] = (dg * y_ref[r, :].astype(F32) * (sig * (1.0 + z * (1.0 - sig)))).astype(BF16)
        return carry + jnp.sum(dy * u_ref[r, :].astype(F32), axis=0, keepdims=True)

    dskip_ref[...] = lax.fori_loop(0, rows // ROWS, gate, jnp.zeros(dskip_ref.shape, F32))
    a = a_ref[...]

    def chunk(j, carry):
        grad, da = carry
        c = chunks - 1 - j
        t0 = pl.multiple_of(c * TC, TC)
        h = ck_ref[c]
        for i in range(TC):
            f = jnp.exp2(a * dk_ref[pl.ds(t0 + i, 1), :])
            fh = f * h
            h = fh + dv_ref[pl.ds(t0 + i, 1), :] * tiled(bb_ref[t0 + i], reps)
            f_ref[i] = f
            fh_ref[i] = fh
            accc_ref[t0 + i] += folded(dy_ref[pl.ds(t0 + i, 1), :] * h)
        for i in range(TC - 1, -1, -1):
            lam = grad + dy_ref[pl.ds(t0 + i, 1), :] * tiled(cb_ref[t0 + i], reps)
            grad = f_ref[i] * lam
            lb_ref[pl.ds(i * states, states), :] = lam.astype(BF16)
            w = lam * fh_ref[i]
            wb_ref[pl.ds(i * states, states), :] = (w * a).astype(BF16)
            da = da + w * dk_ref[pl.ds(t0 + i, 1), :]
            accb_ref[t0 + i] += folded(lam * dv_ref[pl.ds(t0 + i, 1), :])
        q_ref[pl.ds(t0, TC), :] = dot(bm_ref[c], lb_ref[...])
        p_ref[pl.ds(t0, TC), :] = dot(om_ref[...], wb_ref[...])
        return grad, da

    _, da = lax.fori_loop(0, chunks, chunk, (g0_ref[...], jnp.zeros_like(a)))
    da_ref[...] = da * a * LN2

    def finish(i, carry):
        r = pl.ds(pl.multiple_of(i * ROWS, ROWS), ROWS)
        u = u_ref[r, :].astype(F32)
        q = q_ref[r, :]
        pre = pre_ref[r, :]
        delta = jnp.maximum(pre, 0.0) + jnp.log1p(jnp.exp(-jnp.abs(pre)))
        dd = p_ref[r, :] * LN2 + u * q
        ds_ref[r, :] = (dd / (1.0 + jnp.exp(-pre))).astype(BF16)
        du_ref[r, :] = delta * q + dy_ref[r, :] * skip_ref[...].astype(F32)
        return carry

    lax.fori_loop(0, rows // ROWS, finish, 0)

    @pl.when(step == pl.num_programs(0) - 1)
    def _():
        ones = jnp.ones((128, 128), BF16)
        row = lax.broadcasted_iota(jnp.int32, (TC * states, 128), 0) % states
        lane = lax.broadcasted_iota(jnp.int32, (TC * states, 128), 1)

        def gather(c, carry):
            t0 = pl.multiple_of(c * TC, TC)
            b = dot(accb_ref[pl.ds(t0, TC)].reshape(TC * states, 128).astype(BF16), ones)
            d = dot(accc_ref[pl.ds(t0, TC)].reshape(TC * states, 128).astype(BF16), ones)
            both = jnp.where(lane == row, b, jnp.where(lane == row + states, d, 0.0))
            dbc_ref[pl.ds(t0, TC), :] = dot(om_ref[...], both.astype(BF16)).astype(BF16)
            return carry

        lax.fori_loop(0, chunks, gather, 0)


def scan_width(width, limit):
    n = width // 128
    best = max(d for d in range(1, n + 1) if n % d == 0 and d * 128 <= limit)
    return best * 128


def specs(rows, cb, states, chunks):
    tok = lambda n: pl.BlockSpec((rows, n), lambda k: (0, 0))
    chan = lambda n: pl.BlockSpec((n, cb), lambda k: (0, k))
    full3 = lambda a, b, c: pl.BlockSpec((a, b, c), lambda k: (0, 0, 0), pipeline_mode=pl.Buffered(1))
    ck = pl.BlockSpec((chunks, states, cb), lambda k: (0, 0, k))
    return tok, chan, full3, ck


def params():
    return pltpu.CompilerParams(vmem_limit_bytes=58 * 2**20)


def sds(*a):
    return jax.ShapeDtypeStruct(*a)


def end_states(s, w, b, st, u, a, bb):
    rows, width, states = s.shape[0], w.shape[1], a.shape[0]
    cb = scan_width(width, 768)
    tok, chan, full3, ck = specs(rows, cb, states, rows // TC)
    return pl.pallas_call(
        end_kernel,
        grid=(width // cb,),
        in_specs=[tok(s.shape[1]), chan(w.shape[0]), chan(1), tok(1), chan(rows), chan(states), full3(rows, states, 128)],
        out_specs=[chan(states), chan(1)],
        out_shape=[sds((states, width), F32), sds((1, width), F32)],
        scratch_shapes=[pltpu.VMEM((rows, cb), F32)] * 2,
        compiler_params=params(),
        cost_estimate=pl.CostEstimate(flops=6 * rows * width * states, bytes_accessed=rows * width * 2, transcendentals=rows * width * states),
        name="end_states",
    )(s, w, b, st, u, a, bb)


def forward_scan(s, w, b, st, u, z, a, skip, bb, cm, h0):
    rows, width, states = s.shape[0], w.shape[1], a.shape[0]
    cb = scan_width(width, 768)
    tok, chan, full3, ck = specs(rows, cb, states, rows // TC)
    off = z.shape[1] // cb - width // cb
    return pl.pallas_call(
        forward_kernel,
        grid=(width // cb,),
        in_specs=[tok(s.shape[1]), chan(w.shape[0]), chan(1), tok(1), chan(rows), pl.BlockSpec((rows, cb), lambda k: (0, k + off)), chan(states), chan(1), full3(rows, states, 128), full3(*cm.shape), chan(states)],
        out_specs=[chan(rows), chan(rows), ck],
        out_shape=[sds((rows, width), BF16), sds((rows, width), BF16), sds((rows // TC, states, width), F32)],
        scratch_shapes=[pltpu.VMEM((rows, cb), F32)] * 3 + [pltpu.VMEM((TC * states, cb), BF16)] * 2,
        compiler_params=params(),
        cost_estimate=pl.CostEstimate(flops=9 * rows * width * states, bytes_accessed=rows * width * 12, transcendentals=rows * width * states),
        name="forward_scan",
    )(s, w, b, st, u, z, a, skip, bb, cm, h0)


def start_grads(s, w, b, st, dg, z, a, cb_):
    rows, width, states = s.shape[0], w.shape[1], a.shape[0]
    cb = scan_width(width, 768)
    tok, chan, full3, ck = specs(rows, cb, states, rows // TC)
    off = z.shape[1] // cb - width // cb
    return pl.pallas_call(
        start_kernel,
        grid=(width // cb,),
        in_specs=[tok(s.shape[1]), chan(w.shape[0]), chan(1), tok(1), chan(rows), pl.BlockSpec((rows, cb), lambda k: (0, k + off)), chan(states), full3(rows, states, 128)],
        out_specs=chan(states),
        out_shape=sds((states, width), F32),
        scratch_shapes=[pltpu.VMEM((rows, cb), F32)] * 2,
        compiler_params=params(),
        cost_estimate=pl.CostEstimate(flops=6 * rows * width * states, bytes_accessed=rows * width * 6, transcendentals=rows * width * states),
        name="start_grads",
    )(s, w, b, st, dg, z, a, cb_)


def backward_scan(s, w, b, st, u, z, y, dg, a, skip, bb, cb_, bm, om, ck, g0):
    rows, width, states = s.shape[0], w.shape[1], a.shape[0]
    cb = scan_width(width, 384)
    tok, chan, full3, cks = specs(rows, cb, states, rows // TC)
    off = z.shape[1] // cb - width // cb
    return pl.pallas_call(
        backward_kernel,
        grid=(width // cb,),
        in_specs=[tok(s.shape[1]), chan(w.shape[0]), chan(1), tok(1), chan(rows), pl.BlockSpec((rows, cb), lambda k: (0, k + off)), chan(rows), chan(rows), chan(states), chan(1),
                  full3(rows, states, 128), full3(rows, states, 128), full3(*bm.shape), tok_full(om), cks, chan(states)],
        out_specs=[chan(rows), chan(rows), chan(rows), chan(states), chan(1), pl.BlockSpec((rows, 128), lambda k: (0, 0))],
        out_shape=[sds((rows, width), BF16), sds((rows, width), BF16), sds((rows, width), F32), sds((states, width), F32), sds((1, width), F32), sds((rows, 128), BF16)],
        scratch_shapes=[pltpu.VMEM((rows, cb), F32)] * 6
        + [pltpu.VMEM((TC, states, cb), F32)] * 2
        + [pltpu.VMEM((TC * states, cb), BF16)] * 2
        + [pltpu.VMEM((rows, states, 128), F32)] * 2,
        compiler_params=params(),
        cost_estimate=pl.CostEstimate(flops=25 * rows * width * states, bytes_accessed=rows * width * 24, transcendentals=rows * width * states),
        name="backward_scan",
    )(s, w, b, st, u, z, y, dg, a, skip, bb, cb_, bm, om, ck, g0)


def tok_full(x):
    return pl.BlockSpec(x.shape, lambda k: (0,) * x.ndim)


def spread(coeff):
    return jnp.broadcast_to(coeff[:, :, None], (*coeff.shape, 128))


def block_rows(coeff):
    rows, states = coeff.shape
    mask = jnp.arange(TC * states)[None, None] // states == jnp.arange(TC)[None, :, None]
    return jnp.where(mask, coeff.reshape(rows // TC, 1, TC * states), 0.0).astype(BF16)


epsilon = 1e-05


def shifted(array, axis, by):
    length = lax.axis_size(axis)
    pairs = [(i, i + by) for i in range(length) if 0 <= i + by < length]
    return lax.ppermute(array, axis, pairs)


def entering(through, ends, axis, reverse):
    length, here = (lax.axis_size(axis), lax.axis_index(axis))
    every = lax.all_gather(jnp.stack([through, ends]).astype(BF16), axis)
    state = jnp.zeros_like(ends)
    for k in range(length):
        at = length - 1 - k if reverse else k
        reached = at > here if reverse else at < here
        new = every[at, 0].astype(F32) * state + every[at, 1].astype(F32)
        state = jnp.where(reached, new, state)
    return state


def product_back(left, right):
    return lax.dot_general(left, right, (((1,), (1,)), ((), ())), preferred_element_type=F32)


def contract(left, right):
    return lax.dot_general(left, right, (((0,), (0,)), ((), ())), preferred_element_type=F32)


def silu_slope(values):
    sigma = jax.nn.sigmoid(values)
    return sigma * (1.0 + values * (1.0 - sigma))


def inverse_rms(values):
    return lax.rsqrt(jnp.mean(values * values, axis=-1, keepdims=True) + epsilon)


def gather_small(parts):
    n = lax.axis_size("dp")
    flat = jnp.concatenate([p.reshape(-1) for p, _ in parts])
    size = flat.shape[0]
    padded = -(-size // 1024) * 1024
    flat = jnp.pad(flat, (0, padded - size)).reshape(padded // 128, 128)
    every = lax.all_gather(flat, "dp").reshape(n, padded)
    out, at = [], 0
    for p, dim in parts:
        piece = every[:, at : at + p.size].reshape(n, *p.shape)
        at += p.size
        piece = jnp.moveaxis(piece, 0, dim)
        out.append(piece.reshape(*p.shape[:dim], n * p.shape[dim], *p.shape[dim + 1 :]))
    return out


def scatter_small(parts):
    n = lax.axis_size("dp")
    pieces, shapes = [], []
    for p, dim in parts:
        shape = (*p.shape[:dim], p.shape[dim] // n, *p.shape[dim + 1 :])
        split = p.astype(BF16).reshape(*p.shape[:dim], n, p.shape[dim] // n, *p.shape[dim + 1 :])
        pieces.append(jnp.moveaxis(split, dim, 0).reshape(n, -1))
        shapes.append(shape)
    flat = jnp.concatenate(pieces, axis=1)
    size = flat.shape[1]
    padded = -(-size // 1024) * 1024
    flat = jnp.pad(flat, ((0, 0), (0, padded - size))).reshape(n, padded // 128, 128)
    mine = lax.psum_scatter(flat, "dp", scatter_dimension=0, tiled=True)
    mine = lax.psum(mine, "expert").astype(F32).reshape(-1)
    out, at = [], 0
    for shape in shapes:
        count = 1
        for d in shape:
            count *= d
        out.append(mine[at : at + count].reshape(shape))
        at += count
    return out


def body(
    tokens, cotangent, routes, starts, input_proj, conv_kernel, conv_bias, select_proj, step_proj,
    step_bias, decay_log, skip_gain, output_proj, norm_gain, ffn_gain, router, expert_up, expert_down,
):
    w_input = lax.all_gather(input_proj, "dp", axis=1, tiled=True)
    (
        w_conv, b_conv, w_select, w_step, b_step, w_decay, w_skip, g_norm, g_ffn, w_router,
    ) = gather_small(
        [
            (conv_kernel, 1), (conv_bias, 0), (select_proj, 0), (step_proj, 1), (step_bias, 0),
            (decay_log, 0), (skip_gain, 0), (norm_gain, 0), (ffn_gain, 0), (router, 0),
        ]
    )
    w_output = lax.all_gather(output_proj, "dp", axis=0, tiled=True)
    w_up = lax.all_gather(expert_up[0], "dp", axis=1, tiled=True)
    w_down = lax.all_gather(expert_down[0], "dp", axis=0, tiled=True)
    rows, model = tokens.shape
    groups = lax.axis_size("expert")
    width = w_input.shape[1] // 2
    rank = w_step.shape[0]
    states = w_decay.shape[1]
    taps = w_conv.shape[0]
    capacity = 2 * rows // groups
    conv_f = w_conv.astype(F32)
    norm_f = g_norm.astype(F32)
    ffn_f = g_ffn.astype(F32)
    router_f = w_router.astype(F32)

    route = routes[:, 0]
    chosen = (route[:, None] == jnp.arange(groups, dtype=jnp.int32)[None, :]).astype(F32)
    before = (jnp.arange(rows)[:, None] > jnp.arange(rows)[None, :]).astype(BF16)
    ranks = dot(before, chosen.astype(BF16))
    slot = jnp.sum(ranks * chosen, axis=1).astype(jnp.int32)
    target = jnp.where(slot < capacity, route * capacity + slot, groups * capacity)
    place = (jnp.arange(groups * capacity)[:, None] == target[None, :]).astype(BF16)

    hidden_in = tokens.astype(F32)
    norm_r = inverse_rms(hidden_in)
    norm_low = (hidden_in * norm_r * norm_f).astype(BF16)
    mixed = dot(norm_low, w_input).astype(BF16)
    conv_in = mixed[:, :width]
    flag = starts.astype(F32)
    same = 1.0 - flag
    valid = [jnp.ones((rows,), F32)]
    for lag in range(1, taps):
        moved = jnp.concatenate([jnp.ones((lag - 1,), F32), same[: rows - lag + 1]])
        valid.append(valid[-1] * moved)
    edge = [jnp.ones((), F32)]
    for lag in range(1, taps - 1):
        edge.append(edge[-1] * same[rows - lag])
    edge_keep = jnp.stack(edge[::-1])[:, None]
    tail = (conv_in[rows - taps + 1 :].astype(F32) * edge_keep).astype(BF16)
    before_rows = shifted(tail, "expert", 1)
    extended = jnp.concatenate([before_rows, conv_in], 0).astype(F32)
    conv_sum = jnp.broadcast_to(b_conv.astype(F32), (rows, width))
    for lag in range(taps):
        at = taps - 1 - lag
        conv_sum = conv_sum + valid[lag][:, None] * conv_f[at] * extended[at : at + rows]
    inner_low = jax.nn.silu(conv_sum).astype(BF16)
    selected = dot(inner_low, w_select)
    step_low = selected[:, :rank].astype(BF16)
    b_coeff = selected[:, rank : rank + states]
    c_coeff = selected[:, rank + states :]
    rate2 = -jnp.exp(w_decay.astype(F32)).T * LOG2E
    st = flag[:, None]
    bias2 = b_step[None, :]
    skip2 = w_skip[None, :]
    b_wide, c_wide = spread(b_coeff), spread(c_coeff)
    b_block, c_block = block_rows(b_coeff), block_rows(c_coeff)
    one_block = (jnp.arange(TC * states)[None] // states == jnp.arange(TC)[:, None]).astype(BF16)
    local_end, total = end_states(step_low, w_step, bias2, st, inner_low, rate2, b_wide)
    through = jnp.exp2(rate2 * total)
    start_state = entering(through, local_end, "expert", False)
    gated_low, scanned, marks = forward_scan(
        step_low, w_step, bias2, st, inner_low, mixed, rate2, skip2, b_wide, c_block, start_state
    )
    hidden_one = hidden_in + dot(gated_low, w_output)

    r2 = inverse_rms(hidden_one)
    norm_two = hidden_one * r2 * ffn_f
    logits = jnp.dot(norm_two, router_f, precision=lax.Precision.HIGHEST, preferred_element_type=F32)
    probs = jax.nn.softmax(logits, axis=-1)
    gate_value = jnp.sum(probs * chosen, axis=-1)
    grad_out = cotangent.astype(F32)
    grad_picked = (gate_value[:, None] * grad_out).astype(BF16)

    def exchange(x):
        return lax.all_to_all(
            x.reshape(groups, capacity, model), "expert", split_axis=0, concat_axis=0, tiled=True
        ).reshape(groups * capacity, model)

    arrived = exchange(dot(place, norm_two.astype(BF16)).astype(BF16))
    grad_arrived = exchange(dot(place, grad_picked).astype(BF16))
    up_pre = dot(arrived, w_up)
    up_low = jax.nn.gelu(up_pre).astype(BF16)
    returned = exchange(dot(up_low, w_down).astype(BF16))
    _, gelu_back = jax.vjp(jax.nn.gelu, up_pre)
    grad_pre = gelu_back(product_back(grad_arrived, w_down))[0].astype(BF16)
    grad_sent = exchange(product_back(grad_pre, w_up).astype(BF16))
    grad_down = contract(up_low, grad_arrived)
    grad_up = contract(arrived, grad_pre)
    sum_up = lax.psum_scatter(grad_up.astype(BF16), "dp", scatter_dimension=1, tiled=True)
    sum_down = lax.psum_scatter(grad_down.astype(BF16), "dp", scatter_dimension=0, tiled=True)

    picked = contract(place, returned)
    output = (hidden_one + gate_value[:, None] * picked).astype(BF16)
    grad_gate = jnp.sum(grad_out * picked, axis=1)
    grad_logits = probs * (grad_gate[:, None] * chosen - (grad_gate * gate_value)[:, None])
    grad_router = lax.dot_general(
        norm_two, grad_logits, (((0,), (0,)), ((), ())),
        precision=lax.Precision.HIGHEST, preferred_element_type=F32,
    )
    grad_norm_two = contract(place, grad_sent) + lax.dot_general(
        grad_logits, router_f, (((1,), (1,)), ((), ())),
        precision=lax.Precision.HIGHEST, preferred_element_type=F32,
    )
    grad_ffn_gain = jnp.sum(grad_norm_two * hidden_one * r2, axis=0)
    scaled = ffn_f * grad_norm_two
    grad_hidden = (
        grad_out
        + r2 * scaled
        - hidden_one * (r2 * r2 * r2) * jnp.mean(hidden_one * scaled, axis=-1, keepdims=True)
    )

    grad_mixer = grad_hidden.astype(BF16)
    grad_output_w = contract(gated_low, grad_mixer)
    sum_output = lax.psum_scatter(grad_output_w.astype(BF16), "dp", scatter_dimension=0, tiled=True)
    grad_gated = product_back(grad_mixer, w_output)
    start_grad = start_grads(step_low, w_step, bias2, st, grad_gated, mixed, rate2, c_wide)
    later_grad = entering(through, start_grad, "expert", True)
    grad_gate_in, grad_pre_step, grad_inner, grad_decay_t, grad_skip, grad_bc = backward_scan(
        step_low, w_step, bias2, st, inner_low, mixed, scanned, grad_gated, rate2, skip2,
        b_wide, c_wide, b_block, one_block, marks, later_grad,
    )
    grad_step_bias = jnp.sum(grad_pre_step.astype(F32), axis=0)
    grad_step_w = contract(step_low, grad_pre_step)
    grad_step_low = product_back(grad_pre_step, w_step).astype(BF16)
    grad_selected = jnp.concatenate([grad_step_low, grad_bc[:, : 2 * states]], 1)
    grad_select_w = contract(inner_low, grad_selected)
    grad_conv = (grad_inner + product_back(grad_selected, w_select)) * silu_slope(conv_sum)
    grad_conv_b = jnp.sum(grad_conv, axis=0)
    grad_extended = jnp.zeros((rows + taps - 1, width), F32)
    kernel_rows = []
    for lag in range(taps):
        at = taps - 1 - lag
        weighted = valid[lag][:, None] * grad_conv
        kernel_rows.append(jnp.sum(weighted * extended[at : at + rows], axis=0))
        grad_extended = grad_extended + jnp.pad(weighted * conv_f[at], ((at, lag), (0, 0)))
    grad_kernel = jnp.stack(kernel_rows[::-1])
    returned_edge = shifted(grad_extended[: taps - 1], "expert", -1)
    grad_conv_in = grad_extended[taps - 1 :].at[rows - taps + 1 :].add(returned_edge * edge_keep)
    grad_mixed = jnp.concatenate([grad_conv_in.astype(BF16), grad_gate_in], 1)
    grad_input_w = contract(norm_low, grad_mixed)
    sum_input = lax.psum_scatter(grad_input_w.astype(BF16), "dp", scatter_dimension=1, tiled=True)
    grad_norm_one = product_back(grad_mixed, w_input)
    grad_norm_gain = jnp.sum(grad_norm_one * hidden_in * norm_r, axis=0)
    scaled_one = norm_f * grad_norm_one
    grad_tokens = (
        grad_hidden
        + norm_r * scaled_one
        - hidden_in * (norm_r * norm_r * norm_r) * jnp.mean(hidden_in * scaled_one, axis=-1, keepdims=True)
    ).astype(BF16)
    (
        sum_kernel, sum_conv_b, sum_select, sum_step, sum_step_b, sum_decay, sum_skip, sum_norm, sum_ffn, sum_router,
    ) = scatter_small(
        [
            (grad_kernel, 1), (grad_conv_b, 0), (grad_select_w, 0), (grad_step_w, 1), (grad_step_bias, 0),
            (grad_decay_t.T, 0), (grad_skip[0], 0), (grad_norm_gain, 0), (grad_ffn_gain, 0), (grad_router, 0),
        ]
    )
    sum_input = lax.psum(sum_input, "expert").astype(F32)
    sum_output = lax.psum(sum_output, "expert").astype(F32)
    return (
        output, grad_tokens, sum_input, sum_kernel, sum_conv_b, sum_select, sum_step, sum_step_b,
        sum_decay, sum_skip, sum_output, sum_norm, sum_ffn, sum_router,
        sum_up.astype(F32)[None], sum_down.astype(F32)[None],
    )


def solution(mesh):
    placed = (
        P(("dp", "expert"), None),
        P(("dp", "expert"), None),
        P(("dp", "expert"), None),
        P(("dp", "expert")),
        P(None, "dp"),
        P(None, "dp"),
        P("dp"),
        P("dp", None),
        P(None, "dp"),
        P("dp"),
        P("dp", None),
        P("dp"),
        P("dp", None),
        P("dp"),
        P("dp"),
        P("dp", None),
        P("expert", None, "dp"),
        P("expert", "dp", None),
    )
    return jax.shard_map(
        body,
        mesh=mesh,
        in_specs=placed,
        out_specs=(
            P(("dp", "expert"), None),
            P(("dp", "expert"), None),
            P(None, "dp"),
            P(None, "dp"),
            P("dp"),
            P("dp", None),
            P(None, "dp"),
            P("dp"),
            P("dp", None),
            P("dp"),
            P("dp", None),
            P("dp"),
            P("dp"),
            P("dp", None),
            P("expert", None, "dp"),
            P("expert", "dp", None),
        ),
        check_vma=False,
    )
```

```python
from functools import partial

import jax
import jax.numpy as jnp
from jax import lax
from jax.experimental import pallas as pl
from jax.experimental.pallas import tpu as pltpu
from jax.sharding import PartitionSpec as P

TC = 16
ROWS = 256
CONV_ROWS = 128
PAD = 16
UNROLL = 8
FAR = 1e4
LOG2E = 1.4426950408889634
LN2 = 0.6931471805599453
F32 = jnp.float32
BF16 = jnp.bfloat16


def tiled(x, n):
    return jnp.concatenate([x] * n, axis=1) if n > 1 else x


def folded(x):
    n = x.shape[1] // 128
    out = x[:, :128]
    for i in range(1, n):
        out = out + x[:, i * 128 : (i + 1) * 128]
    return out


def dot(a, b):
    return jnp.dot(a, b, preferred_element_type=F32)


def prepare(s_ref, w_ref, b_ref, st_ref, u_ref, dk_ref, dv_ref, pre_ref=None):
    size = min(s_ref.shape[0], ROWS)

    def block(i, carry):
        r = pl.ds(pl.multiple_of(i * size, size), size)
        pre = dot(s_ref[r, :], w_ref[...]) + b_ref[...].astype(F32)
        delta = jnp.maximum(pre, 0.0) + jnp.log1p(jnp.exp(-jnp.abs(pre)))
        dk = jnp.where(st_ref[r, :] > 0.0, FAR, delta)
        dk_ref[r, :] = dk
        if u_ref is not None:
            dv_ref[r, :] = delta * u_ref[r, :].astype(F32)
        if pre_ref is not None:
            pre_ref[r, :] = pre
        return carry + jnp.sum(dk, axis=0, keepdims=True)

    return lax.fori_loop(
        0, s_ref.shape[0] // size, block, jnp.zeros((1, w_ref.shape[1]), F32)
    )


def end_kernel(s_ref, w_ref, b_ref, st_ref, u_ref, a_ref, bb_ref, low_ref, dk_ref, dv_ref, out_ref):
    reps = w_ref.shape[1] // 128
    states = a_ref.shape[0]
    first = pl.program_id(1) == 0
    total = prepare(s_ref, w_ref, b_ref, st_ref, u_ref, dk_ref, dv_ref)
    a = a_ref[...]

    @pl.when(first)
    def _():
        out_ref[...] = jnp.zeros_like(out_ref)

    def chunk(c, h):
        t0 = pl.multiple_of(c * TC, TC)
        for i in range(TC):
            f = jnp.exp2(a * dk_ref[pl.ds(t0 + i, 1), :])
            h = f * h + dv_ref[pl.ds(t0 + i, 1), :] * tiled(bb_ref[t0 + i], reps)
        return h

    out_ref[:states, :] = lax.fori_loop(0, s_ref.shape[0] // TC, chunk, out_ref[:states, :])
    out_ref[states : states + 1, :] += total

    @pl.when(pl.program_id(1) == pl.num_programs(1) - 1)
    def _():
        low_ref[:states, :] = out_ref[:states, :].astype(BF16)
        sums = out_ref[states : states + 1, :]
        high = sums.astype(BF16).astype(F32)
        row = lax.broadcasted_iota(jnp.int32, (states, sums.shape[1]), 0)
        both = jnp.where(row == 0, high, jnp.where(row == 1, sums - high, 0.0))
        low_ref[states:, :] = both.astype(BF16)


def forward_kernel(
    s_ref, w_ref, b_ref, st_ref, u_ref, z_ref, a_ref, skip_ref, bb_ref, cm_ref, h0_ref,
    g_ref, y_ref, hs_ref, ck_ref, dk_ref, dv_ref, ys_ref, h_ref,
):
    reps = w_ref.shape[1] // 128
    states = a_ref.shape[0]
    chunks = s_ref.shape[0] // TC
    prepare(s_ref, w_ref, b_ref, st_ref, u_ref, dk_ref, dv_ref)
    a = a_ref[...]

    @pl.when(pl.program_id(1) == 0)
    def _():
        h_ref[...] = h0_ref[...]

    def scan(c, h):
        t0 = pl.multiple_of(c * TC, TC)
        r0 = pl.multiple_of(c * TC * states, TC * states)
        ck_ref[c] = h.astype(BF16)
        for i in range(TC):
            f = jnp.exp2(a * dk_ref[pl.ds(t0 + i, 1), :])
            h = f * h + dv_ref[pl.ds(t0 + i, 1), :] * tiled(bb_ref[t0 + i], reps)
            hs_ref[pl.ds(r0 + i * states, states), :] = h.astype(BF16)
        return h

    def emit(c):
        t0 = pl.multiple_of(c * TC, TC)
        r0 = pl.multiple_of(c * TC * states, TC * states)
        ys_ref[pl.ds(t0, TC), :] = dot(cm_ref[c], hs_ref[pl.ds(r0, TC * states), :])

    def group(j, h):
        for m in range(UNROLL):
            h = scan(UNROLL * j + m, h)
            emit(UNROLL * j + m)
        return h

    h_ref[...] = lax.fori_loop(0, chunks // UNROLL, group, h_ref[...])

    size = min(s_ref.shape[0], ROWS)

    def finish(i, carry):
        r = pl.ds(pl.multiple_of(i * size, size), size)
        y = ys_ref[r, :] + skip_ref[...].astype(F32) * u_ref[r, :].astype(F32)
        z = z_ref[r, :].astype(F32)
        y_ref[r, :] = y.astype(BF16)
        g_ref[r, :] = (y * (z / (1.0 + jnp.exp(-z)))).astype(BF16)
        return carry

    lax.fori_loop(0, s_ref.shape[0] // size, finish, 0)


def start_kernel(s_ref, w_ref, b_ref, st_ref, dy_ref, a_ref, cb_ref, low_ref, dk_ref, out_ref):
    reps = w_ref.shape[1] // 128
    chunks = s_ref.shape[0] // TC
    prepare(s_ref, w_ref, b_ref, st_ref, None, dk_ref, None)
    a = a_ref[...]

    @pl.when(pl.program_id(1) == 0)
    def _():
        out_ref[...] = jnp.zeros_like(out_ref)

    def chunk(j, grad):
        t0 = pl.multiple_of((chunks - 1 - j) * TC, TC)
        for i in range(TC - 1, -1, -1):
            f = jnp.exp2(a * dk_ref[pl.ds(t0 + i, 1), :])
            lam = grad + dy_ref[pl.ds(t0 + i, 1), :] * tiled(cb_ref[t0 + i], reps)
            grad = f * lam
        return grad

    out_ref[...] = lax.fori_loop(0, chunks, chunk, out_ref[...])

    @pl.when(pl.program_id(1) == pl.num_programs(1) - 1)
    def _():
        low_ref[...] = out_ref[...].astype(BF16)


def backward_kernel(
    s_ref, w_ref, b_ref, st_ref, u_ref, dy_ref, a_ref, skip_ref, cb_ref, bm_ref, om_ref, hs_ref, ck_ref, g0_ref,
    ds_ref, du_ref, da_ref, dskip_ref, db_ref, dc_ref,
    pre_ref, dk_ref, dv_ref, q_ref, p_ref, lb0, lb1, wb0, wb1, grad_ref, accb_ref, accc_ref,
):
    step, seg = pl.program_id(0), pl.program_id(1)
    last = pl.num_programs(1) - 1 - seg
    reps = w_ref.shape[1] // 128
    states = a_ref.shape[0]
    rows = s_ref.shape[0]
    chunks = rows // TC
    prepare(s_ref, w_ref, b_ref, st_ref, u_ref, dk_ref, dv_ref, pre_ref)
    token0 = pl.multiple_of(last * rows, rows)

    @pl.when((step == 0) & (seg == 0))
    def _():
        accb_ref[...] = jnp.zeros_like(accb_ref)
        accc_ref[...] = jnp.zeros_like(accc_ref)

    @pl.when(seg == 0)
    def _():
        grad_ref[...] = g0_ref[...]
        da_ref[...] = jnp.zeros_like(da_ref)
        dskip_ref[...] = jnp.zeros_like(dskip_ref)

    a = a_ref[...]
    a_low = a.astype(BF16)

    def scan(c, grad, lb, wb):
        t0 = pl.multiple_of(c * TC, TC)
        r0 = pl.multiple_of(c * TC * states, TC * states)
        da, four = None, None
        for i in range(TC - 1, -1, -1):
            d = dk_ref[pl.ds(t0 + i, 1), :]
            f = jnp.exp2(a * d)
            lam = grad + dy_ref[pl.ds(t0 + i, 1), :] * tiled(cb_ref[t0 + i], reps)
            grad = f * lam
            lb[pl.ds(i * states, states), :] = lam.astype(BF16)
            h = ck_ref[c] if i == 0 else hs_ref[pl.ds(r0 + (i - 1) * states, states), :]
            w = grad.astype(BF16) * h
            wb[pl.ds(i * states, states), :] = w * a_low
            wd = w * jnp.broadcast_to(d, w.shape).astype(BF16)
            four = wd if four is None else four + wd
            if i % 4 == 0:
                da = four.astype(F32) if da is None else da + four.astype(F32)
                four = None
            accb_ref[token0 + t0 + i] += folded(lam * dv_ref[pl.ds(t0 + i, 1), :])
        da_ref[...] += da
        return grad

    def emit(c, lb, wb):
        t0 = pl.multiple_of(c * TC, TC)
        r0 = pl.multiple_of(c * TC * states, TC * states)
        q_ref[pl.ds(t0, TC), :] = dot(bm_ref[c], lb[...])
        p_ref[pl.ds(t0, TC), :] = dot(om_ref[...], wb[...])
        accc_ref[last * chunks + c] += lax.dot_general(
            dy_ref[pl.ds(t0, TC), :].astype(BF16), hs_ref[pl.ds(r0, TC * states), :],
            (((1,), (1,)), ((), ())), preferred_element_type=F32,
        )

    def pair(j, grad):
        c = chunks - 1 - 2 * j
        grad = scan(c, grad, lb0, wb0)
        emit(c, lb0, wb0)
        grad = scan(c - 1, grad, lb1, wb1)
        emit(c - 1, lb1, wb1)
        return grad

    grad_ref[...] = lax.fori_loop(0, chunks // 2, pair, grad_ref[...])

    @pl.when(last == 0)
    def _():
        da_ref[...] = da_ref[...] * a * LN2

    size = min(s_ref.shape[0], ROWS)

    def finish(i, carry):
        r = pl.ds(pl.multiple_of(i * size, size), size)
        u = u_ref[r, :].astype(F32)
        q = q_ref[r, :]
        dy = dy_ref[r, :]
        pre = pre_ref[r, :]
        delta = jnp.maximum(pre, 0.0) + jnp.log1p(jnp.exp(-jnp.abs(pre)))
        dd = p_ref[r, :] * LN2 + u * q
        ds_ref[r, :] = (dd / (1.0 + jnp.exp(-pre))).astype(BF16)
        du_ref[r, :] = delta * q + dy * skip_ref[...].astype(F32)
        return carry + jnp.sum(dy * u, axis=0, keepdims=True)

    dskip_ref[...] += lax.fori_loop(0, rows // size, finish, jnp.zeros(dskip_ref.shape, F32))

    @pl.when((step == pl.num_programs(0) - 1) & (last == 0))
    def _():
        ones = jnp.ones((128, 128), BF16)
        row = lax.broadcasted_iota(jnp.int32, (TC * states, 128), 0) % states
        lane = lax.broadcasted_iota(jnp.int32, (TC * states, 128), 1)

        def gather(c, carry):
            t0 = pl.multiple_of(c * TC, TC)
            b = dot(accb_ref[pl.ds(t0, TC)].reshape(TC * states, 128).astype(BF16), ones)
            db_ref[pl.ds(t0, TC), :] = dot(om_ref[...], jnp.where(lane == row, b, 0.0).astype(BF16)).astype(BF16)
            own = om_ref[...].astype(F32) * accc_ref[c]
            dc_ref[c] = jnp.broadcast_to(jnp.sum(own, axis=0, keepdims=True), dc_ref.shape[1:])
            return carry

        lax.fori_loop(0, accc_ref.shape[0], gather, 0)


def conv_kernel_back(xs_ref, du_ref, slope_ref, dp_ref, sel_ref, k_ref, ok_ref, dxs_ref, dk_ref, db_ref, dc_ref):
    taps = k_ref.shape[0]
    rows = du_ref.shape[0]
    k = k_ref[...].astype(F32)
    dc_ref[:PAD, :] = jnp.zeros((PAD, dc_ref.shape[1]), F32)
    dc_ref[pl.ds(rows + PAD, PAD), :] = jnp.zeros((PAD, dc_ref.shape[1]), F32)

    def first(i, carry):
        t0 = pl.multiple_of(i * CONV_ROWS, CONV_ROWS)
        at = pl.ds(t0, CONV_ROWS)
        du = du_ref[at, :] + dot(dp_ref[at, :], sel_ref[...])
        dc = du * slope_ref[at, :].astype(F32)
        dc_ref[pl.ds(t0 + PAD, CONV_ROWS), :] = dc
        slab = xs_ref[pl.ds(t0, CONV_ROWS + PAD), :].astype(F32)
        sums = [jnp.sum(dc, axis=0, keepdims=True)]
        for lag in range(taps):
            x = slab[PAD - lag : PAD - lag + CONV_ROWS]
            part = dc * x
            if lag:
                part = part * ok_ref[pl.ds(t0 + PAD, CONV_ROWS), lag : lag + 1]
            sums.append(jnp.sum(part, axis=0, keepdims=True))
        return tuple(a + b for a, b in zip(carry, sums))

    size = max(n for n in range(PAD, 129, PAD) if (rows + PAD) % n == 0)
    zero = jnp.zeros((1, k.shape[1]), F32)
    sums = lax.fori_loop(0, rows // CONV_ROWS, first, (zero,) * (taps + 1))
    db_ref[...] = sums[0]
    for lag in range(taps):
        dk_ref[taps - 1 - lag : taps - lag, :] = sums[1 + lag]

    def second(i, carry):
        r0 = pl.multiple_of(i * size, PAD)
        slab = dc_ref[pl.ds(r0, size + PAD), :]
        ok = ok_ref[pl.ds(r0, size + PAD), :]
        out = k[taps - 1 : taps] * slab[:size]
        for lag in range(1, taps):
            part = (ok[:, lag : lag + 1] * slab)[lag : lag + size]
            out = out + k[taps - 1 - lag : taps - lag] * part
        dxs_ref[pl.ds(r0, size), :] = out.astype(BF16)
        return carry

    lax.fori_loop(0, (rows + PAD) // size, second, 0)


def conv_back(xs, du, slope, dp, sel, k, ok):
    rows, width = du.shape
    cb = scan_width(width, 768)
    col = lambda n: pl.BlockSpec((n, cb), lambda i: (0, i))
    whole = lambda x: pl.BlockSpec(x.shape, lambda i: (0, 0))
    taps = k.shape[0]
    return pl.pallas_call(
        conv_kernel_back,
        grid=(width // cb,),
        in_specs=[col(rows + PAD), col(rows), col(rows), whole(dp), col(sel.shape[0]), col(taps), whole(ok)],
        out_specs=[col(rows + PAD), col(taps), col(1)],
        out_shape=[sds((rows + PAD, width), BF16), sds((taps, width), F32), sds((1, width), F32)],
        scratch_shapes=[pltpu.VMEM((rows + 2 * PAD, cb), F32)],
        compiler_params=params(),
        cost_estimate=pl.CostEstimate(flops=rows * width * 300, bytes_accessed=rows * width * 8, transcendentals=0),
        name="conv_back",
    )(xs, du, slope, dp, sel, k, ok)


def scan_width(width, limit):
    n = width // 128
    best = max(d for d in range(1, n + 1) if n % d == 0 and d * 128 <= limit)
    return best * 128


def params():
    return pltpu.CompilerParams(vmem_limit_bytes=60 * 2**20)


def sds(*a):
    return jax.ShapeDtypeStruct(*a)


class Blocks:
    def __init__(self, rows, width, cb, parts, reverse=False, first=0):
        self.first = first
        self.grid = (width // cb, parts)
        self.cb, self.rows, self.seg = cb, rows, rows // parts
        self.at = (lambda s: parts - 1 - s) if reverse else (lambda s: s)

    def token(self, n):
        return pl.BlockSpec((self.seg, n), lambda k, s: (self.at(s), 0))

    def channel(self, n):
        return pl.BlockSpec((n, self.cb), lambda k, s: (0, k + self.first))

    def both(self, times=1, off=0):
        return pl.BlockSpec((self.seg * times, self.cb), lambda k, s: (self.at(s), k + self.first + off))

    def lead(self, n, *rest):
        return pl.BlockSpec((n, *rest), lambda k, s: (self.at(s),) + (0,) * len(rest))

    def marks(self, states):
        return pl.BlockSpec((self.seg // TC, states, self.cb), lambda k, s: (self.at(s), 0, k))

    def whole(self, shape):
        return pl.BlockSpec(shape, lambda k, s: (0,) * len(shape))


def estimate(rows, width, states, ops, size):
    return pl.CostEstimate(
        flops=ops * rows * width * states, bytes_accessed=rows * width * size, transcendentals=rows * width * states
    )


END, FORWARD, START, BACKWARD = (1152, 3), (1152, 6), (1152, 3), (2304, 24)


def end_states(s, w, b, st, u, a, bb, part, of):
    rows, width, states = s.shape[0], w.shape[1] // of, a.shape[0]
    cb = min(END[0], width)
    k = Blocks(rows, width, cb, END[1], first=part * (width // cb))
    return pl.pallas_call(
        end_kernel,
        grid=k.grid,
        in_specs=[k.token(s.shape[1]), k.channel(w.shape[0]), k.channel(1), k.token(1), k.both(), k.channel(states), k.lead(k.seg, states, 128)],
        out_specs=pl.BlockSpec((2 * states, cb), lambda i, j: (0, i)),
        out_shape=sds((2 * states, width), BF16),
        scratch_shapes=[pltpu.VMEM((k.seg, k.cb), F32)] * 2 + [pltpu.VMEM((states + 8, k.cb), F32)],
        compiler_params=params(),
        cost_estimate=estimate(rows, width, states, 6, 8),
        name="end_states",
    )(s, w, b, st, u, a, bb)


def forward_scan(s, w, b, st, u, z, a, skip, bb, cm, h0):
    rows, width, states = s.shape[0], w.shape[1], a.shape[0]
    k = Blocks(rows, width, *FORWARD)
    return pl.pallas_call(
        forward_kernel,
        grid=k.grid,
        in_specs=[k.token(s.shape[1]), k.channel(w.shape[0]), k.channel(1), k.token(1), k.both(), k.both(), k.channel(states), k.channel(1),
                  k.lead(k.seg, states, 128), k.lead(k.seg // TC, *cm.shape[1:]), k.channel(states)],
        out_specs=[k.both(), k.both(), k.both(states), k.marks(states)],
        out_shape=[sds((rows, width), BF16), sds((rows, width), BF16), sds((rows * states, width), BF16), sds((rows // TC, states, width), BF16)],
        scratch_shapes=[pltpu.VMEM((k.seg, k.cb), F32)] * 3 + [pltpu.VMEM((states, k.cb), F32)],
        compiler_params=params(),
        cost_estimate=estimate(rows, width, states, 9, 44),
        name="forward_scan",
    )(s, w, b, st, u, z, a, skip, bb, cm, h0)


def start_grads(s, w, b, st, dy, a, cb_wide, part, of):
    rows, width, states = s.shape[0], w.shape[1] // of, a.shape[0]
    cb = min(START[0], width)
    k = Blocks(rows, width, cb, START[1], reverse=True, first=part * (width // cb))
    return pl.pallas_call(
        start_kernel,
        grid=k.grid,
        in_specs=[k.token(s.shape[1]), k.channel(w.shape[0]), k.channel(1), k.token(1), k.both(), k.channel(states), k.lead(k.seg, states, 128)],
        out_specs=pl.BlockSpec((states, cb), lambda i, j: (0, i)),
        out_shape=sds((states, width), BF16),
        scratch_shapes=[pltpu.VMEM((k.seg, k.cb), F32), pltpu.VMEM((states, k.cb), F32)],
        compiler_params=params(),
        cost_estimate=estimate(rows, width, states, 6, 8),
        name="start_grads",
    )(s, w, b, st, dy, a, cb_wide)


def backward_scan(s, w, b, st, u, dy, a, skip, cb, bm, om, hs, ck, g0):
    rows, width, states = s.shape[0], w.shape[1], a.shape[0]
    k = Blocks(rows, width, *BACKWARD, reverse=True)
    chunks = rows // TC
    return pl.pallas_call(
        backward_kernel,
        grid=k.grid,
        in_specs=[k.token(s.shape[1]), k.channel(w.shape[0]), k.channel(1), k.token(1), k.both(), k.both(), k.channel(states), k.channel(1),
                  k.lead(k.seg, states, 128), k.lead(k.seg // TC, *bm.shape[1:]), k.whole(om.shape), k.both(states), k.marks(states), k.channel(states)],
        out_specs=[k.both(), k.both(), k.channel(states), k.channel(1), k.whole((rows, 128)), k.whole((chunks, 8, TC * states))],
        out_shape=[sds((rows, width), BF16), sds((rows, width), F32), sds((states, width), F32), sds((1, width), F32),
                   sds((rows, 128), BF16), sds((chunks, 8, TC * states), F32)],
        scratch_shapes=[pltpu.VMEM((k.seg, k.cb), F32)] * 5
        + [pltpu.VMEM((TC * states, k.cb), BF16)] * 4
        + [pltpu.VMEM((states, k.cb), F32), pltpu.VMEM((rows, states, 128), F32), pltpu.VMEM((chunks, TC, TC * states), F32)],
        compiler_params=params(),
        cost_estimate=estimate(rows, width, states, 18, 44),
        name="backward_scan",
    )(s, w, b, st, u, dy, a, skip, cb, bm, om, hs, ck, g0)


def spread(coeff):
    return jnp.broadcast_to(coeff[:, :, None], (*coeff.shape, 128))


def block_rows(coeff):
    rows, states = coeff.shape
    mask = jnp.arange(TC * states)[None, None] // states == jnp.arange(TC)[None, :, None]
    return jnp.where(mask, coeff.reshape(rows // TC, 1, TC * states), 0.0).astype(BF16)


epsilon = 1e-05
HALVES = 2


def shifted(array, axis, by):
    length = lax.axis_size(axis)
    pairs = [(i, i + by) for i in range(length) if 0 <= i + by < length]
    return lax.ppermute(array, axis, pairs)


def entering(came, sums, rate2):
    state, decay = jnp.zeros_like(rate2), jnp.zeros((1, rate2.shape[1]), F32)
    for end, total in zip(came, sums):
        state = state + jnp.exp2(rate2 * decay) * end.astype(F32)
        decay = decay + total
    return state


def product_back(left, right):
    return lax.dot_general(left, right, (((1,), (1,)), ((), ())), preferred_element_type=F32)


def contract(left, right):
    return lax.dot_general(left, right, (((0,), (0,)), ((), ())), preferred_element_type=F32)


def silu_slope(values):
    sigma = jax.nn.sigmoid(values)
    return sigma * (1.0 + values * (1.0 - sigma))


def inverse_rms(values):
    return lax.rsqrt(jnp.mean(values * values, axis=-1, keepdims=True) + epsilon)


def paired_rows(rows, devices):
    r, d = rows.shape
    split = rows.reshape(r // 2, 2, devices, d // devices)
    return split.transpose(0, 2, 1, 3).reshape(r // 2, 2 * d)


def single_rows(rows, devices):
    r, d = rows.shape
    split = rows.reshape(r, devices, 2, d // (2 * devices))
    return split.transpose(0, 2, 1, 3).reshape(2 * r, d // 2)


def stacked(parts):
    whole = jnp.concatenate([p.astype(BF16) for p in parts], axis=0)
    return jnp.pad(whole, ((0, -whole.shape[0] % 16), (0, 0)))


def cut(whole, counts):
    out, at = [], 0
    for n in counts:
        out.append(whole[at : at + n])
        at += n
    return out


def body(
    tokens, cotangent, routes, starts, input_proj, conv_kernel, conv_bias, select_proj, step_proj,
    step_bias, decay_log, skip_gain, output_proj, norm_gain, ffn_gain, router, expert_up, expert_down,
):
    devices = lax.axis_size("dp")
    groups = lax.axis_size("expert")
    rows, model = tokens.shape
    taps, rank, states = conv_kernel.shape[0], step_proj.shape[0], decay_log.shape[1]
    capacity = 2 * rows // groups
    w_input = lax.all_gather(input_proj, "dp", axis=1, tiled=True)
    small = stacked(
        [
            select_proj.T, step_proj, decay_log.T, conv_kernel, conv_bias[None], step_bias[None], skip_gain[None],
            paired_rows(jnp.concatenate([norm_gain[None], ffn_gain[None], router.T], 0), 1),
        ]
    )
    counts = (select_proj.shape[1], rank, states, taps, 1, 1, 1, (groups + 2) // 2)
    w_select, w_step, w_decay, w_conv, b_conv, bias2, skip2, singles = cut(
        lax.all_gather(small, "dp", axis=1, tiled=True), counts
    )
    singles = single_rows(singles, devices).astype(F32)
    norm_f, ffn_f, router_f = singles[0], singles[1], singles[2:]
    w_output = lax.all_gather(output_proj, "dp", axis=0, tiled=True)
    w_up = lax.all_gather(expert_up[0], "dp", axis=1, tiled=True)
    w_down = lax.all_gather(expert_down[0], "dp", axis=0, tiled=True)
    width = w_select.shape[1]
    conv_f = w_conv.astype(F32)

    route = routes[:, 0]
    chosen = (route[:, None] == jnp.arange(groups, dtype=jnp.int32)[None, :]).astype(F32)
    before = (jnp.arange(rows)[:, None] > jnp.arange(rows)[None, :]).astype(BF16)
    ranks = dot(before, chosen.astype(BF16))
    slot = jnp.sum(ranks * chosen, axis=1).astype(jnp.int32)
    distance = jnp.mod(route - lax.axis_index("expert"), groups)
    target = jnp.where(slot < capacity, distance * capacity + slot, groups * capacity)
    place = (jnp.arange(groups * capacity)[:, None] == target[None, :]).astype(BF16)

    hidden_in = tokens.astype(F32)
    norm_r = inverse_rms(hidden_in)
    norm_own = (hidden_in * norm_r * norm_f).astype(BF16)
    flag = starts.astype(F32)
    same = 1.0 - flag
    valid = [jnp.ones((rows,), F32)]
    for lag in range(1, taps):
        moved = jnp.concatenate([jnp.ones((lag - 1,), F32), same[: rows - lag + 1]])
        valid.append(valid[-1] * moved)
    edge = [jnp.ones((), F32)]
    for lag in range(1, taps - 1):
        edge.append(edge[-1] * same[rows - lag])
    edge_keep = jnp.stack(edge[::-1])[:, None]
    tail = (norm_own[rows - taps + 1 :].astype(F32) * edge_keep).astype(BF16)
    borrowed = shifted(tail, "expert", 1)
    norm_low = jnp.concatenate([jnp.zeros((PAD - taps + 1, model), BF16), borrowed, norm_own], 0)
    mixed = dot(norm_low, w_input).astype(BF16)
    conv_sum = jnp.broadcast_to(b_conv.astype(F32), (rows, width))
    for lag in range(taps):
        conv_sum = conv_sum + valid[lag][:, None] * conv_f[taps - 1 - lag] * mixed[PAD - lag : PAD - lag + rows, :width].astype(F32)
    ok = jnp.pad(jnp.stack(valid, 1), ((PAD, PAD), (0, 0)))
    inner_low = jax.nn.silu(conv_sum).astype(BF16)
    slope_low = silu_slope(conv_sum).astype(BF16)
    selected = product_back(inner_low, w_select)
    step_low = selected[:, :rank].astype(BF16)
    b_coeff = selected[:, rank : rank + states]
    c_coeff = selected[:, rank + states :]
    rate2 = -jnp.exp(w_decay.astype(F32)) * LOG2E
    gate_in = mixed[PAD:, width:]
    st = flag[:, None]
    b_wide, c_wide = spread(b_coeff), spread(c_coeff)
    b_block, c_block = block_rows(b_coeff), block_rows(c_coeff)
    one_block = (jnp.arange(TC * states)[None] // states == jnp.arange(TC)[:, None]).astype(BF16)
    hops = range(1, groups)
    own_sums, start_state = [], []
    for part in range(HALVES):
        rate_part = rate2[:, part * width // HALVES : (part + 1) * width // HALVES]
        end = end_states(step_low, w_step, bias2, st, inner_low, rate2, b_wide, part, HALVES)
        came = [shifted(end, "expert", hop) for hop in hops]
        total = lambda x: x[:1].astype(F32) + x[1:2].astype(F32)
        own_sums.append(end[states : states + 8])
        start_state.append(entering([c[:states] for c in came], [total(c[states:]) for c in came], rate_part))
    start_state = jnp.concatenate(start_state, 1)
    gated_low, scanned, history, marks = forward_scan(
        step_low, w_step, bias2, st, inner_low, gate_in, rate2, skip2, b_wide, c_block, start_state
    )
    hidden_one = hidden_in + dot(gated_low, w_output)

    r2 = inverse_rms(hidden_one)
    norm_two = hidden_one * r2 * ffn_f
    logits = lax.dot_general(
        norm_two, router_f, (((1,), (1,)), ((), ())),
        precision=lax.Precision.HIGHEST, preferred_element_type=F32,
    )
    probs = jax.nn.softmax(logits, axis=-1)
    gate_value = jnp.sum(probs * chosen, axis=-1)
    grad_out = cotangent.astype(F32)
    grad_picked = (gate_value[:, None] * grad_out).astype(BF16)

    def moved(x, by):
        return lax.ppermute(x, "expert", [(i, (i + by) % groups) for i in range(groups)]) if by else x

    places = [place[k * capacity : (k + 1) * capacity] for k in range(groups)]
    norm_two_low = norm_two.astype(BF16)
    arrived = [moved(dot(m, norm_two_low).astype(BF16), k) for k, m in enumerate(places)]
    grad_arrived = []
    for k, m in enumerate(places):
        sent = dot(m, grad_picked).astype(BF16)
        if k:
            sent, arrived[k] = lax.optimization_barrier((sent, arrived[k]))
        grad_arrived.append(moved(sent, k))
    up_low, grad_pre, outs, ins = [], [], [], []
    for k in range(groups):
        up_pre = dot(arrived[k], w_up)
        act, gelu_back = jax.vjp(jax.nn.gelu, up_pre)
        up_low.append(act.astype(BF16))
        outs.append(dot(up_low[k], w_down).astype(BF16))
        grad_pre.append(gelu_back(product_back(grad_arrived[k], w_down))[0].astype(BF16))
        ins.append(product_back(grad_pre[k], w_up).astype(BF16))
    returned = jnp.concatenate([moved(x, -k) for k, x in enumerate(outs)])
    grad_sent = jnp.concatenate([moved(x, -k) for k, x in enumerate(ins)])
    up_low, grad_pre, arrived, grad_arrived, _, _ = lax.optimization_barrier(
        (up_low, grad_pre, arrived, grad_arrived, outs, ins)
    )
    grad_up = contract(jnp.concatenate(grad_pre), jnp.concatenate(arrived)).astype(BF16)
    grad_down = contract(jnp.concatenate(up_low), jnp.concatenate(grad_arrived)).astype(BF16)
    grad_sent, grad_up, grad_down = lax.optimization_barrier((grad_sent, grad_up, grad_down))
    sum_up = lax.psum_scatter(grad_up, "dp", scatter_dimension=0, tiled=True)

    picked = contract(place, returned)
    output = (hidden_one + gate_value[:, None] * picked).astype(BF16)
    grad_gate = jnp.sum(grad_out * picked, axis=1)
    grad_logits = probs * (grad_gate[:, None] * chosen - (grad_gate * gate_value)[:, None])
    grad_router = lax.dot_general(
        grad_logits, norm_two, (((0,), (0,)), ((), ())),
        precision=lax.Precision.HIGHEST, preferred_element_type=F32,
    )
    grad_norm_two = contract(place, grad_sent) + lax.dot_general(
        grad_logits, router_f, (((1,), (0,)), ((), ())),
        precision=lax.Precision.HIGHEST, preferred_element_type=F32,
    )
    grad_ffn_gain = jnp.sum(grad_norm_two * hidden_one * r2, axis=0)
    scaled = ffn_f * grad_norm_two
    grad_hidden = (
        grad_out
        + r2 * scaled
        - hidden_one * (r2 * r2 * r2) * jnp.mean(hidden_one * scaled, axis=-1, keepdims=True)
    )

    grad_mixer = grad_hidden.astype(BF16)
    grad_output_w = contract(gated_low, grad_mixer)
    grad_gated = product_back(grad_mixer, w_output)
    gate_f = gate_in.astype(F32)
    sigma = jax.nn.sigmoid(gate_f)
    grad_scanned = grad_gated * (gate_f * sigma)
    grad_gate_in = (grad_gated * scanned.astype(F32) * (sigma * (1.0 + gate_f * (1.0 - sigma)))).astype(BF16)
    grad_scanned, sum_up, grad_down = lax.optimization_barrier((grad_scanned, sum_up, grad_down))
    sum_down = lax.psum_scatter(grad_down, "dp", scatter_dimension=0, tiled=True)
    later_grad = []
    for part in range(HALVES):
        rate_part = rate2[:, part * width // HALVES : (part + 1) * width // HALVES]
        start = start_grads(step_low, w_step, bias2, st, grad_scanned, rate2, c_wide, part, HALVES)
        start = jnp.concatenate([start, own_sums[part]])
        came = [shifted(start, "expert", -hop) for hop in hops]
        later_grad.append(entering([c[:states] for c in came], [total(c[states:]) for c in came], rate_part))
    later_grad, sum_down, grad_output_w = lax.optimization_barrier(
        (jnp.concatenate(later_grad, 1), sum_down, grad_output_w.astype(BF16))
    )
    sum_output = lax.psum_scatter(grad_output_w, "dp", scatter_dimension=0, tiled=True)
    grad_pre_step, grad_inner, grad_decay_t, grad_skip, grad_b, grad_c = backward_scan(
        step_low, w_step, bias2, st, inner_low, grad_scanned, rate2, skip2,
        c_wide, b_block, one_block, history, marks, later_grad,
    )
    grad_pre_step, sum_output = lax.optimization_barrier((grad_pre_step, sum_output))
    sum_output = lax.psum(sum_output, "expert")
    grad_step_bias = jnp.sum(grad_pre_step.astype(F32), axis=0, keepdims=True)
    grad_step_w = contract(step_low, grad_pre_step)
    grad_step_low = product_back(grad_pre_step, w_step).astype(BF16)
    grad_selected = jnp.concatenate(
        [grad_step_low, grad_b[:, :states], grad_c[:, 0].reshape(rows, states).astype(BF16)], 1
    )
    grad_select_w = contract(grad_selected, inner_low)
    summed = stacked(
        [
            grad_select_w, grad_step_w, grad_decay_t, grad_step_bias, grad_skip,
            paired_rows(jnp.concatenate([grad_ffn_gain[None], grad_ffn_gain[None], grad_router], 0), devices),
        ]
    )
    grad_conv_in, grad_kernel, grad_conv_b = conv_back(
        mixed, grad_inner, slope_low, grad_selected, w_select, w_conv, ok
    )
    grad_conv_in, summed, sum_output = lax.optimization_barrier((grad_conv_in, summed, sum_output))
    summed = lax.psum_scatter(summed, "dp", scatter_dimension=1, tiled=True)
    grad_mixed = jnp.concatenate([grad_conv_in, jnp.pad(grad_gate_in, ((PAD, 0), (0, 0)))], 1)
    grad_input_w = contract(grad_mixed, norm_low).astype(BF16)
    grad_input_w, grad_mixed, summed = lax.optimization_barrier((grad_input_w, grad_mixed, summed))
    sum_input = lax.psum_scatter(grad_input_w, "dp", scatter_dimension=0, tiled=True)
    sum_input, summed = lax.psum((sum_input, summed), "expert")
    summed = summed.astype(F32)
    grad_norm_one = product_back(grad_mixed, w_input)
    returned_edge = shifted(grad_norm_one[PAD - taps + 1 : PAD], "expert", -1) * edge_keep
    grad_norm_one = grad_norm_one[PAD:] + jnp.pad(returned_edge, ((rows - taps + 1, 0), (0, 0)))
    grad_norm_gain = jnp.sum(grad_norm_one * hidden_in * norm_r, axis=0, keepdims=True)
    scaled_one = norm_f * grad_norm_one
    grad_tokens = (
        grad_hidden
        + norm_r * scaled_one
        - hidden_in * (norm_r * norm_r * norm_r) * jnp.mean(hidden_in * scaled_one, axis=-1, keepdims=True)
    ).astype(BF16)
    tiny = jnp.concatenate([grad_kernel, grad_conv_b, jnp.pad(grad_norm_gain, ((0, 0), (0, width - model)))])
    tiny = lax.psum(tiny, ("dp", "expert"))
    here = lax.axis_index("dp")
    share, model_share = width // devices, model // devices
    own = lax.dynamic_slice(tiny, (0, here * share), (taps + 1, share))
    sum_kernel, sum_conv_b = own[:taps], own[taps]
    sum_norm = lax.dynamic_slice(tiny, (taps + 1, here * model_share), (1, model_share))[0]
    sum_select, sum_step, sum_decay, sum_step_b, sum_skip, singles = cut(
        summed, (w_select.shape[0], rank, states, 1, 1, (groups + 2) // 2)
    )
    singles = single_rows(singles, 1)
    sum_input, sum_output = sum_input.astype(F32).T, sum_output.astype(F32)
    return (
        output, grad_tokens, sum_input, sum_kernel, sum_conv_b, sum_select.T, sum_step, sum_step_b[0],
        sum_decay.T, sum_skip[0], sum_output, sum_norm, singles[1], singles[2:].T,
        sum_up.astype(F32).T[None], sum_down.astype(F32)[None],
    )


def solution(mesh):
    placed = (
        P(("dp", "expert"), None),
        P(("dp", "expert"), None),
        P(("dp", "expert"), None),
        P(("dp", "expert")),
        P(None, "dp"),
        P(None, "dp"),
        P("dp"),
        P("dp", None),
        P(None, "dp"),
        P("dp"),
        P("dp", None),
        P("dp"),
        P("dp", None),
        P("dp"),
        P("dp"),
        P("dp", None),
        P("expert", None, "dp"),
        P("expert", "dp", None),
    )
    return jax.shard_map(
        body,
        mesh=mesh,
        in_specs=placed,
        out_specs=(
            P(("dp", "expert"), None),
            P(("dp", "expert"), None),
            P(None, "dp"),
            P(None, "dp"),
            P("dp"),
            P("dp", None),
            P(None, "dp"),
            P("dp"),
            P("dp", None),
            P("dp"),
            P("dp", None),
            P("dp"),
            P("dp"),
            P("dp", None),
            P("expert", None, "dp"),
            P("expert", "dp", None),
        ),
        check_vma=False,
    )
```

```python
from functools import partial

import jax
import jax.numpy as jnp
from jax import lax
from jax.experimental import pallas as pl
from jax.experimental.pallas import tpu as pltpu
from jax.sharding import PartitionSpec as P

TC = 16
ROWS = 256
CONV_ROWS = 128
PAD = 16
UNROLL = 8
FAR = 1e4
LOG2E = 1.4426950408889634
LN2 = 0.6931471805599453
F32 = jnp.float32
BF16 = jnp.bfloat16


def tiled(x, n):
    return jnp.concatenate([x] * n, axis=1) if n > 1 else x


def folded(x):
    n = x.shape[1] // 128
    out = x[:, :128]
    for i in range(1, n):
        out = out + x[:, i * 128 : (i + 1) * 128]
    return out


def dot(a, b):
    return jnp.dot(a, b, preferred_element_type=F32)


def prepare(s_ref, w_ref, b_ref, st_ref, u_ref, dk_ref, dv_ref, pre_ref=None):
    size = min(s_ref.shape[0], ROWS)

    def block(i, carry):
        r = pl.ds(pl.multiple_of(i * size, size), size)
        pre = dot(s_ref[r, :], w_ref[...]) + b_ref[...].astype(F32)
        delta = jnp.maximum(pre, 0.0) + jnp.log1p(jnp.exp(-jnp.abs(pre)))
        dk = jnp.where(st_ref[r, :] > 0.0, FAR, delta)
        dk_ref[r, :] = dk
        if u_ref is not None:
            dv_ref[r, :] = delta * u_ref[r, :].astype(F32)
        if pre_ref is not None:
            pre_ref[r, :] = pre
        return carry + jnp.sum(dk, axis=0, keepdims=True)

    return lax.fori_loop(
        0, s_ref.shape[0] // size, block, jnp.zeros((1, w_ref.shape[1]), F32)
    )


def end_kernel(s_ref, w_ref, b_ref, st_ref, u_ref, a_ref, bb_ref, low_ref, dk_ref, dv_ref, out_ref):
    reps = w_ref.shape[1] // 128
    states = a_ref.shape[0]
    first = pl.program_id(1) == 0
    total = prepare(s_ref, w_ref, b_ref, st_ref, u_ref, dk_ref, dv_ref)
    a = a_ref[...]

    @pl.when(first)
    def _():
        out_ref[...] = jnp.zeros_like(out_ref)

    def chunk(c, h):
        t0 = pl.multiple_of(c * TC, TC)
        for i in range(TC):
            f = jnp.exp2(a * dk_ref[pl.ds(t0 + i, 1), :])
            h = f * h + dv_ref[pl.ds(t0 + i, 1), :] * tiled(bb_ref[t0 + i], reps)
        return h

    out_ref[:states, :] = lax.fori_loop(0, s_ref.shape[0] // TC, chunk, out_ref[:states, :])
    out_ref[states : states + 1, :] += total

    @pl.when(pl.program_id(1) == pl.num_programs(1) - 1)
    def _():
        low_ref[:states, :] = out_ref[:states, :].astype(BF16)
        sums = out_ref[states : states + 1, :]
        high = sums.astype(BF16).astype(F32)
        row = lax.broadcasted_iota(jnp.int32, (states, sums.shape[1]), 0)
        both = jnp.where(row == 0, high, jnp.where(row == 1, sums - high, 0.0))
        low_ref[states:, :] = both.astype(BF16)


def forward_kernel(
    s_ref, w_ref, b_ref, st_ref, u_ref, z_ref, a_ref, skip_ref, bb_ref, cm_ref, h0_ref,
    g_ref, y_ref, hs_ref, ck_ref, dk_ref, dv_ref, ys_ref, h_ref,
):
    reps = w_ref.shape[1] // 128
    states = a_ref.shape[0]
    chunks = s_ref.shape[0] // TC
    prepare(s_ref, w_ref, b_ref, st_ref, u_ref, dk_ref, dv_ref)
    a = a_ref[...]

    @pl.when(pl.program_id(1) == 0)
    def _():
        h_ref[...] = h0_ref[...]

    def scan(c, h):
        t0 = pl.multiple_of(c * TC, TC)
        r0 = pl.multiple_of(c * TC * states, TC * states)
        ck_ref[c] = h.astype(BF16)
        for i in range(TC):
            f = jnp.exp2(a * dk_ref[pl.ds(t0 + i, 1), :])
            h = f * h + dv_ref[pl.ds(t0 + i, 1), :] * tiled(bb_ref[t0 + i], reps)
            hs_ref[pl.ds(r0 + i * states, states), :] = h.astype(BF16)
        return h

    def emit(c):
        t0 = pl.multiple_of(c * TC, TC)
        r0 = pl.multiple_of(c * TC * states, TC * states)
        ys_ref[pl.ds(t0, TC), :] = dot(cm_ref[c], hs_ref[pl.ds(r0, TC * states), :])

    def group(j, h):
        for m in range(UNROLL):
            h = scan(UNROLL * j + m, h)
            emit(UNROLL * j + m)
        return h

    h_ref[...] = lax.fori_loop(0, chunks // UNROLL, group, h_ref[...])

    size = min(s_ref.shape[0], ROWS)

    def finish(i, carry):
        r = pl.ds(pl.multiple_of(i * size, size), size)
        y = ys_ref[r, :] + skip_ref[...].astype(F32) * u_ref[r, :].astype(F32)
        z = z_ref[r, :].astype(F32)
        y_ref[r, :] = y.astype(BF16)
        g_ref[r, :] = (y * (z / (1.0 + jnp.exp(-z)))).astype(BF16)
        return carry

    lax.fori_loop(0, s_ref.shape[0] // size, finish, 0)


def start_kernel(s_ref, w_ref, b_ref, st_ref, dy_ref, a_ref, cb_ref, low_ref, dk_ref, out_ref):
    reps = w_ref.shape[1] // 128
    chunks = s_ref.shape[0] // TC
    prepare(s_ref, w_ref, b_ref, st_ref, None, dk_ref, None)
    a = a_ref[...]

    @pl.when(pl.program_id(1) == 0)
    def _():
        out_ref[...] = jnp.zeros_like(out_ref)

    def chunk(j, grad):
        t0 = pl.multiple_of((chunks - 1 - j) * TC, TC)
        for i in range(TC - 1, -1, -1):
            f = jnp.exp2(a * dk_ref[pl.ds(t0 + i, 1), :])
            lam = grad + dy_ref[pl.ds(t0 + i, 1), :] * tiled(cb_ref[t0 + i], reps)
            grad = f * lam
        return grad

    out_ref[...] = lax.fori_loop(0, chunks, chunk, out_ref[...])

    @pl.when(pl.program_id(1) == pl.num_programs(1) - 1)
    def _():
        low_ref[...] = out_ref[...].astype(BF16)


def backward_kernel(
    s_ref, w_ref, b_ref, st_ref, u_ref, dy_ref, a_ref, skip_ref, cb_ref, bm_ref, om_ref, hs_ref, ck_ref, g0_ref,
    ds_ref, du_ref, da_ref, dskip_ref, db_ref, dc_ref,
    pre_ref, dk_ref, dv_ref, q_ref, p_ref, lb0, lb1, wb0, wb1, grad_ref, accb_ref, accc_ref,
):
    step, seg = pl.program_id(0), pl.program_id(1)
    last = pl.num_programs(1) - 1 - seg
    reps = w_ref.shape[1] // 128
    states = a_ref.shape[0]
    rows = s_ref.shape[0]
    chunks = rows // TC
    prepare(s_ref, w_ref, b_ref, st_ref, u_ref, dk_ref, dv_ref, pre_ref)
    token0 = pl.multiple_of(last * rows, rows)

    @pl.when((step == 0) & (seg == 0))
    def _():
        accb_ref[...] = jnp.zeros_like(accb_ref)
        accc_ref[...] = jnp.zeros_like(accc_ref)

    @pl.when(seg == 0)
    def _():
        grad_ref[...] = g0_ref[...]
        da_ref[...] = jnp.zeros_like(da_ref)
        dskip_ref[...] = jnp.zeros_like(dskip_ref)

    a = a_ref[...]
    a_low = a.astype(BF16)

    def scan(c, grad, lb, wb):
        t0 = pl.multiple_of(c * TC, TC)
        r0 = pl.multiple_of(c * TC * states, TC * states)
        da, four = None, None
        for i in range(TC - 1, -1, -1):
            d = dk_ref[pl.ds(t0 + i, 1), :]
            f = jnp.exp2(a * d)
            lam = grad + dy_ref[pl.ds(t0 + i, 1), :] * tiled(cb_ref[t0 + i], reps)
            grad = f * lam
            lb[pl.ds(i * states, states), :] = lam.astype(BF16)
            h = ck_ref[c] if i == 0 else hs_ref[pl.ds(r0 + (i - 1) * states, states), :]
            w = grad.astype(BF16) * h
            wb[pl.ds(i * states, states), :] = w * a_low
            wd = w * jnp.broadcast_to(d, w.shape).astype(BF16)
            four = wd if four is None else four + wd
            if i % 4 == 0:
                da = four.astype(F32) if da is None else da + four.astype(F32)
                four = None
            accb_ref[token0 + t0 + i] += folded(lam * dv_ref[pl.ds(t0 + i, 1), :])
        da_ref[...] += da
        return grad

    def emit(c, lb, wb):
        t0 = pl.multiple_of(c * TC, TC)
        r0 = pl.multiple_of(c * TC * states, TC * states)
        q_ref[pl.ds(t0, TC), :] = dot(bm_ref[c], lb[...])
        p_ref[pl.ds(t0, TC), :] = dot(om_ref[...], wb[...])
        accc_ref[last * chunks + c] += lax.dot_general(
            dy_ref[pl.ds(t0, TC), :].astype(BF16), hs_ref[pl.ds(r0, TC * states), :],
            (((1,), (1,)), ((), ())), preferred_element_type=F32,
        )

    def pair(j, grad):
        c = chunks - 1 - 2 * j
        grad = scan(c, grad, lb0, wb0)
        emit(c, lb0, wb0)
        grad = scan(c - 1, grad, lb1, wb1)
        emit(c - 1, lb1, wb1)
        return grad

    grad_ref[...] = lax.fori_loop(0, chunks // 2, pair, grad_ref[...])

    @pl.when(last == 0)
    def _():
        da_ref[...] = da_ref[...] * a * LN2

    size = min(s_ref.shape[0], ROWS)

    def finish(i, carry):
        r = pl.ds(pl.multiple_of(i * size, size), size)
        u = u_ref[r, :].astype(F32)
        q = q_ref[r, :]
        dy = dy_ref[r, :]
        pre = pre_ref[r, :]
        delta = jnp.maximum(pre, 0.0) + jnp.log1p(jnp.exp(-jnp.abs(pre)))
        dd = p_ref[r, :] * LN2 + u * q
        ds_ref[r, :] = (dd / (1.0 + jnp.exp(-pre))).astype(BF16)
        du_ref[r, :] = delta * q + dy * skip_ref[...].astype(F32)
        return carry + jnp.sum(dy * u, axis=0, keepdims=True)

    dskip_ref[...] += lax.fori_loop(0, rows // size, finish, jnp.zeros(dskip_ref.shape, F32))

    @pl.when((step == pl.num_programs(0) - 1) & (last == 0))
    def _():
        ones = jnp.ones((128, 128), BF16)
        row = lax.broadcasted_iota(jnp.int32, (TC * states, 128), 0) % states
        lane = lax.broadcasted_iota(jnp.int32, (TC * states, 128), 1)

        def gather(c, carry):
            t0 = pl.multiple_of(c * TC, TC)
            b = dot(accb_ref[pl.ds(t0, TC)].reshape(TC * states, 128).astype(BF16), ones)
            db_ref[pl.ds(t0, TC), :] = dot(om_ref[...], jnp.where(lane == row, b, 0.0).astype(BF16)).astype(BF16)
            own = om_ref[...].astype(F32) * accc_ref[c]
            dc_ref[c] = jnp.broadcast_to(jnp.sum(own, axis=0, keepdims=True), dc_ref.shape[1:])
            return carry

        lax.fori_loop(0, accc_ref.shape[0], gather, 0)


def conv_kernel_back(xs_ref, du_ref, slope_ref, dp_ref, sel_ref, k_ref, ok_ref, dxs_ref, dk_ref, db_ref, dc_ref):
    taps = k_ref.shape[0]
    rows = du_ref.shape[0]
    k = k_ref[...].astype(F32)
    dc_ref[:PAD, :] = jnp.zeros((PAD, dc_ref.shape[1]), F32)
    dc_ref[pl.ds(rows + PAD, PAD), :] = jnp.zeros((PAD, dc_ref.shape[1]), F32)

    def first(i, carry):
        t0 = pl.multiple_of(i * CONV_ROWS, CONV_ROWS)
        at = pl.ds(t0, CONV_ROWS)
        du = du_ref[at, :] + dot(dp_ref[at, :], sel_ref[...])
        dc = du * slope_ref[at, :].astype(F32)
        dc_ref[pl.ds(t0 + PAD, CONV_ROWS), :] = dc
        slab = xs_ref[pl.ds(t0, CONV_ROWS + PAD), :].astype(F32)
        sums = [jnp.sum(dc, axis=0, keepdims=True)]
        for lag in range(taps):
            x = slab[PAD - lag : PAD - lag + CONV_ROWS]
            part = dc * x
            if lag:
                part = part * ok_ref[pl.ds(t0 + PAD, CONV_ROWS), lag : lag + 1]
            sums.append(jnp.sum(part, axis=0, keepdims=True))
        return tuple(a + b for a, b in zip(carry, sums))

    size = max(n for n in range(PAD, 129, PAD) if (rows + PAD) % n == 0)
    zero = jnp.zeros((1, k.shape[1]), F32)
    sums = lax.fori_loop(0, rows // CONV_ROWS, first, (zero,) * (taps + 1))
    db_ref[...] = sums[0]
    for lag in range(taps):
        dk_ref[taps - 1 - lag : taps - lag, :] = sums[1 + lag]

    def second(i, carry):
        r0 = pl.multiple_of(i * size, PAD)
        slab = dc_ref[pl.ds(r0, size + PAD), :]
        ok = ok_ref[pl.ds(r0, size + PAD), :]
        out = k[taps - 1 : taps] * slab[:size]
        for lag in range(1, taps):
            part = (ok[:, lag : lag + 1] * slab)[lag : lag + size]
            out = out + k[taps - 1 - lag : taps - lag] * part
        dxs_ref[pl.ds(r0, size), :] = out.astype(BF16)
        return carry

    lax.fori_loop(0, (rows + PAD) // size, second, 0)


def conv_back(xs, du, slope, dp, sel, k, ok):
    rows, width = du.shape
    cb = scan_width(width, 768)
    col = lambda n: pl.BlockSpec((n, cb), lambda i: (0, i))
    whole = lambda x: pl.BlockSpec(x.shape, lambda i: (0, 0))
    taps = k.shape[0]
    return pl.pallas_call(
        conv_kernel_back,
        grid=(width // cb,),
        in_specs=[col(rows + PAD), col(rows), col(rows), whole(dp), col(sel.shape[0]), col(taps), whole(ok)],
        out_specs=[col(rows + PAD), col(taps), col(1)],
        out_shape=[sds((rows + PAD, width), BF16), sds((taps, width), F32), sds((1, width), F32)],
        scratch_shapes=[pltpu.VMEM((rows + 2 * PAD, cb), F32)],
        compiler_params=params(),
        cost_estimate=pl.CostEstimate(flops=rows * width * 300, bytes_accessed=rows * width * 8, transcendentals=0),
        name="conv_back",
    )(xs, du, slope, dp, sel, k, ok)


def scan_width(width, limit):
    n = width // 128
    best = max(d for d in range(1, n + 1) if n % d == 0 and d * 128 <= limit)
    return best * 128


def params():
    return pltpu.CompilerParams(vmem_limit_bytes=60 * 2**20)


def sds(*a):
    return jax.ShapeDtypeStruct(*a)


class Blocks:
    def __init__(self, rows, width, cb, parts, reverse=False, first=0):
        self.first = first
        self.grid = (width // cb, parts)
        self.cb, self.rows, self.seg = cb, rows, rows // parts
        self.at = (lambda s: parts - 1 - s) if reverse else (lambda s: s)

    def token(self, n):
        return pl.BlockSpec((self.seg, n), lambda k, s: (self.at(s), 0))

    def channel(self, n):
        return pl.BlockSpec((n, self.cb), lambda k, s: (0, k + self.first))

    def both(self, times=1, off=0):
        return pl.BlockSpec((self.seg * times, self.cb), lambda k, s: (self.at(s), k + self.first + off))

    def lead(self, n, *rest):
        return pl.BlockSpec((n, *rest), lambda k, s: (self.at(s),) + (0,) * len(rest))

    def marks(self, states):
        return pl.BlockSpec((self.seg // TC, states, self.cb), lambda k, s: (self.at(s), 0, k))

    def whole(self, shape):
        return pl.BlockSpec(shape, lambda k, s: (0,) * len(shape))


def estimate(rows, width, states, ops, size):
    return pl.CostEstimate(
        flops=ops * rows * width * states, bytes_accessed=rows * width * size, transcendentals=rows * width * states
    )


END, FORWARD, START, BACKWARD = (1152, 3), (1152, 6), (1152, 3), (2304, 24)


def end_states(s, w, b, st, u, a, bb, part, of):
    rows, width, states = s.shape[0], w.shape[1] // of, a.shape[0]
    cb = min(END[0], width)
    k = Blocks(rows, width, cb, END[1], first=part * (width // cb))
    return pl.pallas_call(
        end_kernel,
        grid=k.grid,
        in_specs=[k.token(s.shape[1]), k.channel(w.shape[0]), k.channel(1), k.token(1), k.both(), k.channel(states), k.lead(k.seg, states, 128)],
        out_specs=pl.BlockSpec((2 * states, cb), lambda i, j: (0, i)),
        out_shape=sds((2 * states, width), BF16),
        scratch_shapes=[pltpu.VMEM((k.seg, k.cb), F32)] * 2 + [pltpu.VMEM((states + 8, k.cb), F32)],
        compiler_params=params(),
        cost_estimate=estimate(rows, width, states, 6, 8),
        name="end_states",
    )(s, w, b, st, u, a, bb)


def forward_scan(s, w, b, st, u, z, a, skip, bb, cm, h0):
    rows, width, states = s.shape[0], w.shape[1], a.shape[0]
    k = Blocks(rows, width, *FORWARD)
    return pl.pallas_call(
        forward_kernel,
        grid=k.grid,
        in_specs=[k.token(s.shape[1]), k.channel(w.shape[0]), k.channel(1), k.token(1), k.both(), k.both(), k.channel(states), k.channel(1),
                  k.lead(k.seg, states, 128), k.lead(k.seg // TC, *cm.shape[1:]), k.channel(states)],
        out_specs=[k.both(), k.both(), k.both(states), k.marks(states)],
        out_shape=[sds((rows, width), BF16), sds((rows, width), BF16), sds((rows * states, width), BF16), sds((rows // TC, states, width), BF16)],
        scratch_shapes=[pltpu.VMEM((k.seg, k.cb), F32)] * 3 + [pltpu.VMEM((states, k.cb), F32)],
        compiler_params=params(),
        cost_estimate=estimate(rows, width, states, 9, 44),
        name="forward_scan",
    )(s, w, b, st, u, z, a, skip, bb, cm, h0)


def start_grads(s, w, b, st, dy, a, cb_wide, part, of):
    rows, width, states = s.shape[0], w.shape[1] // of, a.shape[0]
    cb = min(START[0], width)
    k = Blocks(rows, width, cb, START[1], reverse=True, first=part * (width // cb))
    return pl.pallas_call(
        start_kernel,
        grid=k.grid,
        in_specs=[k.token(s.shape[1]), k.channel(w.shape[0]), k.channel(1), k.token(1), k.both(), k.channel(states), k.lead(k.seg, states, 128)],
        out_specs=pl.BlockSpec((states, cb), lambda i, j: (0, i)),
        out_shape=sds((states, width), BF16),
        scratch_shapes=[pltpu.VMEM((k.seg, k.cb), F32), pltpu.VMEM((states, k.cb), F32)],
        compiler_params=params(),
        cost_estimate=estimate(rows, width, states, 6, 8),
        name="start_grads",
    )(s, w, b, st, dy, a, cb_wide)


def backward_scan(s, w, b, st, u, dy, a, skip, cb, bm, om, hs, ck, g0):
    rows, width, states = s.shape[0], w.shape[1], a.shape[0]
    k = Blocks(rows, width, *BACKWARD, reverse=True)
    chunks = rows // TC
    return pl.pallas_call(
        backward_kernel,
        grid=k.grid,
        in_specs=[k.token(s.shape[1]), k.channel(w.shape[0]), k.channel(1), k.token(1), k.both(), k.both(), k.channel(states), k.channel(1),
                  k.lead(k.seg, states, 128), k.lead(k.seg // TC, *bm.shape[1:]), k.whole(om.shape), k.both(states), k.marks(states), k.channel(states)],
        out_specs=[k.both(), k.both(), k.channel(states), k.channel(1), k.whole((rows, 128)), k.whole((chunks, 8, TC * states))],
        out_shape=[sds((rows, width), BF16), sds((rows, width), F32), sds((states, width), F32), sds((1, width), F32),
                   sds((rows, 128), BF16), sds((chunks, 8, TC * states), F32)],
        scratch_shapes=[pltpu.VMEM((k.seg, k.cb), F32)] * 5
        + [pltpu.VMEM((TC * states, k.cb), BF16)] * 4
        + [pltpu.VMEM((states, k.cb), F32), pltpu.VMEM((rows, states, 128), F32), pltpu.VMEM((chunks, TC, TC * states), F32)],
        compiler_params=params(),
        cost_estimate=estimate(rows, width, states, 18, 44),
        name="backward_scan",
    )(s, w, b, st, u, dy, a, skip, cb, bm, om, hs, ck, g0)


def spread(coeff):
    return jnp.broadcast_to(coeff[:, :, None], (*coeff.shape, 128))


def block_rows(coeff):
    rows, states = coeff.shape
    mask = jnp.arange(TC * states)[None, None] // states == jnp.arange(TC)[None, :, None]
    return jnp.where(mask, coeff.reshape(rows // TC, 1, TC * states), 0.0).astype(BF16)


epsilon = 1e-05
HALVES = 2


def shifted(array, axis, by):
    length = lax.axis_size(axis)
    pairs = [(i, i + by) for i in range(length) if 0 <= i + by < length]
    return lax.ppermute(array, axis, pairs)


def entering(came, sums, rate2):
    state, decay = jnp.zeros_like(rate2), jnp.zeros((1, rate2.shape[1]), F32)
    for end, total in zip(came, sums):
        state = state + jnp.exp2(rate2 * decay) * end.astype(F32)
        decay = decay + total
    return state


def product_back(left, right):
    return lax.dot_general(left, right, (((1,), (1,)), ((), ())), preferred_element_type=F32)


def contract(left, right):
    return lax.dot_general(left, right, (((0,), (0,)), ((), ())), preferred_element_type=F32)


def silu_slope(values):
    sigma = jax.nn.sigmoid(values)
    return sigma * (1.0 + values * (1.0 - sigma))


def inverse_rms(values):
    return lax.rsqrt(jnp.mean(values * values, axis=-1, keepdims=True) + epsilon)


def paired_rows(rows, devices):
    r, d = rows.shape
    split = rows.reshape(r // 2, 2, devices, d // devices)
    return split.transpose(0, 2, 1, 3).reshape(r // 2, 2 * d)


def single_rows(rows, devices):
    r, d = rows.shape
    split = rows.reshape(r, devices, 2, d // (2 * devices))
    return split.transpose(0, 2, 1, 3).reshape(2 * r, d // 2)


def stacked(parts):
    whole = jnp.concatenate([p.astype(BF16) for p in parts], axis=0)
    return jnp.pad(whole, ((0, -whole.shape[0] % 16), (0, 0)))


def expert_sum(*arrays):
    n, here = lax.axis_size("expert"), lax.axis_index("expert")
    split = [x.reshape(n, x.shape[0] // n, x.shape[1]) for x in arrays]
    padded = [jnp.pad(x, ((0, 0), (0, -x.shape[1] % 8), (0, 0))) for x in split]
    parts = jnp.concatenate(padded, axis=1) if len(padded) > 1 else padded[0]
    moved = lambda x, k: lax.ppermute(x, "expert", [(i, (i + k) % n) for i in range(n)])
    part = lambda k: lax.dynamic_index_in_dim(parts, jnp.mod(here + k, n), 0, keepdims=False)
    total = part(0).astype(F32)
    for x in [moved(part(k), k) for k in range(1, n)]:
        total = total + x.astype(F32)
    total = total.astype(BF16)
    came = [total] + [moved(total, k) for k in range(1, n)]
    twice = jnp.stack(came[::-1] * 2)
    every = lax.dynamic_slice_in_dim(twice, n - 1 - here, n, 0)
    out, at = [], 0
    for x, p in zip(split, padded):
        out.append(every[:, at : at + x.shape[1]].reshape(n * x.shape[1], x.shape[2]))
        at += p.shape[1]
    return out


def shares(rows, devices):
    r, columns = rows.shape
    return rows.reshape(r, devices, columns // devices).transpose(1, 0, 2).reshape(devices, -1)


def halved(grads, devices):
    rows, columns = grads.shape
    split = grads.reshape(devices // 2, 2, rows // devices, columns)
    return split.transpose(1, 0, 2, 3).reshape(devices, rows // devices, columns)


def cut(whole, counts):
    out, at = [], 0
    for n in counts:
        out.append(whole[at : at + n])
        at += n
    return out


def body(
    tokens, cotangent, routes, starts, input_proj, conv_kernel, conv_bias, select_proj, step_proj,
    step_bias, decay_log, skip_gain, output_proj, norm_gain, ffn_gain, router, expert_up, expert_down,
):
    devices = lax.axis_size("dp")
    groups = lax.axis_size("expert")
    rows, model = tokens.shape
    taps, rank, states = conv_kernel.shape[0], step_proj.shape[0], decay_log.shape[1]
    capacity = 2 * rows // groups
    w_input = lax.all_gather(input_proj, "dp", axis=1, tiled=True)
    small = stacked(
        [
            select_proj.T, step_proj, decay_log.T, conv_kernel, conv_bias[None], step_bias[None], skip_gain[None],
            paired_rows(jnp.concatenate([norm_gain[None], ffn_gain[None], router.T], 0), 1),
        ]
    )
    counts = (select_proj.shape[1], rank, states, taps, 1, 1, 1, (groups + 2) // 2)
    w_select, w_step, w_decay, w_conv, b_conv, bias2, skip2, singles = cut(
        lax.all_gather(small, "dp", axis=1, tiled=True), counts
    )
    singles = single_rows(singles, devices).astype(F32)
    norm_f, ffn_f, router_f = singles[0], singles[1], singles[2:]
    w_output = lax.all_gather(output_proj, "dp", axis=0, tiled=True)
    w_up = lax.all_gather(expert_up[0], "dp", axis=1, tiled=True)
    w_down = lax.all_gather(expert_down[0], "dp", axis=0, tiled=True)
    width = w_select.shape[1]
    conv_f = w_conv.astype(F32)

    route = routes[:, 0]
    chosen = (route[:, None] == jnp.arange(groups, dtype=jnp.int32)[None, :]).astype(F32)
    before = (jnp.arange(rows)[:, None] > jnp.arange(rows)[None, :]).astype(BF16)
    ranks = dot(before, chosen.astype(BF16))
    slot = jnp.sum(ranks * chosen, axis=1).astype(jnp.int32)
    assert groups & (groups - 1) == 0
    distance = jnp.bitwise_xor(route, lax.axis_index("expert"))
    target = jnp.where(slot < capacity, distance * capacity + slot, groups * capacity)
    place = (jnp.arange(groups * capacity)[:, None] == target[None, :]).astype(BF16)

    hidden_in = tokens.astype(F32)
    norm_r = inverse_rms(hidden_in)
    norm_own = (hidden_in * norm_r * norm_f).astype(BF16)
    flag = starts.astype(F32)
    same = 1.0 - flag
    valid = [jnp.ones((rows,), F32)]
    for lag in range(1, taps):
        moved = jnp.concatenate([jnp.ones((lag - 1,), F32), same[: rows - lag + 1]])
        valid.append(valid[-1] * moved)
    edge = [jnp.ones((), F32)]
    for lag in range(1, taps - 1):
        edge.append(edge[-1] * same[rows - lag])
    edge_keep = jnp.stack(edge[::-1])[:, None]
    tail = (norm_own[rows - taps + 1 :].astype(F32) * edge_keep).astype(BF16)
    borrowed = shifted(tail, "expert", 1)
    norm_low = jnp.concatenate([jnp.zeros((PAD - taps + 1, model), BF16), borrowed, norm_own], 0)
    mixed = dot(norm_low, w_input).astype(BF16)
    conv_sum = jnp.broadcast_to(b_conv.astype(F32), (rows, width))
    for lag in range(taps):
        conv_sum = conv_sum + valid[lag][:, None] * conv_f[taps - 1 - lag] * mixed[PAD - lag : PAD - lag + rows, :width].astype(F32)
    ok = jnp.pad(jnp.stack(valid, 1), ((PAD, PAD), (0, 0)))
    inner_low = jax.nn.silu(conv_sum).astype(BF16)
    slope_low = silu_slope(conv_sum).astype(BF16)
    selected = product_back(inner_low, w_select)
    step_low = selected[:, :rank].astype(BF16)
    b_coeff = selected[:, rank : rank + states]
    c_coeff = selected[:, rank + states :]
    rate2 = -jnp.exp(w_decay.astype(F32)) * LOG2E
    gate_in = mixed[PAD:, width:]
    st = flag[:, None]
    b_wide, c_wide = spread(b_coeff), spread(c_coeff)
    b_block, c_block = block_rows(b_coeff), block_rows(c_coeff)
    one_block = (jnp.arange(TC * states)[None] // states == jnp.arange(TC)[:, None]).astype(BF16)
    hops = range(1, groups)
    own_sums, start_state = [], []
    for part in range(HALVES):
        rate_part = rate2[:, part * width // HALVES : (part + 1) * width // HALVES]
        end = end_states(step_low, w_step, bias2, st, inner_low, rate2, b_wide, part, HALVES)
        came = [shifted(end, "expert", hop) for hop in hops]
        total = lambda x: x[:1].astype(F32) + x[1:2].astype(F32)
        own_sums.append(end[states : states + 8])
        start_state.append(entering([c[:states] for c in came], [total(c[states:]) for c in came], rate_part))
    start_state = jnp.concatenate(start_state, 1)
    gated_low, scanned, history, marks = forward_scan(
        step_low, w_step, bias2, st, inner_low, gate_in, rate2, skip2, b_wide, c_block, start_state
    )
    hidden_one = hidden_in + dot(gated_low, w_output)

    r2 = inverse_rms(hidden_one)
    norm_two = hidden_one * r2 * ffn_f
    logits = lax.dot_general(
        norm_two, router_f, (((1,), (1,)), ((), ())),
        precision=lax.Precision.HIGHEST, preferred_element_type=F32,
    )
    probs = jax.nn.softmax(logits, axis=-1)
    gate_value = jnp.sum(probs * chosen, axis=-1)
    grad_out = cotangent.astype(F32)
    grad_picked = (gate_value[:, None] * grad_out).astype(BF16)

    def swapped(x, k):
        return lax.ppermute(x, "expert", [(i, i ^ k) for i in range(groups)]) if k else x

    places = [place[k * capacity : (k + 1) * capacity] for k in range(groups)]
    norm_two_low = norm_two.astype(BF16)
    arrived, grad_arrived = [None] * groups, [None] * groups
    far_first = list(range(groups - 1, 0, -1))
    for k in far_first + [0]:
        arrived[k] = swapped(dot(places[k], norm_two_low).astype(BF16), k)
    for k in far_first + [0]:
        sent = dot(places[k], grad_picked).astype(BF16)
        if k:
            sent, arrived[k] = lax.optimization_barrier((sent, arrived[k]))
        grad_arrived[k] = swapped(sent, k)
    up_low, grad_pre, outs, ins = ([None] * groups for _ in range(4))
    for k in [0] + far_first:
        up_pre = dot(arrived[k], w_up)
        act, gelu_back = jax.vjp(jax.nn.gelu, up_pre)
        up_low[k] = act.astype(BF16)
        outs[k] = dot(up_low[k], w_down).astype(BF16)
        grad_pre[k] = gelu_back(product_back(grad_arrived[k], w_down))[0].astype(BF16)
        ins[k] = product_back(grad_pre[k], w_up).astype(BF16)
    returned = [None] * groups
    grad_sent = [None] * groups
    for k in far_first + [0]:
        returned[k] = swapped(outs[k], k)
    for k in far_first + [0]:
        grad_sent[k] = swapped(ins[k], k)
    returned, grad_sent = jnp.concatenate(returned), jnp.concatenate(grad_sent)
    up_low, grad_pre, arrived, grad_arrived, _, _ = lax.optimization_barrier(
        (up_low, grad_pre, arrived, grad_arrived, outs, ins)
    )
    grad_up = contract(jnp.concatenate(grad_pre), jnp.concatenate(arrived)).astype(BF16)
    grad_down = contract(jnp.concatenate(up_low), jnp.concatenate(grad_arrived)).astype(BF16)
    grad_sent, grad_up, grad_down = lax.optimization_barrier((grad_sent, grad_up, grad_down))
    sum_up = lax.psum_scatter(grad_up, "dp", scatter_dimension=0, tiled=True)
    sum_down = lax.psum_scatter(grad_down, "dp", scatter_dimension=0, tiled=True)

    picked = contract(place, returned)
    output = (hidden_one + gate_value[:, None] * picked).astype(BF16)
    grad_gate = jnp.sum(grad_out * picked, axis=1)
    grad_logits = probs * (grad_gate[:, None] * chosen - (grad_gate * gate_value)[:, None])
    grad_router = lax.dot_general(
        grad_logits, norm_two, (((0,), (0,)), ((), ())),
        precision=lax.Precision.HIGHEST, preferred_element_type=F32,
    )
    grad_norm_two = contract(place, grad_sent) + lax.dot_general(
        grad_logits, router_f, (((1,), (0,)), ((), ())),
        precision=lax.Precision.HIGHEST, preferred_element_type=F32,
    )
    grad_ffn_gain = jnp.sum(grad_norm_two * hidden_one * r2, axis=0)
    scaled = ffn_f * grad_norm_two
    grad_hidden = (
        grad_out
        + r2 * scaled
        - hidden_one * (r2 * r2 * r2) * jnp.mean(hidden_one * scaled, axis=-1, keepdims=True)
    )

    grad_mixer = grad_hidden.astype(BF16)
    grad_output_w = contract(gated_low, grad_mixer)
    grad_gated = product_back(grad_mixer, w_output)
    gate_f = gate_in.astype(F32)
    sigma = jax.nn.sigmoid(gate_f)
    grad_scanned = grad_gated * (gate_f * sigma)
    grad_gate_in = (grad_gated * scanned.astype(F32) * (sigma * (1.0 + gate_f * (1.0 - sigma)))).astype(BF16)
    grad_scanned, sum_up = lax.optimization_barrier((grad_scanned, sum_up))
    later_grad = []
    for part in range(HALVES):
        rate_part = rate2[:, part * width // HALVES : (part + 1) * width // HALVES]
        start = start_grads(step_low, w_step, bias2, st, grad_scanned, rate2, c_wide, part, HALVES)
        start = jnp.concatenate([start, own_sums[part]])
        came = [shifted(start, "expert", -hop) for hop in hops]
        later_grad.append(entering([c[:states] for c in came], [total(c[states:]) for c in came], rate_part))
    grad_input_z = halved(contract(grad_gate_in, norm_own).astype(BF16), devices).reshape(width, model)
    grad_norm_z = product_back(grad_gate_in, w_input[:, width:])
    later_grad, sum_down, grad_output_w, grad_input_z, grad_norm_z = lax.optimization_barrier(
        (jnp.concatenate(later_grad, 1), sum_down, grad_output_w.astype(BF16), grad_input_z, grad_norm_z)
    )
    sum_output = lax.psum_scatter(grad_output_w, "dp", scatter_dimension=0, tiled=True)
    sum_input_z = lax.psum_scatter(grad_input_z, "dp", scatter_dimension=0, tiled=True)
    grad_pre_step, grad_inner, grad_decay_t, grad_skip, grad_b, grad_c = backward_scan(
        step_low, w_step, bias2, st, inner_low, grad_scanned, rate2, skip2,
        c_wide, b_block, one_block, history, marks, later_grad,
    )
    grad_pre_step, sum_output, sum_input_z = lax.optimization_barrier((grad_pre_step, sum_output, sum_input_z))
    grad_step_bias = jnp.sum(grad_pre_step.astype(F32), axis=0, keepdims=True)
    grad_step_w = contract(step_low, grad_pre_step)
    grad_step_low = product_back(grad_pre_step, w_step).astype(BF16)
    grad_selected = jnp.concatenate(
        [grad_step_low, grad_b[:, :states], grad_c[:, 0].reshape(rows, states).astype(BF16)], 1
    )
    grad_select_w = contract(grad_selected, inner_low)
    summed = stacked(
        [
            grad_select_w, grad_step_w, grad_decay_t, grad_step_bias, grad_skip,
            paired_rows(jnp.concatenate([grad_ffn_gain[None], grad_ffn_gain[None], grad_router], 0), devices),
        ]
    )
    share, norm_share = width // devices, model // devices
    summed_shape = (summed.shape[0], share)
    summed = shares(summed, devices)
    grad_inner, summed = lax.optimization_barrier((grad_inner, summed))
    grad_conv_in, grad_kernel, grad_conv_b = conv_back(
        mixed, grad_inner, slope_low, grad_selected, w_select, w_conv, ok
    )
    grad_norm_x = product_back(grad_conv_in, w_input[:, :width])
    returned_edge = shifted(grad_norm_x[PAD - taps + 1 : PAD], "expert", -1) * edge_keep
    grad_norm_one = grad_norm_x[PAD:] + grad_norm_z + jnp.pad(returned_edge, ((rows - taps + 1, 0), (0, 0)))
    grad_norm_gain = jnp.sum(grad_norm_one * hidden_in * norm_r, axis=0, keepdims=True)
    grad_input_x = halved(contract(grad_conv_in, norm_low).astype(BF16), devices)
    tiny = jnp.concatenate([shares(jnp.concatenate([grad_kernel, grad_conv_b]), devices), shares(grad_norm_gain, devices)], 1)
    rest = jnp.concatenate([summed, tiny.astype(BF16)], 1)
    more = -(-rest.shape[1] // model)
    more += -(more + share) % (8 * groups)
    rest = jnp.pad(rest, ((0, 0), (0, more * model - rest.shape[1]))).reshape(devices, more, model)
    packed = jnp.concatenate([grad_input_x, rest], axis=1).reshape(devices * (share + more), model)
    packed, sum_output, sum_input_z = lax.optimization_barrier((packed, sum_output, sum_input_z))
    packed = lax.psum_scatter(packed, "dp", scatter_dimension=0, tiled=True)
    sum_output, sum_input_z = expert_sum(sum_output, sum_input_z)
    scaled_one = norm_f * grad_norm_one
    grad_tokens = (
        grad_hidden
        + norm_r * scaled_one
        - hidden_in * (norm_r * norm_r * norm_r) * jnp.mean(hidden_in * scaled_one, axis=-1, keepdims=True)
    ).astype(BF16)
    packed, sum_output, sum_input_z, grad_tokens = lax.optimization_barrier((packed, sum_output, sum_input_z, grad_tokens))
    (packed,) = expert_sum(packed)
    sum_input_x, tiny = packed[:share], packed[share:].astype(F32).reshape(-1)
    summed = tiny[: summed_shape[0] * share].reshape(summed_shape)
    tiny = tiny[summed_shape[0] * share :]
    half = devices // 2
    low = lax.axis_index("dp") < half
    other = lax.ppermute(
        jnp.where(low, sum_input_z, sum_input_x), "dp", [(i, (i + half) % devices) for i in range(devices)]
    )
    own_half = jnp.where(low, sum_input_x, sum_input_z)
    sum_input = jnp.concatenate([jnp.where(low, own_half, other), jnp.where(low, other, own_half)])
    sum_kernel = tiny[: taps * share].reshape(taps, share)
    sum_conv_b = tiny[taps * share : (taps + 1) * share]
    sum_norm = tiny[(taps + 1) * share : (taps + 1) * share + norm_share]
    sum_select, sum_step, sum_decay, sum_step_b, sum_skip, singles = cut(
        summed, (w_select.shape[0], rank, states, 1, 1, (groups + 2) // 2)
    )
    singles = single_rows(singles, 1)
    sum_input, sum_output = sum_input.astype(F32).T, sum_output.astype(F32)
    return (
        output, grad_tokens, sum_input, sum_kernel, sum_conv_b, sum_select.T, sum_step, sum_step_b[0],
        sum_decay.T, sum_skip[0], sum_output, sum_norm, singles[1], singles[2:].T,
        sum_up.astype(F32).T[None], sum_down.astype(F32)[None],
    )


def solution(mesh):
    placed = (
        P(("dp", "expert"), None),
        P(("dp", "expert"), None),
        P(("dp", "expert"), None),
        P(("dp", "expert")),
        P(None, "dp"),
        P(None, "dp"),
        P("dp"),
        P("dp", None),
        P(None, "dp"),
        P("dp"),
        P("dp", None),
        P("dp"),
        P("dp", None),
        P("dp"),
        P("dp"),
        P("dp", None),
        P("expert", None, "dp"),
        P("expert", "dp", None),
    )
    return jax.shard_map(
        body,
        mesh=mesh,
        in_specs=placed,
        out_specs=(
            P(("dp", "expert"), None),
            P(("dp", "expert"), None),
            P(None, "dp"),
            P(None, "dp"),
            P("dp"),
            P("dp", None),
            P(None, "dp"),
            P("dp"),
            P("dp", None),
            P("dp"),
            P("dp", None),
            P("dp"),
            P("dp"),
            P("dp", None),
            P("expert", None, "dp"),
            P("expert", "dp", None),
        ),
        check_vma=False,
    )
```

```python
from functools import partial

import jax
import jax.numpy as jnp
from jax import lax
from jax.experimental import pallas as pl
from jax.experimental.pallas import tpu as pltpu
from jax.sharding import PartitionSpec as P

TC = 16
ROWS = 256
CONV_ROWS = 128
PAD = 16
UNROLL = 8
FAR = 1e4
LOG2E = 1.4426950408889634
LN2 = 0.6931471805599453
F32 = jnp.float32
BF16 = jnp.bfloat16


def tiled(x, n):
    return jnp.concatenate([x] * n, axis=1) if n > 1 else x


def folded(x):
    n = x.shape[1] // 128
    out = x[:, :128]
    for i in range(1, n):
        out = out + x[:, i * 128 : (i + 1) * 128]
    return out


def dot(a, b):
    return jnp.dot(a, b, preferred_element_type=F32)


def prepare(s_ref, w_ref, b_ref, st_ref, u_ref, dk_ref, dv_ref, pre_ref=None):
    size = min(s_ref.shape[0], ROWS)

    def block(i, carry):
        r = pl.ds(pl.multiple_of(i * size, size), size)
        pre = dot(s_ref[r, :], w_ref[...]) + b_ref[...].astype(F32)
        delta = jnp.maximum(pre, 0.0) + jnp.log1p(jnp.exp(-jnp.abs(pre)))
        dk = jnp.where(st_ref[r, :] > 0.0, FAR, delta)
        dk_ref[r, :] = dk
        if u_ref is not None:
            dv_ref[r, :] = delta * u_ref[r, :].astype(F32)
        if pre_ref is not None:
            pre_ref[r, :] = pre
        return carry + jnp.sum(dk, axis=0, keepdims=True)

    return lax.fori_loop(
        0, s_ref.shape[0] // size, block, jnp.zeros((1, w_ref.shape[1]), F32)
    )


def end_kernel(s_ref, w_ref, b_ref, st_ref, u_ref, a_ref, bb_ref, low_ref, dk_ref, dv_ref, out_ref):
    reps = w_ref.shape[1] // 128
    states = a_ref.shape[0]
    first = pl.program_id(1) == 0
    total = prepare(s_ref, w_ref, b_ref, st_ref, u_ref, dk_ref, dv_ref)
    a = a_ref[...]

    @pl.when(first)
    def _():
        out_ref[...] = jnp.zeros_like(out_ref)

    def chunk(c, h):
        t0 = pl.multiple_of(c * TC, TC)
        for i in range(TC):
            f = jnp.exp2(a * dk_ref[pl.ds(t0 + i, 1), :])
            h = f * h + dv_ref[pl.ds(t0 + i, 1), :] * tiled(bb_ref[t0 + i], reps)
        return h

    out_ref[:states, :] = lax.fori_loop(0, s_ref.shape[0] // TC, chunk, out_ref[:states, :])
    out_ref[states : states + 1, :] += total

    @pl.when(pl.program_id(1) == pl.num_programs(1) - 1)
    def _():
        low_ref[:states, :] = out_ref[:states, :].astype(BF16)
        sums = out_ref[states : states + 1, :]
        high = sums.astype(BF16).astype(F32)
        row = lax.broadcasted_iota(jnp.int32, (states, sums.shape[1]), 0)
        both = jnp.where(row == 0, high, jnp.where(row == 1, sums - high, 0.0))
        low_ref[states:, :] = both.astype(BF16)


def forward_kernel(
    s_ref, w_ref, b_ref, st_ref, u_ref, z_ref, a_ref, skip_ref, bb_ref, cm_ref, h0_ref,
    g_ref, y_ref, hs_ref, ck_ref, dk_ref, dv_ref, ys_ref, h_ref,
):
    reps = w_ref.shape[1] // 128
    states = a_ref.shape[0]
    chunks = s_ref.shape[0] // TC
    prepare(s_ref, w_ref, b_ref, st_ref, u_ref, dk_ref, dv_ref)
    a = a_ref[...]

    @pl.when(pl.program_id(1) == 0)
    def _():
        h_ref[...] = h0_ref[...]

    def scan(c, h):
        t0 = pl.multiple_of(c * TC, TC)
        r0 = pl.multiple_of(c * TC * states, TC * states)
        ck_ref[c] = h.astype(BF16)
        for i in range(TC):
            f = jnp.exp2(a * dk_ref[pl.ds(t0 + i, 1), :])
            h = f * h + dv_ref[pl.ds(t0 + i, 1), :] * tiled(bb_ref[t0 + i], reps)
            hs_ref[pl.ds(r0 + i * states, states), :] = h.astype(BF16)
        return h

    def emit(c):
        t0 = pl.multiple_of(c * TC, TC)
        r0 = pl.multiple_of(c * TC * states, TC * states)
        ys_ref[pl.ds(t0, TC), :] = dot(cm_ref[c], hs_ref[pl.ds(r0, TC * states), :])

    def group(j, h):
        for m in range(UNROLL):
            h = scan(UNROLL * j + m, h)
            emit(UNROLL * j + m)
        return h

    h_ref[...] = lax.fori_loop(0, chunks // UNROLL, group, h_ref[...])

    size = min(s_ref.shape[0], ROWS)

    def finish(i, carry):
        r = pl.ds(pl.multiple_of(i * size, size), size)
        y = ys_ref[r, :] + skip_ref[...].astype(F32) * u_ref[r, :].astype(F32)
        z = z_ref[r, :].astype(F32)
        y_ref[r, :] = y.astype(BF16)
        g_ref[r, :] = (y * (z / (1.0 + jnp.exp(-z)))).astype(BF16)
        return carry

    lax.fori_loop(0, s_ref.shape[0] // size, finish, 0)


def start_kernel(s_ref, w_ref, b_ref, st_ref, dy_ref, a_ref, cb_ref, low_ref, dk_ref, out_ref):
    reps = w_ref.shape[1] // 128
    chunks = s_ref.shape[0] // TC
    prepare(s_ref, w_ref, b_ref, st_ref, None, dk_ref, None)
    a = a_ref[...]

    @pl.when(pl.program_id(1) == 0)
    def _():
        out_ref[...] = jnp.zeros_like(out_ref)

    def chunk(j, grad):
        t0 = pl.multiple_of((chunks - 1 - j) * TC, TC)
        for i in range(TC - 1, -1, -1):
            f = jnp.exp2(a * dk_ref[pl.ds(t0 + i, 1), :])
            lam = grad + dy_ref[pl.ds(t0 + i, 1), :] * tiled(cb_ref[t0 + i], reps)
            grad = f * lam
        return grad

    out_ref[...] = lax.fori_loop(0, chunks, chunk, out_ref[...])

    @pl.when(pl.program_id(1) == pl.num_programs(1) - 1)
    def _():
        low_ref[...] = out_ref[...].astype(BF16)


def backward_kernel(
    s_ref, w_ref, b_ref, st_ref, u_ref, dy_ref, a_ref, skip_ref, cb_ref, bm_ref, om_ref, hs_ref, ck_ref, g0_ref,
    ds_ref, du_ref, da_ref, dskip_ref, db_ref, dc_ref,
    pre_ref, dk_ref, dv_ref, q_ref, p_ref, lb0, lb1, wb0, wb1, grad_ref, accb_ref, accc_ref,
):
    step, seg = pl.program_id(0), pl.program_id(1)
    last = pl.num_programs(1) - 1 - seg
    reps = w_ref.shape[1] // 128
    states = a_ref.shape[0]
    rows = s_ref.shape[0]
    chunks = rows // TC
    prepare(s_ref, w_ref, b_ref, st_ref, u_ref, dk_ref, dv_ref, pre_ref)
    token0 = pl.multiple_of(last * rows, rows)

    @pl.when((step == 0) & (seg == 0))
    def _():
        accb_ref[...] = jnp.zeros_like(accb_ref)
        accc_ref[...] = jnp.zeros_like(accc_ref)

    @pl.when(seg == 0)
    def _():
        grad_ref[...] = g0_ref[...]
        da_ref[...] = jnp.zeros_like(da_ref)
        dskip_ref[...] = jnp.zeros_like(dskip_ref)

    a = a_ref[...]
    a_low = a.astype(BF16)

    def scan(c, grad, lb, wb):
        t0 = pl.multiple_of(c * TC, TC)
        r0 = pl.multiple_of(c * TC * states, TC * states)
        da, four = None, None
        for i in range(TC - 1, -1, -1):
            d = dk_ref[pl.ds(t0 + i, 1), :]
            f = jnp.exp2(a * d)
            lam = grad + dy_ref[pl.ds(t0 + i, 1), :] * tiled(cb_ref[t0 + i], reps)
            grad = f * lam
            lb[pl.ds(i * states, states), :] = lam.astype(BF16)
            h = ck_ref[c] if i == 0 else hs_ref[pl.ds(r0 + (i - 1) * states, states), :]
            w = grad.astype(BF16) * h
            wb[pl.ds(i * states, states), :] = w * a_low
            wd = w * jnp.broadcast_to(d, w.shape).astype(BF16)
            four = wd if four is None else four + wd
            if i % 4 == 0:
                da = four.astype(F32) if da is None else da + four.astype(F32)
                four = None
            accb_ref[token0 + t0 + i] += folded(lam * dv_ref[pl.ds(t0 + i, 1), :])
        da_ref[...] += da
        return grad

    def emit(c, lb, wb):
        t0 = pl.multiple_of(c * TC, TC)
        r0 = pl.multiple_of(c * TC * states, TC * states)
        q_ref[pl.ds(t0, TC), :] = dot(bm_ref[c], lb[...])
        p_ref[pl.ds(t0, TC), :] = dot(om_ref[...], wb[...])
        accc_ref[last * chunks + c] += lax.dot_general(
            dy_ref[pl.ds(t0, TC), :].astype(BF16), hs_ref[pl.ds(r0, TC * states), :],
            (((1,), (1,)), ((), ())), preferred_element_type=F32,
        )

    def pair(j, grad):
        c = chunks - 1 - 2 * j
        grad = scan(c, grad, lb0, wb0)
        emit(c, lb0, wb0)
        grad = scan(c - 1, grad, lb1, wb1)
        emit(c - 1, lb1, wb1)
        return grad

    grad_ref[...] = lax.fori_loop(0, chunks // 2, pair, grad_ref[...])

    @pl.when(last == 0)
    def _():
        da_ref[...] = da_ref[...] * a * LN2

    size = min(s_ref.shape[0], ROWS)

    def finish(i, carry):
        r = pl.ds(pl.multiple_of(i * size, size), size)
        u = u_ref[r, :].astype(F32)
        q = q_ref[r, :]
        dy = dy_ref[r, :]
        pre = pre_ref[r, :]
        delta = jnp.maximum(pre, 0.0) + jnp.log1p(jnp.exp(-jnp.abs(pre)))
        dd = p_ref[r, :] * LN2 + u * q
        ds_ref[r, :] = (dd / (1.0 + jnp.exp(-pre))).astype(BF16)
        du_ref[r, :] = delta * q + dy * skip_ref[...].astype(F32)
        return carry + jnp.sum(dy * u, axis=0, keepdims=True)

    dskip_ref[...] += lax.fori_loop(0, rows // size, finish, jnp.zeros(dskip_ref.shape, F32))

    @pl.when((step == pl.num_programs(0) - 1) & (last == 0))
    def _():
        ones = jnp.ones((128, 128), BF16)
        row = lax.broadcasted_iota(jnp.int32, (TC * states, 128), 0) % states
        lane = lax.broadcasted_iota(jnp.int32, (TC * states, 128), 1)

        def gather(c, carry):
            t0 = pl.multiple_of(c * TC, TC)
            b = dot(accb_ref[pl.ds(t0, TC)].reshape(TC * states, 128).astype(BF16), ones)
            db_ref[pl.ds(t0, TC), :] = dot(om_ref[...], jnp.where(lane == row, b, 0.0).astype(BF16)).astype(BF16)
            own = om_ref[...].astype(F32) * accc_ref[c]
            dc_ref[c] = jnp.broadcast_to(jnp.sum(own, axis=0, keepdims=True), dc_ref.shape[1:])
            return carry

        lax.fori_loop(0, accc_ref.shape[0], gather, 0)


def conv_kernel_back(xs_ref, du_ref, slope_ref, dp_ref, sel_ref, k_ref, ok_ref, dxs_ref, dk_ref, db_ref, dc_ref):
    taps = k_ref.shape[0]
    rows = du_ref.shape[0]
    k = k_ref[...].astype(F32)
    dc_ref[:PAD, :] = jnp.zeros((PAD, dc_ref.shape[1]), F32)
    dc_ref[pl.ds(rows + PAD, PAD), :] = jnp.zeros((PAD, dc_ref.shape[1]), F32)

    def first(i, carry):
        t0 = pl.multiple_of(i * CONV_ROWS, CONV_ROWS)
        at = pl.ds(t0, CONV_ROWS)
        du = du_ref[at, :] + dot(dp_ref[at, :], sel_ref[...])
        dc = du * slope_ref[at, :].astype(F32)
        dc_ref[pl.ds(t0 + PAD, CONV_ROWS), :] = dc
        slab = xs_ref[pl.ds(t0, CONV_ROWS + PAD), :].astype(F32)
        sums = [jnp.sum(dc, axis=0, keepdims=True)]
        for lag in range(taps):
            x = slab[PAD - lag : PAD - lag + CONV_ROWS]
            part = dc * x
            if lag:
                part = part * ok_ref[pl.ds(t0 + PAD, CONV_ROWS), lag : lag + 1]
            sums.append(jnp.sum(part, axis=0, keepdims=True))
        return tuple(a + b for a, b in zip(carry, sums))

    size = max(n for n in range(PAD, 129, PAD) if (rows + PAD) % n == 0)
    zero = jnp.zeros((1, k.shape[1]), F32)
    sums = lax.fori_loop(0, rows // CONV_ROWS, first, (zero,) * (taps + 1))
    db_ref[...] = sums[0]
    for lag in range(taps):
        dk_ref[taps - 1 - lag : taps - lag, :] = sums[1 + lag]

    def second(i, carry):
        r0 = pl.multiple_of(i * size, PAD)
        slab = dc_ref[pl.ds(r0, size + PAD), :]
        ok = ok_ref[pl.ds(r0, size + PAD), :]
        out = k[taps - 1 : taps] * slab[:size]
        for lag in range(1, taps):
            part = (ok[:, lag : lag + 1] * slab)[lag : lag + size]
            out = out + k[taps - 1 - lag : taps - lag] * part
        dxs_ref[pl.ds(r0, size), :] = out.astype(BF16)
        return carry

    lax.fori_loop(0, (rows + PAD) // size, second, 0)


def conv_back(xs, du, slope, dp, sel, k, ok):
    rows, width = du.shape
    cb = scan_width(width, 768)
    col = lambda n: pl.BlockSpec((n, cb), lambda i: (0, i))
    whole = lambda x: pl.BlockSpec(x.shape, lambda i: (0, 0))
    taps = k.shape[0]
    return pl.pallas_call(
        conv_kernel_back,
        grid=(width // cb,),
        in_specs=[col(rows + PAD), col(rows), col(rows), whole(dp), col(sel.shape[0]), col(taps), whole(ok)],
        out_specs=[col(rows + PAD), col(taps), col(1)],
        out_shape=[sds((rows + PAD, width), BF16), sds((taps, width), F32), sds((1, width), F32)],
        scratch_shapes=[pltpu.VMEM((rows + 2 * PAD, cb), F32)],
        compiler_params=params(),
        cost_estimate=pl.CostEstimate(flops=rows * width * 300, bytes_accessed=rows * width * 8, transcendentals=0),
        name="conv_back",
    )(xs, du, slope, dp, sel, k, ok)


def scan_width(width, limit):
    n = width // 128
    best = max(d for d in range(1, n + 1) if n % d == 0 and d * 128 <= limit)
    return best * 128


def params():
    return pltpu.CompilerParams(vmem_limit_bytes=60 * 2**20)


def sds(*a):
    return jax.ShapeDtypeStruct(*a)


class Blocks:
    def __init__(self, rows, width, cb, parts, reverse=False, first=0):
        self.first = first
        self.grid = (width // cb, parts)
        self.cb, self.rows, self.seg = cb, rows, rows // parts
        self.at = (lambda s: parts - 1 - s) if reverse else (lambda s: s)

    def token(self, n):
        return pl.BlockSpec((self.seg, n), lambda k, s: (self.at(s), 0))

    def channel(self, n):
        return pl.BlockSpec((n, self.cb), lambda k, s: (0, k + self.first))

    def both(self, times=1, off=0):
        return pl.BlockSpec((self.seg * times, self.cb), lambda k, s: (self.at(s), k + self.first + off))

    def lead(self, n, *rest):
        return pl.BlockSpec((n, *rest), lambda k, s: (self.at(s),) + (0,) * len(rest))

    def marks(self, states):
        return pl.BlockSpec((self.seg // TC, states, self.cb), lambda k, s: (self.at(s), 0, k))

    def whole(self, shape):
        return pl.BlockSpec(shape, lambda k, s: (0,) * len(shape))


def estimate(rows, width, states, ops, size):
    return pl.CostEstimate(
        flops=ops * rows * width * states, bytes_accessed=rows * width * size, transcendentals=rows * width * states
    )


END, FORWARD, START, BACKWARD = (1152, 3), (1152, 6), (1152, 3), (2304, 24)


def end_states(s, w, b, st, u, a, bb, part, of):
    rows, width, states = s.shape[0], w.shape[1] // of, a.shape[0]
    cb = min(END[0], width)
    k = Blocks(rows, width, cb, END[1], first=part * (width // cb))
    return pl.pallas_call(
        end_kernel,
        grid=k.grid,
        in_specs=[k.token(s.shape[1]), k.channel(w.shape[0]), k.channel(1), k.token(1), k.both(), k.channel(states), k.lead(k.seg, states, 128)],
        out_specs=pl.BlockSpec((2 * states, cb), lambda i, j: (0, i)),
        out_shape=sds((2 * states, width), BF16),
        scratch_shapes=[pltpu.VMEM((k.seg, k.cb), F32)] * 2 + [pltpu.VMEM((states + 8, k.cb), F32)],
        compiler_params=params(),
        cost_estimate=estimate(rows, width, states, 6, 8),
        name="end_states",
    )(s, w, b, st, u, a, bb)


def forward_scan(s, w, b, st, u, z, a, skip, bb, cm, h0):
    rows, width, states = s.shape[0], w.shape[1], a.shape[0]
    k = Blocks(rows, width, *FORWARD)
    return pl.pallas_call(
        forward_kernel,
        grid=k.grid,
        in_specs=[k.token(s.shape[1]), k.channel(w.shape[0]), k.channel(1), k.token(1), k.both(), k.both(), k.channel(states), k.channel(1),
                  k.lead(k.seg, states, 128), k.lead(k.seg // TC, *cm.shape[1:]), k.channel(states)],
        out_specs=[k.both(), k.both(), k.both(states), k.marks(states)],
        out_shape=[sds((rows, width), BF16), sds((rows, width), BF16), sds((rows * states, width), BF16), sds((rows // TC, states, width), BF16)],
        scratch_shapes=[pltpu.VMEM((k.seg, k.cb), F32)] * 3 + [pltpu.VMEM((states, k.cb), F32)],
        compiler_params=params(),
        cost_estimate=estimate(rows, width, states, 9, 44),
        name="forward_scan",
    )(s, w, b, st, u, z, a, skip, bb, cm, h0)


def start_grads(s, w, b, st, dy, a, cb_wide, part, of):
    rows, width, states = s.shape[0], w.shape[1] // of, a.shape[0]
    cb = min(START[0], width)
    k = Blocks(rows, width, cb, START[1], reverse=True, first=part * (width // cb))
    return pl.pallas_call(
        start_kernel,
        grid=k.grid,
        in_specs=[k.token(s.shape[1]), k.channel(w.shape[0]), k.channel(1), k.token(1), k.both(), k.channel(states), k.lead(k.seg, states, 128)],
        out_specs=pl.BlockSpec((states, cb), lambda i, j: (0, i)),
        out_shape=sds((states, width), BF16),
        scratch_shapes=[pltpu.VMEM((k.seg, k.cb), F32), pltpu.VMEM((states, k.cb), F32)],
        compiler_params=params(),
        cost_estimate=estimate(rows, width, states, 6, 8),
        name="start_grads",
    )(s, w, b, st, dy, a, cb_wide)


def backward_scan(s, w, b, st, u, dy, a, skip, cb, bm, om, hs, ck, g0):
    rows, width, states = s.shape[0], w.shape[1], a.shape[0]
    k = Blocks(rows, width, *BACKWARD, reverse=True)
    chunks = rows // TC
    return pl.pallas_call(
        backward_kernel,
        grid=k.grid,
        in_specs=[k.token(s.shape[1]), k.channel(w.shape[0]), k.channel(1), k.token(1), k.both(), k.both(), k.channel(states), k.channel(1),
                  k.lead(k.seg, states, 128), k.lead(k.seg // TC, *bm.shape[1:]), k.whole(om.shape), k.both(states), k.marks(states), k.channel(states)],
        out_specs=[k.both(), k.both(), k.channel(states), k.channel(1), k.whole((rows, 128)), k.whole((chunks, 8, TC * states))],
        out_shape=[sds((rows, width), BF16), sds((rows, width), F32), sds((states, width), F32), sds((1, width), F32),
                   sds((rows, 128), BF16), sds((chunks, 8, TC * states), F32)],
        scratch_shapes=[pltpu.VMEM((k.seg, k.cb), F32)] * 5
        + [pltpu.VMEM((TC * states, k.cb), BF16)] * 4
        + [pltpu.VMEM((states, k.cb), F32), pltpu.VMEM((rows, states, 128), F32), pltpu.VMEM((chunks, TC, TC * states), F32)],
        compiler_params=params(),
        cost_estimate=estimate(rows, width, states, 18, 44),
        name="backward_scan",
    )(s, w, b, st, u, dy, a, skip, cb, bm, om, hs, ck, g0)


def spread(coeff):
    return jnp.broadcast_to(coeff[:, :, None], (*coeff.shape, 128))


def block_rows(coeff):
    rows, states = coeff.shape
    mask = jnp.arange(TC * states)[None, None] // states == jnp.arange(TC)[None, :, None]
    return jnp.where(mask, coeff.reshape(rows // TC, 1, TC * states), 0.0).astype(BF16)


epsilon = 1e-05
HALVES = 2


def shifted(array, axis, by):
    length = lax.axis_size(axis)
    pairs = [(i, i + by) for i in range(length) if 0 <= i + by < length]
    return lax.ppermute(array, axis, pairs)


def entering(came, sums, rate2):
    state, decay = jnp.zeros_like(rate2), jnp.zeros((1, rate2.shape[1]), F32)
    for end, total in zip(came, sums):
        state = state + jnp.exp2(rate2 * decay) * end.astype(F32)
        decay = decay + total
    return state


def product_back(left, right):
    return lax.dot_general(left, right, (((1,), (1,)), ((), ())), preferred_element_type=F32)


def contract(left, right):
    return lax.dot_general(left, right, (((0,), (0,)), ((), ())), preferred_element_type=F32)


def silu_slope(values):
    sigma = jax.nn.sigmoid(values)
    return sigma * (1.0 + values * (1.0 - sigma))


def inverse_rms(values):
    return lax.rsqrt(jnp.mean(values * values, axis=-1, keepdims=True) + epsilon)


def paired_rows(rows, devices):
    r, d = rows.shape
    split = rows.reshape(r // 2, 2, devices, d // devices)
    return split.transpose(0, 2, 1, 3).reshape(r // 2, 2 * d)


def single_rows(rows, devices):
    r, d = rows.shape
    split = rows.reshape(r, devices, 2, d // (2 * devices))
    return split.transpose(0, 2, 1, 3).reshape(2 * r, d // 2)


def stacked(parts):
    whole = jnp.concatenate([p.astype(BF16) for p in parts], axis=0)
    return jnp.pad(whole, ((0, -whole.shape[0] % 16), (0, 0)))


def expert_part(parts):
    n, here = lax.axis_size("expert"), lax.axis_index("expert")
    part = lambda k: lax.dynamic_index_in_dim(parts, jnp.mod(here + k, n), 0, keepdims=False)
    total = part(0).astype(F32)
    for k in range(1, n):
        total = total + turned(part(k), k).astype(F32)
    return total.astype(BF16)


def turned(x, k):
    n = lax.axis_size("expert")
    return lax.ppermute(x, "expert", [(i, (i + k) % n) for i in range(n)]) if k else x


def in_order(came):
    n, here = lax.axis_size("expert"), lax.axis_index("expert")
    return lax.dynamic_slice_in_dim(jnp.stack(came[::-1] * 2), n - 1 - here, n, 0)


def expert_sum(*arrays):
    n = lax.axis_size("expert")
    split = [x.reshape(n, x.shape[0] // n, x.shape[1]) for x in arrays]
    padded = [jnp.pad(x, ((0, 0), (0, -x.shape[1] % 8), (0, 0))) for x in split]
    total = expert_part(jnp.concatenate(padded, axis=1))
    every = in_order([turned(total, k) for k in range(n)])
    out, at = [], 0
    for x, p in zip(split, padded):
        out.append(every[:, at : at + x.shape[1]].reshape(n * x.shape[1], x.shape[2]))
        at += p.shape[1]
    return out


def shares(rows, devices):
    r, columns = rows.shape
    return rows.reshape(r, devices, columns // devices).transpose(1, 0, 2).reshape(devices, -1)


def halved(grads, devices):
    rows, columns = grads.shape
    split = grads.reshape(devices // 2, 2, rows // devices, columns)
    return split.transpose(1, 0, 2, 3).reshape(devices, rows // devices, columns)


def cut(whole, counts):
    out, at = [], 0
    for n in counts:
        out.append(whole[at : at + n])
        at += n
    return out


def body(
    tokens, cotangent, routes, starts, input_proj, conv_kernel, conv_bias, select_proj, step_proj,
    step_bias, decay_log, skip_gain, output_proj, norm_gain, ffn_gain, router, expert_up, expert_down,
):
    devices = lax.axis_size("dp")
    groups = lax.axis_size("expert")
    rows, model = tokens.shape
    taps, rank, states = conv_kernel.shape[0], step_proj.shape[0], decay_log.shape[1]
    capacity = 2 * rows // groups
    w_input = lax.all_gather(input_proj, "dp", axis=1, tiled=True)
    small = stacked(
        [
            select_proj.T, step_proj, decay_log.T, conv_kernel, conv_bias[None], step_bias[None], skip_gain[None],
            paired_rows(jnp.concatenate([norm_gain[None], ffn_gain[None], router.T], 0), 1),
        ]
    )
    counts = (select_proj.shape[1], rank, states, taps, 1, 1, 1, (groups + 2) // 2)
    w_select, w_step, w_decay, w_conv, b_conv, bias2, skip2, singles = cut(
        lax.all_gather(small, "dp", axis=1, tiled=True), counts
    )
    singles = single_rows(singles, devices).astype(F32)
    norm_f, ffn_f, router_f = singles[0], singles[1], singles[2:]
    w_output = lax.all_gather(output_proj, "dp", axis=0, tiled=True)
    w_up = lax.all_gather(expert_up[0], "dp", axis=1, tiled=True)
    w_down = lax.all_gather(expert_down[0], "dp", axis=0, tiled=True)
    width = w_select.shape[1]
    conv_f = w_conv.astype(F32)

    route = routes[:, 0]
    chosen = (route[:, None] == jnp.arange(groups, dtype=jnp.int32)[None, :]).astype(F32)
    before = (jnp.arange(rows)[:, None] > jnp.arange(rows)[None, :]).astype(BF16)
    ranks = dot(before, chosen.astype(BF16))
    slot = jnp.sum(ranks * chosen, axis=1).astype(jnp.int32)
    assert groups & (groups - 1) == 0
    distance = jnp.bitwise_xor(route, lax.axis_index("expert"))
    target = jnp.where(slot < capacity, distance * capacity + slot, groups * capacity)
    place = (jnp.arange(groups * capacity)[:, None] == target[None, :]).astype(BF16)

    hidden_in = tokens.astype(F32)
    norm_r = inverse_rms(hidden_in)
    norm_own = (hidden_in * norm_r * norm_f).astype(BF16)
    flag = starts.astype(F32)
    same = 1.0 - flag
    valid = [jnp.ones((rows,), F32)]
    for lag in range(1, taps):
        moved = jnp.concatenate([jnp.ones((lag - 1,), F32), same[: rows - lag + 1]])
        valid.append(valid[-1] * moved)
    edge = [jnp.ones((), F32)]
    for lag in range(1, taps - 1):
        edge.append(edge[-1] * same[rows - lag])
    edge_keep = jnp.stack(edge[::-1])[:, None]
    tail = (norm_own[rows - taps + 1 :].astype(F32) * edge_keep).astype(BF16)
    borrowed = shifted(tail, "expert", 1)
    norm_low = jnp.concatenate([jnp.zeros((PAD - taps + 1, model), BF16), borrowed, norm_own], 0)
    ok = jnp.pad(jnp.stack(valid, 1), ((PAD, PAD), (0, 0)))
    norm_low, ok = lax.optimization_barrier((norm_low, ok))
    conv_in = dot(norm_low, w_input[:, :width]).astype(BF16)
    conv_sum = jnp.broadcast_to(b_conv.astype(F32), (rows, width))
    for lag in range(taps):
        conv_sum = conv_sum + valid[lag][:, None] * conv_f[taps - 1 - lag] * conv_in[PAD - lag : PAD - lag + rows].astype(F32)
    inner_low = jax.nn.silu(conv_sum).astype(BF16)
    slope_low = silu_slope(conv_sum).astype(BF16)
    selected = product_back(inner_low, w_select)
    step_low = selected[:, :rank].astype(BF16)
    b_coeff = selected[:, rank : rank + states]
    c_coeff = selected[:, rank + states :]
    rate2 = -jnp.exp(w_decay.astype(F32)) * LOG2E
    st = flag[:, None]
    b_wide, c_wide = spread(b_coeff), spread(c_coeff)
    b_block, c_block = block_rows(b_coeff), block_rows(c_coeff)
    one_block = (jnp.arange(TC * states)[None] // states == jnp.arange(TC)[:, None]).astype(BF16)
    hops = range(1, groups)
    own_sums, start_state = [], []
    for part in range(HALVES):
        rate_part = rate2[:, part * width // HALVES : (part + 1) * width // HALVES]
        end = end_states(step_low, w_step, bias2, st, inner_low, rate2, b_wide, part, HALVES)
        came = [shifted(end, "expert", hop) for hop in hops]
        total = lambda x: x[:1].astype(F32) + x[1:2].astype(F32)
        own_sums.append(end[states : states + 8])
        start_state.append(entering([c[:states] for c in came], [total(c[states:]) for c in came], rate_part))
    start_state = jnp.concatenate(start_state, 1)
    norm_late, _ = lax.optimization_barrier((norm_own, end))
    gate_in = dot(norm_late, w_input[:, width:]).astype(BF16)
    gated_low, scanned, history, marks = forward_scan(
        step_low, w_step, bias2, st, inner_low, gate_in, rate2, skip2, b_wide, c_block, start_state
    )
    hidden_one = hidden_in + dot(gated_low, w_output)

    r2 = inverse_rms(hidden_one)
    norm_two = hidden_one * r2 * ffn_f
    logits = lax.dot_general(
        norm_two, router_f, (((1,), (1,)), ((), ())),
        precision=lax.Precision.HIGHEST, preferred_element_type=F32,
    )
    probs = jax.nn.softmax(logits, axis=-1)
    gate_value = jnp.sum(probs * chosen, axis=-1)
    grad_out = cotangent.astype(F32)
    grad_picked = (gate_value[:, None] * grad_out).astype(BF16)

    def swapped(x, k):
        return lax.ppermute(x, "expert", [(i, i ^ k) for i in range(groups)]) if k else x

    places = [place[k * capacity : (k + 1) * capacity] for k in range(groups)]
    norm_two_low = norm_two.astype(BF16)
    arrived, grad_arrived = [None] * groups, [None] * groups
    far_first = list(range(groups - 1, 0, -1))
    for k in far_first + [0]:
        arrived[k] = swapped(dot(places[k], norm_two_low).astype(BF16), k)
    for k in far_first + [0]:
        sent = dot(places[k], grad_picked).astype(BF16)
        if k:
            sent, arrived[k] = lax.optimization_barrier((sent, arrived[k]))
        grad_arrived[k] = swapped(sent, k)
    up_low, grad_pre, outs, ins = ([None] * groups for _ in range(4))
    for k in [0] + far_first:
        up_pre = dot(arrived[k], w_up)
        act, gelu_back = jax.vjp(jax.nn.gelu, up_pre)
        up_low[k] = act.astype(BF16)
        outs[k] = dot(up_low[k], w_down).astype(BF16)
        grad_pre[k] = gelu_back(product_back(grad_arrived[k], w_down))[0].astype(BF16)
        ins[k] = product_back(grad_pre[k], w_up).astype(BF16)
    returned = [None] * groups
    grad_sent = [None] * groups
    for k in far_first + [0]:
        returned[k] = swapped(outs[k], k)
    for k in far_first + [0]:
        grad_sent[k] = swapped(ins[k], k)
    returned, grad_sent = jnp.concatenate(returned), jnp.concatenate(grad_sent)
    up_low, grad_pre, arrived, grad_arrived, _, _ = lax.optimization_barrier(
        (up_low, grad_pre, arrived, grad_arrived, outs, ins)
    )
    grad_up = contract(jnp.concatenate(grad_pre), jnp.concatenate(arrived)).astype(BF16)
    grad_down = contract(jnp.concatenate(up_low), jnp.concatenate(grad_arrived)).astype(BF16)
    grad_sent, grad_up, grad_down, c_wide, b_block = lax.optimization_barrier(
        (grad_sent, grad_up, grad_down, c_wide, b_block)
    )
    sum_up = lax.psum_scatter(grad_up, "dp", scatter_dimension=0, tiled=True)
    sum_down = lax.psum_scatter(grad_down, "dp", scatter_dimension=0, tiled=True)

    picked = contract(place, returned)
    output = (hidden_one + gate_value[:, None] * picked).astype(BF16)
    grad_gate = jnp.sum(grad_out * picked, axis=1)
    grad_logits = probs * (grad_gate[:, None] * chosen - (grad_gate * gate_value)[:, None])
    grad_router = lax.dot_general(
        grad_logits, norm_two, (((0,), (0,)), ((), ())),
        precision=lax.Precision.HIGHEST, preferred_element_type=F32,
    )
    grad_norm_two = contract(place, grad_sent) + lax.dot_general(
        grad_logits, router_f, (((1,), (0,)), ((), ())),
        precision=lax.Precision.HIGHEST, preferred_element_type=F32,
    )
    grad_ffn_gain = jnp.sum(grad_norm_two * hidden_one * r2, axis=0)
    scaled = ffn_f * grad_norm_two
    grad_hidden = (
        grad_out
        + r2 * scaled
        - hidden_one * (r2 * r2 * r2) * jnp.mean(hidden_one * scaled, axis=-1, keepdims=True)
    )

    grad_mixer = grad_hidden.astype(BF16)
    grad_output_w = contract(gated_low, grad_mixer)
    grad_gated = product_back(grad_mixer, w_output)
    gate_f = gate_in.astype(F32)
    sigma = jax.nn.sigmoid(gate_f)
    grad_scanned = grad_gated * (gate_f * sigma)
    grad_gate_in = (grad_gated * scanned.astype(F32) * (sigma * (1.0 + gate_f * (1.0 - sigma)))).astype(BF16)
    grad_scanned, sum_up = lax.optimization_barrier((grad_scanned, sum_up))
    later_grad = []
    for part in range(HALVES):
        rate_part = rate2[:, part * width // HALVES : (part + 1) * width // HALVES]
        start = start_grads(step_low, w_step, bias2, st, grad_scanned, rate2, c_wide, part, HALVES)
        start = jnp.concatenate([start, own_sums[part]])
        came = [shifted(start, "expert", -hop) for hop in hops]
        later_grad.append(entering([c[:states] for c in came], [total(c[states:]) for c in came], rate_part))
    grad_input_z = halved(contract(grad_gate_in, norm_own).astype(BF16), devices).reshape(width, model)
    grad_norm_z = product_back(grad_gate_in, w_input[:, width:])
    later_grad, sum_down, grad_output_w, grad_input_z, grad_norm_z = lax.optimization_barrier(
        (jnp.concatenate(later_grad, 1), sum_down, grad_output_w.astype(BF16), grad_input_z, grad_norm_z)
    )
    sum_output = lax.psum_scatter(grad_output_w, "dp", scatter_dimension=0, tiled=True)
    sum_input_z = lax.psum_scatter(grad_input_z, "dp", scatter_dimension=0, tiled=True)
    grad_pre_step, grad_inner, grad_decay_t, grad_skip, grad_b, grad_c = backward_scan(
        step_low, w_step, bias2, st, inner_low, grad_scanned, rate2, skip2,
        c_wide, b_block, one_block, history, marks, later_grad,
    )
    grad_pre_step, sum_output, sum_input_z = lax.optimization_barrier((grad_pre_step, sum_output, sum_input_z))
    grad_step_bias = jnp.sum(grad_pre_step.astype(F32), axis=0, keepdims=True)
    grad_step_w = contract(step_low, grad_pre_step)
    grad_step_low = product_back(grad_pre_step, w_step).astype(BF16)
    grad_selected = jnp.concatenate(
        [grad_step_low, grad_b[:, :states], grad_c[:, 0].reshape(rows, states).astype(BF16)], 1
    )
    grad_select_w = contract(grad_selected, inner_low)
    summed = stacked(
        [
            grad_select_w, grad_step_w, grad_decay_t, grad_step_bias, grad_skip,
            paired_rows(jnp.concatenate([grad_ffn_gain[None], grad_ffn_gain[None], grad_router], 0), devices),
        ]
    )
    share, norm_share = width // devices, model // devices
    summed_shape = (summed.shape[0], share)
    summed = shares(summed, devices)
    grad_inner, summed = lax.optimization_barrier((grad_inner, summed))
    grad_conv_in, grad_kernel, grad_conv_b = conv_back(
        conv_in, grad_inner, slope_low, grad_selected, w_select, w_conv, ok
    )
    grad_norm_x = product_back(grad_conv_in, w_input[:, :width])
    returned_edge = shifted(grad_norm_x[PAD - taps + 1 : PAD], "expert", -1) * edge_keep
    grad_norm_one = grad_norm_x[PAD:] + grad_norm_z + jnp.pad(returned_edge, ((rows - taps + 1, 0), (0, 0)))
    grad_norm_gain = jnp.sum(grad_norm_one * hidden_in * norm_r, axis=0, keepdims=True)
    grad_input_x = halved(contract(grad_conv_in, norm_low).astype(BF16), devices)
    tiny = jnp.concatenate([shares(jnp.concatenate([grad_kernel, grad_conv_b]), devices), shares(grad_norm_gain, devices)], 1)
    rest = jnp.concatenate([summed, tiny.astype(BF16)], 1)
    more = -(-rest.shape[1] // model)
    more += -(more + share) % (8 * groups)
    rest = jnp.pad(rest, ((0, 0), (0, more * model - rest.shape[1]))).reshape(devices, more, model)
    packed = jnp.concatenate([grad_input_x, rest], axis=1).reshape(devices * (share + more), model)
    packed, sum_output, sum_input_z = lax.optimization_barrier((packed, sum_output, sum_input_z))
    packed = lax.psum_scatter(packed, "dp", scatter_dimension=0, tiled=True)
    sum_output, sum_input_z = expert_sum(sum_output, sum_input_z)
    scaled_one = norm_f * grad_norm_one
    grad_tokens = (
        grad_hidden
        + norm_r * scaled_one
        - hidden_in * (norm_r * norm_r * norm_r) * jnp.mean(hidden_in * scaled_one, axis=-1, keepdims=True)
    ).astype(BF16)
    half = devices // 2
    other_z = lax.ppermute(sum_input_z, "dp", [(d, d + half) for d in range(half)])
    packed, sum_output, sum_input_z, other_z, grad_tokens = lax.optimization_barrier(
        (packed, sum_output, sum_input_z, other_z, grad_tokens)
    )
    part = expert_part(packed.reshape(groups, -1, model))
    across = [
        lax.ppermute(
            part, ("dp", "expert"),
            [(d * groups + z, (d - half) * groups + (z + k) % groups) for d in range(half, devices) for z in range(groups)],
        )
        for k in range(groups)
    ]
    packed = in_order([turned(part, k) for k in range(groups)]).reshape(-1, model)
    other_x = in_order(across).reshape(-1, model)[:share]
    sum_input_x, tiny = packed[:share], packed[share:].astype(F32).reshape(-1)
    summed = tiny[: summed_shape[0] * share].reshape(summed_shape)
    tiny = tiny[summed_shape[0] * share :]
    low = lax.axis_index("dp") < half
    sum_input = jnp.concatenate([jnp.where(low, sum_input_x, other_z), jnp.where(low, other_x, sum_input_z)])
    sum_kernel = tiny[: taps * share].reshape(taps, share)
    sum_conv_b = tiny[taps * share : (taps + 1) * share]
    sum_norm = tiny[(taps + 1) * share : (taps + 1) * share + norm_share]
    sum_select, sum_step, sum_decay, sum_step_b, sum_skip, singles = cut(
        summed, (w_select.shape[0], rank, states, 1, 1, (groups + 2) // 2)
    )
    singles = single_rows(singles, 1)
    sum_input, sum_output = sum_input.astype(F32).T, sum_output.astype(F32)
    return (
        output, grad_tokens, sum_input, sum_kernel, sum_conv_b, sum_select.T, sum_step, sum_step_b[0],
        sum_decay.T, sum_skip[0], sum_output, sum_norm, singles[1], singles[2:].T,
        sum_up.astype(F32).T[None], sum_down.astype(F32)[None],
    )


def solution(mesh):
    placed = (
        P(("dp", "expert"), None),
        P(("dp", "expert"), None),
        P(("dp", "expert"), None),
        P(("dp", "expert")),
        P(None, "dp"),
        P(None, "dp"),
        P("dp"),
        P("dp", None),
        P(None, "dp"),
        P("dp"),
        P("dp", None),
        P("dp"),
        P("dp", None),
        P("dp"),
        P("dp"),
        P("dp", None),
        P("expert", None, "dp"),
        P("expert", "dp", None),
    )
    return jax.shard_map(
        body,
        mesh=mesh,
        in_specs=placed,
        out_specs=(
            P(("dp", "expert"), None),
            P(("dp", "expert"), None),
            P(None, "dp"),
            P(None, "dp"),
            P("dp"),
            P("dp", None),
            P(None, "dp"),
            P("dp"),
            P("dp", None),
            P("dp"),
            P("dp", None),
            P("dp"),
            P("dp"),
            P("dp", None),
            P("expert", None, "dp"),
            P("expert", "dp", None),
        ),
        check_vma=False,
    )
```

```python
from functools import partial

import jax
import jax.numpy as jnp
from jax import lax
from jax.experimental import pallas as pl
from jax.experimental.pallas import tpu as pltpu
from jax.sharding import PartitionSpec as P

TC = 16
ROWS = 256
CONV_ROWS = 128
PAD = 16
UNROLL = 8
FAR = 1e4
LOG2E = 1.4426950408889634
LN2 = 0.6931471805599453
F32 = jnp.float32
BF16 = jnp.bfloat16


def tiled(x, n):
    return jnp.concatenate([x] * n, axis=1) if n > 1 else x


def folded(x):
    n = x.shape[1] // 128
    out = x[:, :128]
    for i in range(1, n):
        out = out + x[:, i * 128 : (i + 1) * 128]
    return out


def dot(a, b):
    return jnp.dot(a, b, preferred_element_type=F32)


def prepare(s_ref, w_ref, b_ref, st_ref, u_ref, dk_ref, dv_ref, pre_ref=None):
    size = min(s_ref.shape[0], ROWS)

    def block(i, carry):
        r = pl.ds(pl.multiple_of(i * size, size), size)
        pre = dot(s_ref[r, :], w_ref[...]) + b_ref[...].astype(F32)
        delta = jnp.maximum(pre, 0.0) + jnp.log1p(jnp.exp(-jnp.abs(pre)))
        dk = jnp.where(st_ref[r, :] > 0.0, FAR, delta)
        dk_ref[r, :] = dk
        if u_ref is not None:
            dv_ref[r, :] = delta * u_ref[r, :].astype(F32)
        if pre_ref is not None:
            pre_ref[r, :] = pre
        return carry + jnp.sum(dk, axis=0, keepdims=True)

    return lax.fori_loop(
        0, s_ref.shape[0] // size, block, jnp.zeros((1, w_ref.shape[1]), F32)
    )


def end_kernel(s_ref, w_ref, b_ref, st_ref, u_ref, a_ref, bb_ref, low_ref, dk_ref, dv_ref, out_ref):
    reps = w_ref.shape[1] // 128
    states = a_ref.shape[0]
    first = pl.program_id(1) == 0
    total = prepare(s_ref, w_ref, b_ref, st_ref, u_ref, dk_ref, dv_ref)
    a = a_ref[...]

    @pl.when(first)
    def _():
        out_ref[...] = jnp.zeros_like(out_ref)

    def chunk(c, h):
        t0 = pl.multiple_of(c * TC, TC)
        for i in range(TC):
            f = jnp.exp2(a * dk_ref[pl.ds(t0 + i, 1), :])
            h = f * h + dv_ref[pl.ds(t0 + i, 1), :] * tiled(bb_ref[t0 + i], reps)
        return h

    out_ref[:states, :] = lax.fori_loop(0, s_ref.shape[0] // TC, chunk, out_ref[:states, :])
    out_ref[states : states + 1, :] += total

    @pl.when(pl.program_id(1) == pl.num_programs(1) - 1)
    def _():
        low_ref[:states, :] = out_ref[:states, :].astype(BF16)
        sums = out_ref[states : states + 1, :]
        high = sums.astype(BF16).astype(F32)
        row = lax.broadcasted_iota(jnp.int32, (states, sums.shape[1]), 0)
        both = jnp.where(row == 0, high, jnp.where(row == 1, sums - high, 0.0))
        low_ref[states:, :] = both.astype(BF16)


def forward_kernel(
    s_ref, w_ref, b_ref, st_ref, u_ref, z_ref, a_ref, skip_ref, bb_ref, cm_ref, h0_ref,
    g_ref, y_ref, hs_ref, ck_ref, dk_ref, dv_ref, ys_ref, h_ref,
):
    reps = w_ref.shape[1] // 128
    states = a_ref.shape[0]
    chunks = s_ref.shape[0] // TC
    prepare(s_ref, w_ref, b_ref, st_ref, u_ref, dk_ref, dv_ref)
    a = a_ref[...]

    @pl.when(pl.program_id(1) == 0)
    def _():
        h_ref[...] = h0_ref[...]

    def scan(c, h):
        t0 = pl.multiple_of(c * TC, TC)
        r0 = pl.multiple_of(c * TC * states, TC * states)
        ck_ref[c] = h.astype(BF16)
        for i in range(TC):
            f = jnp.exp2(a * dk_ref[pl.ds(t0 + i, 1), :])
            h = f * h + dv_ref[pl.ds(t0 + i, 1), :] * tiled(bb_ref[t0 + i], reps)
            hs_ref[pl.ds(r0 + i * states, states), :] = h.astype(BF16)
        return h

    def emit(c):
        t0 = pl.multiple_of(c * TC, TC)
        r0 = pl.multiple_of(c * TC * states, TC * states)
        ys_ref[pl.ds(t0, TC), :] = dot(cm_ref[c], hs_ref[pl.ds(r0, TC * states), :])

    def group(j, h):
        for m in range(UNROLL):
            h = scan(UNROLL * j + m, h)
            emit(UNROLL * j + m)
        return h

    h_ref[...] = lax.fori_loop(0, chunks // UNROLL, group, h_ref[...])

    size = min(s_ref.shape[0], ROWS)

    def finish(i, carry):
        r = pl.ds(pl.multiple_of(i * size, size), size)
        y = ys_ref[r, :] + skip_ref[...].astype(F32) * u_ref[r, :].astype(F32)
        z = z_ref[r, :].astype(F32)
        y_ref[r, :] = y.astype(BF16)
        g_ref[r, :] = (y * (z / (1.0 + jnp.exp(-z)))).astype(BF16)
        return carry

    lax.fori_loop(0, s_ref.shape[0] // size, finish, 0)


def start_kernel(s_ref, w_ref, b_ref, st_ref, dy_ref, a_ref, cb_ref, low_ref, dk_ref, out_ref):
    reps = w_ref.shape[1] // 128
    chunks = s_ref.shape[0] // TC
    prepare(s_ref, w_ref, b_ref, st_ref, None, dk_ref, None)
    a = a_ref[...]

    @pl.when(pl.program_id(1) == 0)
    def _():
        out_ref[...] = jnp.zeros_like(out_ref)

    def chunk(j, grad):
        t0 = pl.multiple_of((chunks - 1 - j) * TC, TC)
        for i in range(TC - 1, -1, -1):
            f = jnp.exp2(a * dk_ref[pl.ds(t0 + i, 1), :])
            lam = grad + dy_ref[pl.ds(t0 + i, 1), :] * tiled(cb_ref[t0 + i], reps)
            grad = f * lam
        return grad

    out_ref[...] = lax.fori_loop(0, chunks, chunk, out_ref[...])

    @pl.when(pl.program_id(1) == pl.num_programs(1) - 1)
    def _():
        low_ref[...] = out_ref[...].astype(BF16)


def backward_kernel(
    s_ref, w_ref, b_ref, st_ref, u_ref, dy_ref, a_ref, skip_ref, cb_ref, bm_ref, om_ref, hs_ref, ck_ref, g0_ref,
    ds_ref, du_ref, da_ref, dskip_ref, db_ref, dc_ref,
    pre_ref, dk_ref, dv_ref, q_ref, p_ref, lb0, lb1, wb0, wb1, grad_ref, accb_ref, accc_ref,
):
    step, seg = pl.program_id(0), pl.program_id(1)
    last = pl.num_programs(1) - 1 - seg
    reps = w_ref.shape[1] // 128
    states = a_ref.shape[0]
    rows = s_ref.shape[0]
    chunks = rows // TC
    prepare(s_ref, w_ref, b_ref, st_ref, u_ref, dk_ref, dv_ref, pre_ref)
    token0 = pl.multiple_of(last * rows, rows)

    @pl.when((step == 0) & (seg == 0))
    def _():
        accb_ref[...] = jnp.zeros_like(accb_ref)
        accc_ref[...] = jnp.zeros_like(accc_ref)

    @pl.when(seg == 0)
    def _():
        grad_ref[...] = g0_ref[...]
        da_ref[...] = jnp.zeros_like(da_ref)
        dskip_ref[...] = jnp.zeros_like(dskip_ref)

    a = a_ref[...]
    a_low = a.astype(BF16)

    def scan(c, grad, lb, wb):
        t0 = pl.multiple_of(c * TC, TC)
        r0 = pl.multiple_of(c * TC * states, TC * states)
        da, four = None, None
        for i in range(TC - 1, -1, -1):
            d = dk_ref[pl.ds(t0 + i, 1), :]
            f = jnp.exp2(a * d)
            lam = grad + dy_ref[pl.ds(t0 + i, 1), :] * tiled(cb_ref[t0 + i], reps)
            grad = f * lam
            lb[pl.ds(i * states, states), :] = lam.astype(BF16)
            h = ck_ref[c] if i == 0 else hs_ref[pl.ds(r0 + (i - 1) * states, states), :]
            w = grad.astype(BF16) * h
            wb[pl.ds(i * states, states), :] = w * a_low
            wd = w * jnp.broadcast_to(d, w.shape).astype(BF16)
            four = wd if four is None else four + wd
            if i % 4 == 0:
                da = four.astype(F32) if da is None else da + four.astype(F32)
                four = None
            accb_ref[token0 + t0 + i] += folded(lam * dv_ref[pl.ds(t0 + i, 1), :])
        da_ref[...] += da
        return grad

    def emit(c, lb, wb):
        t0 = pl.multiple_of(c * TC, TC)
        r0 = pl.multiple_of(c * TC * states, TC * states)
        q_ref[pl.ds(t0, TC), :] = dot(bm_ref[c], lb[...])
        p_ref[pl.ds(t0, TC), :] = dot(om_ref[...], wb[...])
        accc_ref[last * chunks + c] += lax.dot_general(
            dy_ref[pl.ds(t0, TC), :].astype(BF16), hs_ref[pl.ds(r0, TC * states), :],
            (((1,), (1,)), ((), ())), preferred_element_type=F32,
        )

    def pair(j, grad):
        c = chunks - 1 - 2 * j
        grad = scan(c, grad, lb0, wb0)
        emit(c, lb0, wb0)
        grad = scan(c - 1, grad, lb1, wb1)
        emit(c - 1, lb1, wb1)
        return grad

    grad_ref[...] = lax.fori_loop(0, chunks // 2, pair, grad_ref[...])

    @pl.when(last == 0)
    def _():
        da_ref[...] = da_ref[...] * a * LN2

    size = min(s_ref.shape[0], ROWS)

    def finish(i, carry):
        r = pl.ds(pl.multiple_of(i * size, size), size)
        u = u_ref[r, :].astype(F32)
        q = q_ref[r, :]
        dy = dy_ref[r, :]
        pre = pre_ref[r, :]
        delta = jnp.maximum(pre, 0.0) + jnp.log1p(jnp.exp(-jnp.abs(pre)))
        dd = p_ref[r, :] * LN2 + u * q
        ds_ref[r, :] = (dd / (1.0 + jnp.exp(-pre))).astype(BF16)
        du_ref[r, :] = delta * q + dy * skip_ref[...].astype(F32)
        return carry + jnp.sum(dy * u, axis=0, keepdims=True)

    dskip_ref[...] += lax.fori_loop(0, rows // size, finish, jnp.zeros(dskip_ref.shape, F32))

    @pl.when((step == pl.num_programs(0) - 1) & (last == 0))
    def _():
        ones = jnp.ones((128, 128), BF16)
        row = lax.broadcasted_iota(jnp.int32, (TC * states, 128), 0) % states
        lane = lax.broadcasted_iota(jnp.int32, (TC * states, 128), 1)

        def gather(c, carry):
            t0 = pl.multiple_of(c * TC, TC)
            b = dot(accb_ref[pl.ds(t0, TC)].reshape(TC * states, 128).astype(BF16), ones)
            db_ref[pl.ds(t0, TC), :] = dot(om_ref[...], jnp.where(lane == row, b, 0.0).astype(BF16)).astype(BF16)
            own = om_ref[...].astype(F32) * accc_ref[c]
            dc_ref[c] = jnp.broadcast_to(jnp.sum(own, axis=0, keepdims=True), dc_ref.shape[1:])
            return carry

        lax.fori_loop(0, accc_ref.shape[0], gather, 0)


def conv_kernel_back(xs_ref, du_ref, slope_ref, dp_ref, sel_ref, k_ref, ok_ref, dxs_ref, dk_ref, db_ref, dc_ref):
    taps = k_ref.shape[0]
    rows = du_ref.shape[0]
    k = k_ref[...].astype(F32)
    dc_ref[:PAD, :] = jnp.zeros((PAD, dc_ref.shape[1]), F32)
    dc_ref[pl.ds(rows + PAD, PAD), :] = jnp.zeros((PAD, dc_ref.shape[1]), F32)

    def first(i, carry):
        t0 = pl.multiple_of(i * CONV_ROWS, CONV_ROWS)
        at = pl.ds(t0, CONV_ROWS)
        du = du_ref[at, :] + dot(dp_ref[at, :], sel_ref[...])
        dc = du * slope_ref[at, :].astype(F32)
        dc_ref[pl.ds(t0 + PAD, CONV_ROWS), :] = dc
        slab = xs_ref[pl.ds(t0, CONV_ROWS + PAD), :].astype(F32)
        sums = [jnp.sum(dc, axis=0, keepdims=True)]
        for lag in range(taps):
            x = slab[PAD - lag : PAD - lag + CONV_ROWS]
            part = dc * x
            if lag:
                part = part * ok_ref[pl.ds(t0 + PAD, CONV_ROWS), lag : lag + 1]
            sums.append(jnp.sum(part, axis=0, keepdims=True))
        return tuple(a + b for a, b in zip(carry, sums))

    size = max(n for n in range(PAD, 129, PAD) if (rows + PAD) % n == 0)
    zero = jnp.zeros((1, k.shape[1]), F32)
    sums = lax.fori_loop(0, rows // CONV_ROWS, first, (zero,) * (taps + 1))
    db_ref[...] = sums[0]
    for lag in range(taps):
        dk_ref[taps - 1 - lag : taps - lag, :] = sums[1 + lag]

    def second(i, carry):
        r0 = pl.multiple_of(i * size, PAD)
        slab = dc_ref[pl.ds(r0, size + PAD), :]
        ok = ok_ref[pl.ds(r0, size + PAD), :]
        out = k[taps - 1 : taps] * slab[:size]
        for lag in range(1, taps):
            part = (ok[:, lag : lag + 1] * slab)[lag : lag + size]
            out = out + k[taps - 1 - lag : taps - lag] * part
        dxs_ref[pl.ds(r0, size), :] = out.astype(BF16)
        return carry

    lax.fori_loop(0, (rows + PAD) // size, second, 0)


def conv_back(xs, du, slope, dp, sel, k, ok):
    rows, width = du.shape
    cb = scan_width(width, 768)
    col = lambda n: pl.BlockSpec((n, cb), lambda i: (0, i))
    whole = lambda x: pl.BlockSpec(x.shape, lambda i: (0, 0))
    taps = k.shape[0]
    return pl.pallas_call(
        conv_kernel_back,
        grid=(width // cb,),
        in_specs=[col(rows + PAD), col(rows), col(rows), whole(dp), col(sel.shape[0]), col(taps), whole(ok)],
        out_specs=[col(rows + PAD), col(taps), col(1)],
        out_shape=[sds((rows + PAD, width), BF16), sds((taps, width), F32), sds((1, width), F32)],
        scratch_shapes=[pltpu.VMEM((rows + 2 * PAD, cb), F32)],
        compiler_params=params(),
        cost_estimate=pl.CostEstimate(flops=rows * width * 300, bytes_accessed=rows * width * 8, transcendentals=0),
        name="conv_back",
    )(xs, du, slope, dp, sel, k, ok)


def scan_width(width, limit):
    n = width // 128
    best = max(d for d in range(1, n + 1) if n % d == 0 and d * 128 <= limit)
    return best * 128


def params():
    return pltpu.CompilerParams(vmem_limit_bytes=60 * 2**20)


def sds(*a):
    return jax.ShapeDtypeStruct(*a)


class Blocks:
    def __init__(self, rows, width, cb, parts, reverse=False, first=0):
        self.first = first
        self.grid = (width // cb, parts)
        self.cb, self.rows, self.seg = cb, rows, rows // parts
        self.at = (lambda s: parts - 1 - s) if reverse else (lambda s: s)

    def token(self, n):
        return pl.BlockSpec((self.seg, n), lambda k, s: (self.at(s), 0))

    def channel(self, n):
        return pl.BlockSpec((n, self.cb), lambda k, s: (0, k + self.first))

    def both(self, times=1, off=0):
        return pl.BlockSpec((self.seg * times, self.cb), lambda k, s: (self.at(s), k + self.first + off))

    def lead(self, n, *rest):
        return pl.BlockSpec((n, *rest), lambda k, s: (self.at(s),) + (0,) * len(rest))

    def marks(self, states):
        return pl.BlockSpec((self.seg // TC, states, self.cb), lambda k, s: (self.at(s), 0, k))

    def whole(self, shape):
        return pl.BlockSpec(shape, lambda k, s: (0,) * len(shape))


def estimate(rows, width, states, ops, size):
    return pl.CostEstimate(
        flops=ops * rows * width * states, bytes_accessed=rows * width * size, transcendentals=rows * width * states
    )


END, FORWARD, START, BACKWARD = (1152, 3), (1152, 6), (1152, 3), (2304, 24)


def end_states(s, w, b, st, u, a, bb, part, of):
    rows, width, states = s.shape[0], w.shape[1] // of, a.shape[0]
    cb = min(END[0], width)
    k = Blocks(rows, width, cb, END[1], first=part * (width // cb))
    return pl.pallas_call(
        end_kernel,
        grid=k.grid,
        in_specs=[k.token(s.shape[1]), k.channel(w.shape[0]), k.channel(1), k.token(1), k.both(), k.channel(states), k.lead(k.seg, states, 128)],
        out_specs=pl.BlockSpec((2 * states, cb), lambda i, j: (0, i)),
        out_shape=sds((2 * states, width), BF16),
        scratch_shapes=[pltpu.VMEM((k.seg, k.cb), F32)] * 2 + [pltpu.VMEM((states + 8, k.cb), F32)],
        compiler_params=params(),
        cost_estimate=estimate(rows, width, states, 6, 8),
        name="end_states",
    )(s, w, b, st, u, a, bb)


def forward_scan(s, w, b, st, u, z, a, skip, bb, cm, h0):
    rows, width, states = s.shape[0], w.shape[1], a.shape[0]
    k = Blocks(rows, width, *FORWARD)
    return pl.pallas_call(
        forward_kernel,
        grid=k.grid,
        in_specs=[k.token(s.shape[1]), k.channel(w.shape[0]), k.channel(1), k.token(1), k.both(), k.both(), k.channel(states), k.channel(1),
                  k.lead(k.seg, states, 128), k.lead(k.seg // TC, *cm.shape[1:]), k.channel(states)],
        out_specs=[k.both(), k.both(), k.both(states), k.marks(states)],
        out_shape=[sds((rows, width), BF16), sds((rows, width), BF16), sds((rows * states, width), BF16), sds((rows // TC, states, width), BF16)],
        scratch_shapes=[pltpu.VMEM((k.seg, k.cb), F32)] * 3 + [pltpu.VMEM((states, k.cb), F32)],
        compiler_params=params(),
        cost_estimate=estimate(rows, width, states, 9, 44),
        name="forward_scan",
    )(s, w, b, st, u, z, a, skip, bb, cm, h0)


def start_grads(s, w, b, st, dy, a, cb_wide, part, of):
    rows, width, states = s.shape[0], w.shape[1] // of, a.shape[0]
    cb = min(START[0], width)
    k = Blocks(rows, width, cb, START[1], reverse=True, first=part * (width // cb))
    return pl.pallas_call(
        start_kernel,
        grid=k.grid,
        in_specs=[k.token(s.shape[1]), k.channel(w.shape[0]), k.channel(1), k.token(1), k.both(), k.channel(states), k.lead(k.seg, states, 128)],
        out_specs=pl.BlockSpec((states, cb), lambda i, j: (0, i)),
        out_shape=sds((states, width), BF16),
        scratch_shapes=[pltpu.VMEM((k.seg, k.cb), F32), pltpu.VMEM((states, k.cb), F32)],
        compiler_params=params(),
        cost_estimate=estimate(rows, width, states, 6, 8),
        name="start_grads",
    )(s, w, b, st, dy, a, cb_wide)


def backward_scan(s, w, b, st, u, dy, a, skip, cb, bm, om, hs, ck, g0):
    rows, width, states = s.shape[0], w.shape[1], a.shape[0]
    k = Blocks(rows, width, *BACKWARD, reverse=True)
    chunks = rows // TC
    return pl.pallas_call(
        backward_kernel,
        grid=k.grid,
        in_specs=[k.token(s.shape[1]), k.channel(w.shape[0]), k.channel(1), k.token(1), k.both(), k.both(), k.channel(states), k.channel(1),
                  k.lead(k.seg, states, 128), k.lead(k.seg // TC, *bm.shape[1:]), k.whole(om.shape), k.both(states), k.marks(states), k.channel(states)],
        out_specs=[k.both(), k.both(), k.channel(states), k.channel(1), k.whole((rows, 128)), k.whole((chunks, 8, TC * states))],
        out_shape=[sds((rows, width), BF16), sds((rows, width), F32), sds((states, width), F32), sds((1, width), F32),
                   sds((rows, 128), BF16), sds((chunks, 8, TC * states), F32)],
        scratch_shapes=[pltpu.VMEM((k.seg, k.cb), F32)] * 5
        + [pltpu.VMEM((TC * states, k.cb), BF16)] * 4
        + [pltpu.VMEM((states, k.cb), F32), pltpu.VMEM((rows, states, 128), F32), pltpu.VMEM((chunks, TC, TC * states), F32)],
        compiler_params=params(),
        cost_estimate=estimate(rows, width, states, 18, 44),
        name="backward_scan",
    )(s, w, b, st, u, dy, a, skip, cb, bm, om, hs, ck, g0)


def spread(coeff):
    return jnp.broadcast_to(coeff[:, :, None], (*coeff.shape, 128))


def block_rows(coeff):
    rows, states = coeff.shape
    mask = jnp.arange(TC * states)[None, None] // states == jnp.arange(TC)[None, :, None]
    return jnp.where(mask, coeff.reshape(rows // TC, 1, TC * states), 0.0).astype(BF16)


epsilon = 1e-05
HALVES = 2


def shifted(array, axis, by):
    length = lax.axis_size(axis)
    pairs = [(i, i + by) for i in range(length) if 0 <= i + by < length]
    return lax.ppermute(array, axis, pairs)


def entering(came, sums, rate2):
    state, decay = jnp.zeros_like(rate2), jnp.zeros((1, rate2.shape[1]), F32)
    for end, total in zip(came, sums):
        state = state + jnp.exp2(rate2 * decay) * end.astype(F32)
        decay = decay + total
    return state


def product_back(left, right):
    return lax.dot_general(left, right, (((1,), (1,)), ((), ())), preferred_element_type=F32)


def contract(left, right):
    return lax.dot_general(left, right, (((0,), (0,)), ((), ())), preferred_element_type=F32)


def silu_slope(values):
    sigma = jax.nn.sigmoid(values)
    return sigma * (1.0 + values * (1.0 - sigma))


def inverse_rms(values):
    return lax.rsqrt(jnp.mean(values * values, axis=-1, keepdims=True) + epsilon)


def paired_rows(rows, devices):
    r, d = rows.shape
    split = rows.reshape(r // 2, 2, devices, d // devices)
    return split.transpose(0, 2, 1, 3).reshape(r // 2, 2 * d)


def single_rows(rows, devices):
    r, d = rows.shape
    split = rows.reshape(r, devices, 2, d // (2 * devices))
    return split.transpose(0, 2, 1, 3).reshape(2 * r, d // 2)


def stacked(parts):
    whole = jnp.concatenate([p.astype(BF16) for p in parts], axis=0)
    return jnp.pad(whole, ((0, -whole.shape[0] % 16), (0, 0)))


def expert_part(parts):
    n, here = lax.axis_size("expert"), lax.axis_index("expert")
    part = lambda k: lax.dynamic_index_in_dim(parts, jnp.mod(here + k, n), 0, keepdims=False)
    total = part(0).astype(F32)
    for k in range(1, n):
        total = total + turned(part(k), k).astype(F32)
    return total.astype(BF16)


def turned(x, k):
    n = lax.axis_size("expert")
    return lax.ppermute(x, "expert", [(i, (i + k) % n) for i in range(n)]) if k else x


def in_order(came):
    n, here = lax.axis_size("expert"), lax.axis_index("expert")
    return lax.dynamic_slice_in_dim(jnp.stack(came[::-1] * 2), n - 1 - here, n, 0)


def expert_sum(*arrays):
    n = lax.axis_size("expert")
    split = [x.reshape(n, x.shape[0] // n, x.shape[1]) for x in arrays]
    padded = [jnp.pad(x, ((0, 0), (0, -x.shape[1] % 8), (0, 0))) for x in split]
    total = expert_part(jnp.concatenate(padded, axis=1))
    every = in_order([turned(total, k) for k in range(n)])
    out, at = [], 0
    for x, p in zip(split, padded):
        out.append(every[:, at : at + x.shape[1]].reshape(n * x.shape[1], x.shape[2]))
        at += p.shape[1]
    return out


def shares(rows, devices):
    r, columns = rows.shape
    return rows.reshape(r, devices, columns // devices).transpose(1, 0, 2).reshape(devices, -1)


def halved(grads, devices):
    rows, columns = grads.shape
    split = grads.reshape(devices // 2, 2, rows // devices, columns)
    return split.transpose(1, 0, 2, 3).reshape(devices, rows // devices, columns)


def cut(whole, counts):
    out, at = [], 0
    for n in counts:
        out.append(whole[at : at + n])
        at += n
    return out


def body(
    tokens, cotangent, routes, starts, input_proj, conv_kernel, conv_bias, select_proj, step_proj,
    step_bias, decay_log, skip_gain, output_proj, norm_gain, ffn_gain, router, expert_up, expert_down,
):
    devices = lax.axis_size("dp")
    groups = lax.axis_size("expert")
    rows, model = tokens.shape
    taps, rank, states = conv_kernel.shape[0], step_proj.shape[0], decay_log.shape[1]
    capacity = 2 * rows // groups
    w_input = lax.all_gather(input_proj, "dp", axis=1, tiled=True)
    small = stacked(
        [
            select_proj.T, step_proj, decay_log.T, conv_kernel, conv_bias[None], step_bias[None], skip_gain[None],
            paired_rows(jnp.concatenate([norm_gain[None], ffn_gain[None], router.T], 0), 1),
        ]
    )
    counts = (select_proj.shape[1], rank, states, taps, 1, 1, 1, (groups + 2) // 2)
    w_select, w_step, w_decay, w_conv, b_conv, bias2, skip2, singles = cut(
        lax.all_gather(small, "dp", axis=1, tiled=True), counts
    )
    singles = single_rows(singles, devices).astype(F32)
    norm_f, ffn_f, router_f = singles[0], singles[1], singles[2:]
    w_output = lax.all_gather(output_proj, "dp", axis=0, tiled=True)
    w_up = lax.all_gather(expert_up[0], "dp", axis=1, tiled=True)
    w_down = lax.all_gather(expert_down[0], "dp", axis=0, tiled=True)
    width = w_select.shape[1]
    conv_f = w_conv.astype(F32)

    route = routes[:, 0]
    chosen = (route[:, None] == jnp.arange(groups, dtype=jnp.int32)[None, :]).astype(F32)
    before = (jnp.arange(rows)[:, None] > jnp.arange(rows)[None, :]).astype(BF16)
    ranks = dot(before, chosen.astype(BF16))
    slot = jnp.sum(ranks * chosen, axis=1).astype(jnp.int32)
    assert groups & (groups - 1) == 0
    distance = jnp.bitwise_xor(route, lax.axis_index("expert"))
    target = jnp.where(slot < capacity, distance * capacity + slot, groups * capacity)
    place = (jnp.arange(groups * capacity)[:, None] == target[None, :]).astype(BF16)

    hidden_in = tokens.astype(F32)
    norm_r = inverse_rms(hidden_in)
    norm_own = (hidden_in * norm_r * norm_f).astype(BF16)
    flag = starts.astype(F32)
    same = 1.0 - flag
    valid = [jnp.ones((rows,), F32)]
    for lag in range(1, taps):
        moved = jnp.concatenate([jnp.ones((lag - 1,), F32), same[: rows - lag + 1]])
        valid.append(valid[-1] * moved)
    edge = [jnp.ones((), F32)]
    for lag in range(1, taps - 1):
        edge.append(edge[-1] * same[rows - lag])
    edge_keep = jnp.stack(edge[::-1])[:, None]
    tail = (norm_own[rows - taps + 1 :].astype(F32) * edge_keep).astype(BF16)
    borrowed = shifted(tail, "expert", 1)
    norm_low = jnp.concatenate([jnp.zeros((PAD - taps + 1, model), BF16), borrowed, norm_own], 0)
    ok = jnp.pad(jnp.stack(valid, 1), ((PAD, PAD), (0, 0)))
    norm_low, ok = lax.optimization_barrier((norm_low, ok))
    conv_in = dot(norm_low, w_input[:, :width]).astype(BF16)
    conv_sum = jnp.broadcast_to(b_conv.astype(F32), (rows, width))
    for lag in range(taps):
        conv_sum = conv_sum + valid[lag][:, None] * conv_f[taps - 1 - lag] * conv_in[PAD - lag : PAD - lag + rows].astype(F32)
    inner_low = jax.nn.silu(conv_sum).astype(BF16)
    slope_low = silu_slope(conv_sum).astype(BF16)
    selected = product_back(inner_low, w_select)
    step_low = selected[:, :rank].astype(BF16)
    b_coeff = selected[:, rank : rank + states]
    c_coeff = selected[:, rank + states :]
    rate2 = -jnp.exp(w_decay.astype(F32)) * LOG2E
    st = flag[:, None]
    b_wide, c_wide = spread(b_coeff), spread(c_coeff)
    b_block, c_block = block_rows(b_coeff), block_rows(c_coeff)
    one_block = (jnp.arange(TC * states)[None] // states == jnp.arange(TC)[:, None]).astype(BF16)
    hops = range(1, groups)
    own_sums, start_state = [], []
    for part in range(HALVES):
        rate_part = rate2[:, part * width // HALVES : (part + 1) * width // HALVES]
        end = end_states(step_low, w_step, bias2, st, inner_low, rate2, b_wide, part, HALVES)
        came = [shifted(end, "expert", hop) for hop in hops]
        total = lambda x: x[:1].astype(F32) + x[1:2].astype(F32)
        own_sums.append(end[states : states + 8])
        start_state.append(entering([c[:states] for c in came], [total(c[states:]) for c in came], rate_part))
    start_state = jnp.concatenate(start_state, 1)
    norm_late, _ = lax.optimization_barrier((norm_own, end))
    gate_in = dot(norm_late, w_input[:, width:]).astype(BF16)
    gated_low, scanned, history, marks = forward_scan(
        step_low, w_step, bias2, st, inner_low, gate_in, rate2, skip2, b_wide, c_block, start_state
    )
    hidden_one = hidden_in + dot(gated_low, w_output)

    r2 = inverse_rms(hidden_one)
    norm_two = hidden_one * r2 * ffn_f
    logits = lax.dot_general(
        norm_two, router_f, (((1,), (1,)), ((), ())),
        precision=lax.Precision.HIGHEST, preferred_element_type=F32,
    )
    probs = jax.nn.softmax(logits, axis=-1)
    gate_value = jnp.sum(probs * chosen, axis=-1)
    grad_out = cotangent.astype(F32)
    grad_picked = (gate_value[:, None] * grad_out).astype(BF16)

    def swapped(x, k):
        return lax.ppermute(x, "expert", [(i, i ^ k) for i in range(groups)]) if k else x

    places = [place[k * capacity : (k + 1) * capacity] for k in range(groups)]
    norm_two_low = norm_two.astype(BF16)
    arrived, grad_arrived = [None] * groups, [None] * groups
    far_first = list(range(groups - 1, 0, -1))
    for k in far_first + [0]:
        arrived[k] = swapped(dot(places[k], norm_two_low).astype(BF16), k)
    for k in far_first + [0]:
        sent = dot(places[k], grad_picked).astype(BF16)
        if k:
            sent, arrived[k] = lax.optimization_barrier((sent, arrived[k]))
        grad_arrived[k] = swapped(sent, k)
    up_low, grad_pre, outs, ins = ([None] * groups for _ in range(4))
    for k in [0] + far_first:
        up_pre = dot(arrived[k], w_up)
        act, gelu_back = jax.vjp(jax.nn.gelu, up_pre)
        up_low[k] = act.astype(BF16)
        outs[k] = dot(up_low[k], w_down).astype(BF16)
        grad_pre[k] = gelu_back(product_back(grad_arrived[k], w_down))[0].astype(BF16)
        ins[k] = product_back(grad_pre[k], w_up).astype(BF16)
    returned = [None] * groups
    grad_sent = [None] * groups
    for k in far_first + [0]:
        returned[k] = swapped(outs[k], k)
    for k in far_first + [0]:
        grad_sent[k] = swapped(ins[k], k)
    returned, grad_sent = jnp.concatenate(returned), jnp.concatenate(grad_sent)
    up_low, grad_pre, arrived, grad_arrived, _, _ = lax.optimization_barrier(
        (up_low, grad_pre, arrived, grad_arrived, outs, ins)
    )
    grad_up = contract(jnp.concatenate(grad_pre), jnp.concatenate(arrived)).astype(BF16)
    grad_down = contract(jnp.concatenate(up_low), jnp.concatenate(grad_arrived)).astype(BF16)
    grad_sent, grad_up, grad_down, c_wide, b_block = lax.optimization_barrier(
        (grad_sent, grad_up, grad_down, c_wide, b_block)
    )
    sum_up = lax.psum_scatter(grad_up, "dp", scatter_dimension=0, tiled=True)
    sum_down = lax.psum_scatter(grad_down, "dp", scatter_dimension=0, tiled=True)

    picked = contract(place, returned)
    output = (hidden_one + gate_value[:, None] * picked).astype(BF16)
    grad_gate = jnp.sum(grad_out * picked, axis=1)
    grad_logits = probs * (grad_gate[:, None] * chosen - (grad_gate * gate_value)[:, None])
    grad_router = lax.dot_general(
        grad_logits, norm_two, (((0,), (0,)), ((), ())),
        precision=lax.Precision.HIGHEST, preferred_element_type=F32,
    )
    grad_norm_two = contract(place, grad_sent) + lax.dot_general(
        grad_logits, router_f, (((1,), (0,)), ((), ())),
        precision=lax.Precision.HIGHEST, preferred_element_type=F32,
    )
    grad_ffn_gain = jnp.sum(grad_norm_two * hidden_one * r2, axis=0)
    scaled = ffn_f * grad_norm_two
    grad_hidden = (
        grad_out
        + r2 * scaled
        - hidden_one * (r2 * r2 * r2) * jnp.mean(hidden_one * scaled, axis=-1, keepdims=True)
    )

    grad_mixer = grad_hidden.astype(BF16)
    grad_output_w = contract(gated_low, grad_mixer)
    grad_gated = product_back(grad_mixer, w_output)
    gate_f = gate_in.astype(F32)
    sigma = jax.nn.sigmoid(gate_f)
    grad_scanned = grad_gated * (gate_f * sigma)
    grad_gate_in = (grad_gated * scanned.astype(F32) * (sigma * (1.0 + gate_f * (1.0 - sigma)))).astype(BF16)
    grad_scanned, sum_up = lax.optimization_barrier((grad_scanned, sum_up))
    later_grad = []
    for part in range(HALVES):
        rate_part = rate2[:, part * width // HALVES : (part + 1) * width // HALVES]
        start = start_grads(step_low, w_step, bias2, st, grad_scanned, rate2, c_wide, part, HALVES)
        start = jnp.concatenate([start, own_sums[part]])
        came = [shifted(start, "expert", -hop) for hop in hops]
        later_grad.append(entering([c[:states] for c in came], [total(c[states:]) for c in came], rate_part))
    grad_input_z = halved(contract(grad_gate_in, norm_own).astype(BF16), devices).reshape(width, model)
    grad_norm_z = product_back(grad_gate_in, w_input[:, width:])
    later_grad, sum_down, grad_output_w, grad_input_z, grad_norm_z = lax.optimization_barrier(
        (jnp.concatenate(later_grad, 1), sum_down, grad_output_w.astype(BF16), grad_input_z, grad_norm_z)
    )
    sum_output = lax.psum_scatter(grad_output_w, "dp", scatter_dimension=0, tiled=True)
    sum_input_z = lax.psum_scatter(grad_input_z, "dp", scatter_dimension=0, tiled=True)
    grad_pre_step, grad_inner, grad_decay_t, grad_skip, grad_b, grad_c = backward_scan(
        step_low, w_step, bias2, st, inner_low, grad_scanned, rate2, skip2,
        c_wide, b_block, one_block, history, marks, later_grad,
    )
    grad_pre_step, sum_output, sum_input_z = lax.optimization_barrier((grad_pre_step, sum_output, sum_input_z))
    grad_step_bias = jnp.sum(grad_pre_step.astype(F32), axis=0, keepdims=True)
    grad_step_w = contract(step_low, grad_pre_step)
    grad_step_low = product_back(grad_pre_step, w_step).astype(BF16)
    grad_selected = jnp.concatenate(
        [grad_step_low, grad_b[:, :states], grad_c[:, 0].reshape(rows, states).astype(BF16)], 1
    )
    grad_select_w = contract(grad_selected, inner_low)
    summed = stacked(
        [
            grad_select_w, grad_step_w, grad_decay_t, grad_step_bias, grad_skip,
            paired_rows(jnp.concatenate([grad_ffn_gain[None], grad_ffn_gain[None], grad_router], 0), devices),
        ]
    )
    share, norm_share = width // devices, model // devices
    summed_shape = (summed.shape[0], share)
    summed = shares(summed, devices)
    grad_inner, summed = lax.optimization_barrier((grad_inner, summed))
    grad_conv_in, grad_kernel, grad_conv_b = conv_back(
        conv_in, grad_inner, slope_low, grad_selected, w_select, w_conv, ok
    )
    grad_norm_x = product_back(grad_conv_in, w_input[:, :width])
    returned_edge = shifted(grad_norm_x[PAD - taps + 1 : PAD], "expert", -1) * edge_keep
    grad_norm_one = grad_norm_x[PAD:] + grad_norm_z + jnp.pad(returned_edge, ((rows - taps + 1, 0), (0, 0)))
    grad_norm_gain = jnp.sum(grad_norm_one * hidden_in * norm_r, axis=0, keepdims=True)
    grad_input_x = halved(contract(grad_conv_in, norm_low).astype(BF16), devices)
    tiny = jnp.concatenate([shares(jnp.concatenate([grad_kernel, grad_conv_b]), devices), shares(grad_norm_gain, devices)], 1)
    rest = jnp.concatenate([summed, tiny.astype(BF16)], 1)
    more = -(-rest.shape[1] // model)
    more += -(more + share) % (8 * groups)
    rest = jnp.pad(rest, ((0, 0), (0, more * model - rest.shape[1]))).reshape(devices, more, model)
    packed = jnp.concatenate([grad_input_x, rest], axis=1).reshape(devices * (share + more), model)
    packed, sum_output, sum_input_z = lax.optimization_barrier((packed, sum_output, sum_input_z))
    packed = lax.psum_scatter(packed, "dp", scatter_dimension=0, tiled=True)
    sum_output, sum_input_z = expert_sum(sum_output, sum_input_z)
    scaled_one = norm_f * grad_norm_one
    grad_tokens = (
        grad_hidden
        + norm_r * scaled_one
        - hidden_in * (norm_r * norm_r * norm_r) * jnp.mean(hidden_in * scaled_one, axis=-1, keepdims=True)
    ).astype(BF16)
    packed, sum_output, sum_input_z, grad_tokens = lax.optimization_barrier((packed, sum_output, sum_input_z, grad_tokens))
    (packed,) = expert_sum(packed)
    sum_input_x, tiny = packed[:share], packed[share:].astype(F32).reshape(-1)
    summed = tiny[: summed_shape[0] * share].reshape(summed_shape)
    tiny = tiny[summed_shape[0] * share :]
    half = devices // 2
    low = lax.axis_index("dp") < half
    other = lax.ppermute(
        jnp.where(low, sum_input_z, sum_input_x), "dp", [(i, (i + half) % devices) for i in range(devices)]
    )
    own_half = jnp.where(low, sum_input_x, sum_input_z)
    sum_input = jnp.concatenate([jnp.where(low, own_half, other), jnp.where(low, other, own_half)])
    sum_kernel = tiny[: taps * share].reshape(taps, share)
    sum_conv_b = tiny[taps * share : (taps + 1) * share]
    sum_norm = tiny[(taps + 1) * share : (taps + 1) * share + norm_share]
    sum_select, sum_step, sum_decay, sum_step_b, sum_skip, singles = cut(
        summed, (w_select.shape[0], rank, states, 1, 1, (groups + 2) // 2)
    )
    singles = single_rows(singles, 1)
    sum_input, sum_output = sum_input.astype(F32).T, sum_output.astype(F32)
    return (
        output, grad_tokens, sum_input, sum_kernel, sum_conv_b, sum_select.T, sum_step, sum_step_b[0],
        sum_decay.T, sum_skip[0], sum_output, sum_norm, singles[1], singles[2:].T,
        sum_up.astype(F32).T[None], sum_down.astype(F32)[None],
    )


def solution(mesh):
    placed = (
        P(("dp", "expert"), None),
        P(("dp", "expert"), None),
        P(("dp", "expert"), None),
        P(("dp", "expert")),
        P(None, "dp"),
        P(None, "dp"),
        P("dp"),
        P("dp", None),
        P(None, "dp"),
        P("dp"),
        P("dp", None),
        P("dp"),
        P("dp", None),
        P("dp"),
        P("dp"),
        P("dp", None),
        P("expert", None, "dp"),
        P("expert", "dp", None),
    )
    return jax.shard_map(
        body,
        mesh=mesh,
        in_specs=placed,
        out_specs=(
            P(("dp", "expert"), None),
            P(("dp", "expert"), None),
            P(None, "dp"),
            P(None, "dp"),
            P("dp"),
            P("dp", None),
            P(None, "dp"),
            P("dp"),
            P("dp", None),
            P("dp"),
            P("dp", None),
            P("dp"),
            P("dp"),
            P("dp", None),
            P("expert", None, "dp"),
            P("expert", "dp", None),
        ),
        check_vma=False,
    )
```

```python
from functools import partial

import jax
import jax.numpy as jnp
from jax import lax
from jax.experimental import pallas as pl
from jax.experimental.pallas import tpu as pltpu
from jax.sharding import PartitionSpec as P

TC = 16
ROWS = 256
CONV_ROWS = 256
PAD = 16
UNROLL = 8
FAR = 1e4
LOG2E = 1.4426950408889634
LN2 = 0.6931471805599453
F32 = jnp.float32
BF16 = jnp.bfloat16


def tiled(x, n):
    return jnp.concatenate([x] * n, axis=1) if n > 1 else x


def folded(x):
    n = x.shape[1] // 128
    out = x[:, :128]
    for i in range(1, n):
        out = out + x[:, i * 128 : (i + 1) * 128]
    return out


def dot(a, b):
    return jnp.dot(a, b, preferred_element_type=F32)


def prepare(s_ref, w_ref, b_ref, st_ref, u_ref, dk_ref, dv_ref, pre_ref=None):
    size = min(s_ref.shape[0], ROWS)

    def block(i, carry):
        r = pl.ds(pl.multiple_of(i * size, size), size)
        pre = dot(s_ref[r, :], w_ref[...]) + b_ref[...].astype(F32)
        delta = jnp.maximum(pre, 0.0) + jnp.log1p(jnp.exp(-jnp.abs(pre)))
        dk = jnp.where(st_ref[r, :] > 0.0, FAR, delta)
        dk_ref[r, :] = dk
        if u_ref is not None:
            dv_ref[r, :] = delta * u_ref[r, :].astype(F32)
        if pre_ref is not None:
            pre_ref[r, :] = pre
        return carry + jnp.sum(dk, axis=0, keepdims=True)

    return lax.fori_loop(
        0, s_ref.shape[0] // size, block, jnp.zeros((1, w_ref.shape[1]), F32)
    )


def end_kernel(s_ref, w_ref, b_ref, st_ref, u_ref, a_ref, bb_ref, low_ref, dk_ref, dv_ref, out_ref):
    reps = w_ref.shape[1] // 128
    states = a_ref.shape[0]
    first = pl.program_id(1) == 0
    total = prepare(s_ref, w_ref, b_ref, st_ref, u_ref, dk_ref, dv_ref)
    a = a_ref[...]

    @pl.when(first)
    def _():
        out_ref[...] = jnp.zeros_like(out_ref)

    def chunk(c, h):
        t0 = pl.multiple_of(c * TC, TC)
        for i in range(TC):
            f = jnp.exp2(a * dk_ref[pl.ds(t0 + i, 1), :])
            h = f * h + dv_ref[pl.ds(t0 + i, 1), :] * tiled(bb_ref[t0 + i], reps)
        return h

    out_ref[:states, :] = lax.fori_loop(0, s_ref.shape[0] // TC, chunk, out_ref[:states, :])
    out_ref[states : states + 1, :] += total

    @pl.when(pl.program_id(1) == pl.num_programs(1) - 1)
    def _():
        low_ref[:states, :] = out_ref[:states, :].astype(BF16)
        sums = out_ref[states : states + 1, :]
        high = sums.astype(BF16).astype(F32)
        row = lax.broadcasted_iota(jnp.int32, (states, sums.shape[1]), 0)
        both = jnp.where(row == 0, high, jnp.where(row == 1, sums - high, 0.0))
        low_ref[states:, :] = both.astype(BF16)


def forward_kernel(
    s_ref, w_ref, b_ref, st_ref, u_ref, z_ref, a_ref, skip_ref, bb_ref, cm_ref, h0_ref,
    g_ref, y_ref, hs_ref, ck_ref, dk_ref, dv_ref, ys_ref, h_ref,
):
    reps = w_ref.shape[1] // 128
    states = a_ref.shape[0]
    chunks = s_ref.shape[0] // TC
    prepare(s_ref, w_ref, b_ref, st_ref, u_ref, dk_ref, dv_ref)
    a = a_ref[...]

    @pl.when(pl.program_id(1) == 0)
    def _():
        h_ref[...] = h0_ref[...]

    def scan(c, h):
        t0 = pl.multiple_of(c * TC, TC)
        r0 = pl.multiple_of(c * TC * states, TC * states)
        ck_ref[c] = h.astype(BF16)
        for i in range(TC):
            f = jnp.exp2(a * dk_ref[pl.ds(t0 + i, 1), :])
            h = f * h + dv_ref[pl.ds(t0 + i, 1), :] * tiled(bb_ref[t0 + i], reps)
            hs_ref[pl.ds(r0 + i * states, states), :] = h.astype(BF16)
        return h

    def emit(c):
        t0 = pl.multiple_of(c * TC, TC)
        r0 = pl.multiple_of(c * TC * states, TC * states)
        ys_ref[pl.ds(t0, TC), :] = dot(cm_ref[c], hs_ref[pl.ds(r0, TC * states), :])

    def group(j, h):
        for m in range(UNROLL):
            h = scan(UNROLL * j + m, h)
            emit(UNROLL * j + m)
        return h

    h_ref[...] = lax.fori_loop(0, chunks // UNROLL, group, h_ref[...])

    size = min(s_ref.shape[0], ROWS)

    def finish(i, carry):
        r = pl.ds(pl.multiple_of(i * size, size), size)
        y = ys_ref[r, :] + skip_ref[...].astype(F32) * u_ref[r, :].astype(F32)
        z = z_ref[r, :].astype(F32)
        y_ref[r, :] = y.astype(BF16)
        g_ref[r, :] = (y * (z / (1.0 + jnp.exp(-z)))).astype(BF16)
        return carry

    lax.fori_loop(0, s_ref.shape[0] // size, finish, 0)


def start_kernel(s_ref, w_ref, b_ref, st_ref, dy_ref, a_ref, cb_ref, low_ref, dk_ref, out_ref):
    reps = w_ref.shape[1] // 128
    chunks = s_ref.shape[0] // TC
    prepare(s_ref, w_ref, b_ref, st_ref, None, dk_ref, None)
    a = a_ref[...]

    @pl.when(pl.program_id(1) == 0)
    def _():
        out_ref[...] = jnp.zeros_like(out_ref)

    def chunk(j, grad):
        t0 = pl.multiple_of((chunks - 1 - j) * TC, TC)
        for i in range(TC - 1, -1, -1):
            f = jnp.exp2(a * dk_ref[pl.ds(t0 + i, 1), :])
            lam = grad + dy_ref[pl.ds(t0 + i, 1), :] * tiled(cb_ref[t0 + i], reps)
            grad = f * lam
        return grad

    out_ref[...] = lax.fori_loop(0, chunks, chunk, out_ref[...])

    @pl.when(pl.program_id(1) == pl.num_programs(1) - 1)
    def _():
        low_ref[...] = out_ref[...].astype(BF16)


def backward_kernel(
    s_ref, w_ref, b_ref, st_ref, u_ref, dy_ref, a_ref, skip_ref, cb_ref, bm_ref, om_ref, hs_ref, ck_ref, g0_ref,
    ds_ref, du_ref, da_ref, dskip_ref, dbias_ref, db_ref, dc_ref,
    pre_ref, dk_ref, dv_ref, q_ref, p_ref, lb0, lb1, wb0, wb1, grad_ref, accb_ref, accc_ref,
):
    step, seg = pl.program_id(0), pl.program_id(1)
    last = pl.num_programs(1) - 1 - seg
    reps = w_ref.shape[1] // 128
    states = a_ref.shape[0]
    rows = s_ref.shape[0]
    chunks = rows // TC
    prepare(s_ref, w_ref, b_ref, st_ref, u_ref, dk_ref, dv_ref, pre_ref)
    token0 = pl.multiple_of(last * rows, rows)

    @pl.when((step == 0) & (seg == 0))
    def _():
        accb_ref[...] = jnp.zeros_like(accb_ref)
        accc_ref[...] = jnp.zeros_like(accc_ref)

    @pl.when(seg == 0)
    def _():
        grad_ref[...] = g0_ref[...]
        da_ref[...] = jnp.zeros_like(da_ref)
        dskip_ref[...] = jnp.zeros_like(dskip_ref)
        dbias_ref[...] = jnp.zeros_like(dbias_ref)

    a = a_ref[...]
    a_low = a.astype(BF16)

    def scan(c, grad, lb, wb):
        t0 = pl.multiple_of(c * TC, TC)
        r0 = pl.multiple_of(c * TC * states, TC * states)
        da, four = None, None
        for i in range(TC - 1, -1, -1):
            d = dk_ref[pl.ds(t0 + i, 1), :]
            f = jnp.exp2(a * d)
            lam = grad + dy_ref[pl.ds(t0 + i, 1), :] * tiled(cb_ref[t0 + i], reps)
            grad = f * lam
            lb[pl.ds(i * states, states), :] = lam.astype(BF16)
            h = ck_ref[c] if i == 0 else hs_ref[pl.ds(r0 + (i - 1) * states, states), :]
            w = grad.astype(BF16) * h
            wb[pl.ds(i * states, states), :] = w * a_low
            wd = w * jnp.broadcast_to(d, w.shape).astype(BF16)
            four = wd if four is None else four + wd
            if i % 4 == 0:
                da = four.astype(F32) if da is None else da + four.astype(F32)
                four = None
            accb_ref[token0 + t0 + i] += folded(lam * dv_ref[pl.ds(t0 + i, 1), :])
        da_ref[...] += da
        return grad

    def emit(c, lb, wb):
        t0 = pl.multiple_of(c * TC, TC)
        r0 = pl.multiple_of(c * TC * states, TC * states)
        q_ref[pl.ds(t0, TC), :] = dot(bm_ref[c], lb[...])
        p_ref[pl.ds(t0, TC), :] = dot(om_ref[...], wb[...])
        accc_ref[last * chunks + c] += lax.dot_general(
            dy_ref[pl.ds(t0, TC), :].astype(BF16), hs_ref[pl.ds(r0, TC * states), :],
            (((1,), (1,)), ((), ())), preferred_element_type=F32,
        )

    def pair(j, grad):
        c = chunks - 1 - 2 * j
        grad = scan(c, grad, lb0, wb0)
        emit(c, lb0, wb0)
        grad = scan(c - 1, grad, lb1, wb1)
        emit(c - 1, lb1, wb1)
        return grad

    grad_ref[...] = lax.fori_loop(0, chunks // 2, pair, grad_ref[...])

    @pl.when(last == 0)
    def _():
        da_ref[...] = da_ref[...] * a * LN2

    size = min(s_ref.shape[0], ROWS)

    def finish(i, carry):
        r = pl.ds(pl.multiple_of(i * size, size), size)
        u = u_ref[r, :].astype(F32)
        q = q_ref[r, :]
        dy = dy_ref[r, :]
        pre = pre_ref[r, :]
        delta = jnp.maximum(pre, 0.0) + jnp.log1p(jnp.exp(-jnp.abs(pre)))
        dd = p_ref[r, :] * LN2 + u * q
        ds = (dd / (1.0 + jnp.exp(-pre))).astype(BF16)
        ds_ref[r, :] = ds
        du_ref[r, :] = delta * q + dy * skip_ref[...].astype(F32)
        skip, bias = carry
        return (
            skip + jnp.sum(dy * u, axis=0, keepdims=True),
            bias + jnp.sum(ds.astype(F32), axis=0, keepdims=True),
        )

    zero = jnp.zeros(dskip_ref.shape, F32)
    skip, bias = lax.fori_loop(0, rows // size, finish, (zero, zero))
    dskip_ref[...] += skip
    dbias_ref[...] += bias

    @pl.when((step == pl.num_programs(0) - 1) & (last == 0))
    def _():
        ones = jnp.ones((128, 128), BF16)
        row = lax.broadcasted_iota(jnp.int32, (TC * states, 128), 0) % states
        lane = lax.broadcasted_iota(jnp.int32, (TC * states, 128), 1)

        def gather(c, carry):
            t0 = pl.multiple_of(c * TC, TC)
            b = dot(accb_ref[pl.ds(t0, TC)].reshape(TC * states, 128).astype(BF16), ones)
            db_ref[pl.ds(t0, TC), :] = dot(om_ref[...], jnp.where(lane == row, b, 0.0).astype(BF16)).astype(BF16)
            own = om_ref[...].astype(F32) * accc_ref[c]
            dc_ref[c] = jnp.broadcast_to(jnp.sum(own, axis=0, keepdims=True), dc_ref.shape[1:])
            return carry

        lax.fori_loop(0, accc_ref.shape[0], gather, 0)


def conv_kernel_back(xs_ref, du_ref, slope_ref, dp_ref, sel_ref, k_ref, ok_ref, dxs_ref, dk_ref, db_ref, dc_ref):
    taps = k_ref.shape[0]
    rows = du_ref.shape[0]
    k = k_ref[...].astype(F32)
    dc_ref[:PAD, :] = jnp.zeros((PAD, dc_ref.shape[1]), F32)
    dc_ref[pl.ds(rows + PAD, PAD), :] = jnp.zeros((PAD, dc_ref.shape[1]), F32)

    def first(i, carry):
        t0 = pl.multiple_of(i * CONV_ROWS, CONV_ROWS)
        at = pl.ds(t0, CONV_ROWS)
        du = du_ref[at, :] + dot(dp_ref[at, :], sel_ref[...])
        dc = du * slope_ref[at, :].astype(F32)
        dc_ref[pl.ds(t0 + PAD, CONV_ROWS), :] = dc
        slab = xs_ref[pl.ds(t0, CONV_ROWS + PAD), :].astype(F32)
        sums = [jnp.sum(dc, axis=0, keepdims=True)]
        for lag in range(taps):
            x = slab[PAD - lag : PAD - lag + CONV_ROWS]
            part = dc * x
            if lag:
                part = part * ok_ref[pl.ds(t0 + PAD, CONV_ROWS), lag : lag + 1]
            sums.append(jnp.sum(part, axis=0, keepdims=True))
        return tuple(a + b for a, b in zip(carry, sums))

    size = max(n for n in range(PAD, 129, PAD) if (rows + PAD) % n == 0)
    zero = jnp.zeros((1, k.shape[1]), F32)
    sums = lax.fori_loop(0, rows // CONV_ROWS, first, (zero,) * (taps + 1))
    db_ref[...] = sums[0]
    for lag in range(taps):
        dk_ref[taps - 1 - lag : taps - lag, :] = sums[1 + lag]

    def second(i, carry):
        r0 = pl.multiple_of(i * size, PAD)
        slab = dc_ref[pl.ds(r0, size + PAD), :]
        ok = ok_ref[pl.ds(r0, size + PAD), :]
        out = k[taps - 1 : taps] * slab[:size]
        for lag in range(1, taps):
            part = (ok[:, lag : lag + 1] * slab)[lag : lag + size]
            out = out + k[taps - 1 - lag : taps - lag] * part
        dxs_ref[pl.ds(r0, size), :] = out.astype(BF16)
        return carry

    lax.fori_loop(0, (rows + PAD) // size, second, 0)


def conv_back(xs, du, slope, dp, sel, k, ok):
    rows, width = du.shape
    cb = scan_width(width, 768)
    col = lambda n: pl.BlockSpec((n, cb), lambda i: (0, i))
    whole = lambda x: pl.BlockSpec(x.shape, lambda i: (0, 0))
    taps = k.shape[0]
    return pl.pallas_call(
        conv_kernel_back,
        grid=(width // cb,),
        in_specs=[col(rows + PAD), col(rows), col(rows), whole(dp), col(sel.shape[0]), col(taps), whole(ok)],
        out_specs=[col(rows + PAD), col(taps), col(1)],
        out_shape=[sds((rows + PAD, width), BF16), sds((taps, width), F32), sds((1, width), F32)],
        scratch_shapes=[pltpu.VMEM((rows + 2 * PAD, cb), F32)],
        compiler_params=params(),
        cost_estimate=pl.CostEstimate(flops=rows * width * 300, bytes_accessed=rows * width * 8, transcendentals=0),
        name="conv_back",
    )(xs, du, slope, dp, sel, k, ok)


def scan_width(width, limit):
    n = width // 128
    best = max(d for d in range(1, n + 1) if n % d == 0 and d * 128 <= limit)
    return best * 128


def params():
    return pltpu.CompilerParams(vmem_limit_bytes=60 * 2**20)


def sds(*a):
    return jax.ShapeDtypeStruct(*a)


class Blocks:
    def __init__(self, rows, width, cb, parts, reverse=False, first=0):
        self.first = first
        self.grid = (width // cb, parts)
        self.cb, self.rows, self.seg = cb, rows, rows // parts
        self.at = (lambda s: parts - 1 - s) if reverse else (lambda s: s)

    def token(self, n):
        return pl.BlockSpec((self.seg, n), lambda k, s: (self.at(s), 0))

    def channel(self, n):
        return pl.BlockSpec((n, self.cb), lambda k, s: (0, k + self.first))

    def both(self, times=1, off=0):
        return pl.BlockSpec((self.seg * times, self.cb), lambda k, s: (self.at(s), k + self.first + off))

    def lead(self, n, *rest):
        return pl.BlockSpec((n, *rest), lambda k, s: (self.at(s),) + (0,) * len(rest))

    def marks(self, states):
        return pl.BlockSpec((self.seg // TC, states, self.cb), lambda k, s: (self.at(s), 0, k))

    def whole(self, shape):
        return pl.BlockSpec(shape, lambda k, s: (0,) * len(shape))


def estimate(rows, width, states, ops, size):
    return pl.CostEstimate(
        flops=ops * rows * width * states, bytes_accessed=rows * width * size, transcendentals=rows * width * states
    )


END, FORWARD, START, BACKWARD = (1152, 3), (1152, 6), (1152, 3), (2304, 24)


def end_states(s, w, b, st, u, a, bb, part, of):
    rows, width, states = s.shape[0], w.shape[1] // of, a.shape[0]
    cb = min(END[0], width)
    k = Blocks(rows, width, cb, END[1], first=part * (width // cb))
    return pl.pallas_call(
        end_kernel,
        grid=k.grid,
        in_specs=[k.token(s.shape[1]), k.channel(w.shape[0]), k.channel(1), k.token(1), k.both(), k.channel(states), k.lead(k.seg, states, 128)],
        out_specs=pl.BlockSpec((2 * states, cb), lambda i, j: (0, i)),
        out_shape=sds((2 * states, width), BF16),
        scratch_shapes=[pltpu.VMEM((k.seg, k.cb), F32)] * 2 + [pltpu.VMEM((states + 8, k.cb), F32)],
        compiler_params=params(),
        cost_estimate=estimate(rows, width, states, 6, 8),
        name="end_states",
    )(s, w, b, st, u, a, bb)


def forward_scan(s, w, b, st, u, z, a, skip, bb, cm, h0):
    rows, width, states = s.shape[0], w.shape[1], a.shape[0]
    k = Blocks(rows, width, *FORWARD)
    return pl.pallas_call(
        forward_kernel,
        grid=k.grid,
        in_specs=[k.token(s.shape[1]), k.channel(w.shape[0]), k.channel(1), k.token(1), k.both(), k.both(), k.channel(states), k.channel(1),
                  k.lead(k.seg, states, 128), k.lead(k.seg // TC, *cm.shape[1:]), k.channel(states)],
        out_specs=[k.both(), k.both(), k.both(states), k.marks(states)],
        out_shape=[sds((rows, width), BF16), sds((rows, width), BF16), sds((rows * states, width), BF16), sds((rows // TC, states, width), BF16)],
        scratch_shapes=[pltpu.VMEM((k.seg, k.cb), F32)] * 3 + [pltpu.VMEM((states, k.cb), F32)],
        compiler_params=params(),
        cost_estimate=estimate(rows, width, states, 9, 44),
        name="forward_scan",
    )(s, w, b, st, u, z, a, skip, bb, cm, h0)


def start_grads(s, w, b, st, dy, a, cb_wide, part, of):
    rows, width, states = s.shape[0], w.shape[1] // of, a.shape[0]
    cb = min(START[0], width)
    k = Blocks(rows, width, cb, START[1], reverse=True, first=part * (width // cb))
    return pl.pallas_call(
        start_kernel,
        grid=k.grid,
        in_specs=[k.token(s.shape[1]), k.channel(w.shape[0]), k.channel(1), k.token(1), k.both(), k.channel(states), k.lead(k.seg, states, 128)],
        out_specs=pl.BlockSpec((states, cb), lambda i, j: (0, i)),
        out_shape=sds((states, width), BF16),
        scratch_shapes=[pltpu.VMEM((k.seg, k.cb), F32), pltpu.VMEM((states, k.cb), F32)],
        compiler_params=params(),
        cost_estimate=estimate(rows, width, states, 6, 8),
        name="start_grads",
    )(s, w, b, st, dy, a, cb_wide)


def backward_scan(s, w, b, st, u, dy, a, skip, cb, bm, om, hs, ck, g0):
    rows, width, states = s.shape[0], w.shape[1], a.shape[0]
    k = Blocks(rows, width, *BACKWARD, reverse=True)
    chunks = rows // TC
    return pl.pallas_call(
        backward_kernel,
        grid=k.grid,
        in_specs=[k.token(s.shape[1]), k.channel(w.shape[0]), k.channel(1), k.token(1), k.both(), k.both(), k.channel(states), k.channel(1),
                  k.lead(k.seg, states, 128), k.lead(k.seg // TC, *bm.shape[1:]), k.whole(om.shape), k.both(states), k.marks(states), k.channel(states)],
        out_specs=[k.both(), k.both(), k.channel(states), k.channel(1), k.channel(1), k.whole((rows, 128)), k.whole((chunks, 8, TC * states))],
        out_shape=[sds((rows, width), BF16), sds((rows, width), F32), sds((states, width), F32), sds((1, width), F32), sds((1, width), F32),
                   sds((rows, 128), BF16), sds((chunks, 8, TC * states), F32)],
        scratch_shapes=[pltpu.VMEM((k.seg, k.cb), F32)] * 5
        + [pltpu.VMEM((TC * states, k.cb), BF16)] * 4
        + [pltpu.VMEM((states, k.cb), F32), pltpu.VMEM((rows, states, 128), F32), pltpu.VMEM((chunks, TC, TC * states), F32)],
        compiler_params=params(),
        cost_estimate=estimate(rows, width, states, 18, 44),
        name="backward_scan",
    )(s, w, b, st, u, dy, a, skip, cb, bm, om, hs, ck, g0)


def spread(coeff):
    return jnp.broadcast_to(coeff[:, :, None], (*coeff.shape, 128))


def block_rows(coeff):
    rows, states = coeff.shape
    mask = jnp.arange(TC * states)[None, None] // states == jnp.arange(TC)[None, :, None]
    return jnp.where(mask, coeff.reshape(rows // TC, 1, TC * states), 0.0).astype(BF16)


epsilon = 1e-05
HALVES = 2


def shifted(array, axis, by):
    length = lax.axis_size(axis)
    pairs = [(i, i + by) for i in range(length) if 0 <= i + by < length]
    return lax.ppermute(array, axis, pairs)


def entering(came, sums, rate2):
    state, decay = jnp.zeros_like(rate2), jnp.zeros((1, rate2.shape[1]), F32)
    for end, total in zip(came, sums):
        state = state + jnp.exp2(rate2 * decay) * end.astype(F32)
        decay = decay + total
    return state


def product_back(left, right):
    return lax.dot_general(left, right, (((1,), (1,)), ((), ())), preferred_element_type=F32)


def contract(left, right):
    return lax.dot_general(left, right, (((0,), (0,)), ((), ())), preferred_element_type=F32)


def silu_slope(values):
    sigma = jax.nn.sigmoid(values)
    return sigma * (1.0 + values * (1.0 - sigma))


def inverse_rms(values):
    return lax.rsqrt(jnp.mean(values * values, axis=-1, keepdims=True) + epsilon)


def paired_rows(rows, devices):
    r, d = rows.shape
    split = rows.reshape(r // 2, 2, devices, d // devices)
    return split.transpose(0, 2, 1, 3).reshape(r // 2, 2 * d)


def single_rows(rows, devices):
    r, d = rows.shape
    split = rows.reshape(r, devices, 2, d // (2 * devices))
    return split.transpose(0, 2, 1, 3).reshape(2 * r, d // 2)


def stacked(parts):
    whole = jnp.concatenate([p.astype(BF16) for p in parts], axis=0)
    return jnp.pad(whole, ((0, -whole.shape[0] % 16), (0, 0)))


def expert_part(parts):
    n, here = lax.axis_size("expert"), lax.axis_index("expert")
    part = lambda k: lax.dynamic_index_in_dim(parts, jnp.mod(here + k, n), 0, keepdims=False)
    total = part(0).astype(F32)
    for k in range(1, n):
        total = total + turned(part(k), k).astype(F32)
    return total.astype(BF16)


def turned(x, k):
    n = lax.axis_size("expert")
    return lax.ppermute(x, "expert", [(i, (i + k) % n) for i in range(n)]) if k else x


def in_order(came):
    n, here = lax.axis_size("expert"), lax.axis_index("expert")
    return lax.dynamic_slice_in_dim(jnp.stack(came[::-1] * 2), n - 1 - here, n, 0)


def expert_sum(*arrays):
    n = lax.axis_size("expert")
    split = [x.reshape(n, x.shape[0] // n, x.shape[1]) for x in arrays]
    padded = [jnp.pad(x, ((0, 0), (0, -x.shape[1] % 8), (0, 0))) for x in split]
    total = expert_part(jnp.concatenate(padded, axis=1))
    every = in_order([turned(total, k) for k in range(n)])
    out, at = [], 0
    for x, p in zip(split, padded):
        out.append(every[:, at : at + x.shape[1]].reshape(n * x.shape[1], x.shape[2]))
        at += p.shape[1]
    return out


def shares(rows, devices):
    r, columns = rows.shape
    return rows.reshape(r, devices, columns // devices).transpose(1, 0, 2).reshape(devices, -1)


def halved(grads, devices):
    rows, columns = grads.shape
    split = grads.reshape(devices // 2, 2, rows // devices, columns)
    return split.transpose(1, 0, 2, 3).reshape(devices, rows // devices, columns)


def cut(whole, counts):
    out, at = [], 0
    for n in counts:
        out.append(whole[at : at + n])
        at += n
    return out


def body(
    tokens, cotangent, routes, starts, input_proj, conv_kernel, conv_bias, select_proj, step_proj,
    step_bias, decay_log, skip_gain, output_proj, norm_gain, ffn_gain, router, expert_up, expert_down,
):
    devices = lax.axis_size("dp")
    groups = lax.axis_size("expert")
    rows, model = tokens.shape
    taps, rank, states = conv_kernel.shape[0], step_proj.shape[0], decay_log.shape[1]
    capacity = 2 * rows // groups
    w_input = lax.all_gather(input_proj, "dp", axis=1, tiled=True)
    small = stacked(
        [
            select_proj.T, step_proj, decay_log.T, conv_kernel, conv_bias[None], step_bias[None], skip_gain[None],
            paired_rows(jnp.concatenate([norm_gain[None], ffn_gain[None], router.T], 0), 1),
        ]
    )
    counts = (select_proj.shape[1], rank, states, taps, 1, 1, 1, (groups + 2) // 2)
    w_select, w_step, w_decay, w_conv, b_conv, bias2, skip2, singles = cut(
        lax.all_gather(small, "dp", axis=1, tiled=True), counts
    )
    singles = single_rows(singles, devices).astype(F32)
    norm_f, ffn_f, router_f = singles[0], singles[1], singles[2:]
    w_output = lax.all_gather(output_proj, "dp", axis=0, tiled=True)
    w_up = lax.all_gather(expert_up[0], "dp", axis=1, tiled=True)
    w_down = lax.all_gather(expert_down[0], "dp", axis=0, tiled=True)
    width = w_select.shape[1]
    conv_f = w_conv.astype(F32)

    route = routes[:, 0]
    chosen = (route[:, None] == jnp.arange(groups, dtype=jnp.int32)[None, :]).astype(F32)
    before = (jnp.arange(rows)[:, None] > jnp.arange(rows)[None, :]).astype(BF16)
    ranks = dot(before, chosen.astype(BF16))
    slot = jnp.sum(ranks * chosen, axis=1).astype(jnp.int32)
    assert groups & (groups - 1) == 0
    distance = jnp.bitwise_xor(route, lax.axis_index("expert"))
    target = jnp.where(slot < capacity, distance * capacity + slot, groups * capacity)
    place = (jnp.arange(groups * capacity)[:, None] == target[None, :]).astype(BF16)

    hidden_in = tokens.astype(F32)
    norm_r = inverse_rms(hidden_in)
    norm_own = (hidden_in * norm_r * norm_f).astype(BF16)
    flag = starts.astype(F32)
    same = 1.0 - flag
    valid = [jnp.ones((rows,), F32)]
    for lag in range(1, taps):
        moved = jnp.concatenate([jnp.ones((lag - 1,), F32), same[: rows - lag + 1]])
        valid.append(valid[-1] * moved)
    edge = [jnp.ones((), F32)]
    for lag in range(1, taps - 1):
        edge.append(edge[-1] * same[rows - lag])
    edge_keep = jnp.stack(edge[::-1])[:, None]
    tail = (norm_own[rows - taps + 1 :].astype(F32) * edge_keep).astype(BF16)
    borrowed = shifted(tail, "expert", 1)
    norm_low = jnp.concatenate([jnp.zeros((PAD - taps + 1, model), BF16), borrowed, norm_own], 0)
    ok = jnp.pad(jnp.stack(valid, 1), ((PAD, PAD), (0, 0)))
    norm_low, ok = lax.optimization_barrier((norm_low, ok))
    conv_in = dot(norm_low, w_input[:, :width]).astype(BF16)
    conv_sum = jnp.broadcast_to(b_conv.astype(F32), (rows, width))
    for lag in range(taps):
        conv_sum = conv_sum + valid[lag][:, None] * conv_f[taps - 1 - lag] * conv_in[PAD - lag : PAD - lag + rows].astype(F32)
    inner_low = jax.nn.silu(conv_sum).astype(BF16)
    slope_low = silu_slope(conv_sum).astype(BF16)
    selected = product_back(inner_low, w_select)
    step_low = selected[:, :rank].astype(BF16)
    b_coeff = selected[:, rank : rank + states]
    c_coeff = selected[:, rank + states :]
    rate2 = -jnp.exp(w_decay.astype(F32)) * LOG2E
    st = flag[:, None]
    b_wide, c_wide = spread(b_coeff), spread(c_coeff)
    b_block, c_block = block_rows(b_coeff), block_rows(c_coeff)
    one_block = (jnp.arange(TC * states)[None] // states == jnp.arange(TC)[:, None]).astype(BF16)
    hops = range(1, groups)
    own_sums, start_state = [], []
    for part in range(HALVES):
        rate_part = rate2[:, part * width // HALVES : (part + 1) * width // HALVES]
        end = end_states(step_low, w_step, bias2, st, inner_low, rate2, b_wide, part, HALVES)
        came = [shifted(end, "expert", hop) for hop in hops]
        total = lambda x: x[:1].astype(F32) + x[1:2].astype(F32)
        own_sums.append(end[states : states + 8])
        start_state.append(entering([c[:states] for c in came], [total(c[states:]) for c in came], rate_part))
    start_state = jnp.concatenate(start_state, 1)
    norm_late, _ = lax.optimization_barrier((norm_own, end))
    gate_in = dot(norm_late, w_input[:, width:]).astype(BF16)
    gated_low, scanned, history, marks = forward_scan(
        step_low, w_step, bias2, st, inner_low, gate_in, rate2, skip2, b_wide, c_block, start_state
    )
    hidden_one = hidden_in + dot(gated_low, w_output)

    r2 = inverse_rms(hidden_one)
    norm_two = hidden_one * r2 * ffn_f
    logits = lax.dot_general(
        norm_two, router_f, (((1,), (1,)), ((), ())),
        precision=lax.Precision.HIGHEST, preferred_element_type=F32,
    )
    probs = jax.nn.softmax(logits, axis=-1)
    gate_value = jnp.sum(probs * chosen, axis=-1)
    grad_out = cotangent.astype(F32)
    grad_picked = (gate_value[:, None] * grad_out).astype(BF16)

    def swapped(x, k):
        return lax.ppermute(x, "expert", [(i, i ^ k) for i in range(groups)]) if k else x

    places = [place[k * capacity : (k + 1) * capacity] for k in range(groups)]
    norm_two_low = norm_two.astype(BF16)
    arrived, grad_arrived = [None] * groups, [None] * groups
    far_first = list(range(groups - 1, 0, -1))
    for k in far_first + [0]:
        arrived[k] = swapped(dot(places[k], norm_two_low).astype(BF16), k)
    for k in far_first + [0]:
        sent = dot(places[k], grad_picked).astype(BF16)
        if k:
            sent, arrived[k] = lax.optimization_barrier((sent, arrived[k]))
        grad_arrived[k] = swapped(sent, k)
    up_low, grad_pre, outs, ins = ([None] * groups for _ in range(4))
    for k in [0] + far_first:
        up_pre = dot(arrived[k], w_up)
        act, gelu_back = jax.vjp(jax.nn.gelu, up_pre)
        up_low[k] = act.astype(BF16)
        outs[k] = dot(up_low[k], w_down).astype(BF16)
        grad_pre[k] = gelu_back(product_back(grad_arrived[k], w_down))[0].astype(BF16)
        ins[k] = product_back(grad_pre[k], w_up).astype(BF16)
    returned = [None] * groups
    grad_sent = [None] * groups
    for k in far_first + [0]:
        returned[k] = swapped(outs[k], k)
    for k in far_first + [0]:
        grad_sent[k] = swapped(ins[k], k)
    returned, grad_sent = jnp.concatenate(returned), jnp.concatenate(grad_sent)
    up_low, grad_pre, arrived, grad_arrived, _, _ = lax.optimization_barrier(
        (up_low, grad_pre, arrived, grad_arrived, outs, ins)
    )
    grad_up = contract(jnp.concatenate(grad_pre), jnp.concatenate(arrived)).astype(BF16)
    grad_down = contract(jnp.concatenate(up_low), jnp.concatenate(grad_arrived)).astype(BF16)
    grad_sent, grad_up, grad_down, c_wide, b_block = lax.optimization_barrier(
        (grad_sent, grad_up, grad_down, c_wide, b_block)
    )
    sum_up = lax.psum_scatter(grad_up, "dp", scatter_dimension=0, tiled=True)
    sum_down = lax.psum_scatter(grad_down, "dp", scatter_dimension=0, tiled=True)

    picked = contract(place, returned)
    output = (hidden_one + gate_value[:, None] * picked).astype(BF16)
    grad_gate = jnp.sum(grad_out * picked, axis=1)
    grad_logits = probs * (grad_gate[:, None] * chosen - (grad_gate * gate_value)[:, None])
    grad_router = lax.dot_general(
        grad_logits, norm_two, (((0,), (0,)), ((), ())),
        precision=lax.Precision.HIGHEST, preferred_element_type=F32,
    )
    grad_norm_two = contract(place, grad_sent) + lax.dot_general(
        grad_logits, router_f, (((1,), (0,)), ((), ())),
        precision=lax.Precision.HIGHEST, preferred_element_type=F32,
    )
    grad_ffn_gain = jnp.sum(grad_norm_two * hidden_one * r2, axis=0)
    scaled = ffn_f * grad_norm_two
    grad_hidden = (
        grad_out
        + r2 * scaled
        - hidden_one * (r2 * r2 * r2) * jnp.mean(hidden_one * scaled, axis=-1, keepdims=True)
    )

    grad_mixer = grad_hidden.astype(BF16)
    grad_output_w = contract(gated_low, grad_mixer)
    grad_gated = product_back(grad_mixer, w_output)
    gate_f = gate_in.astype(F32)
    sigma = jax.nn.sigmoid(gate_f)
    grad_scanned = grad_gated * (gate_f * sigma)
    grad_gate_in = (grad_gated * scanned.astype(F32) * (sigma * (1.0 + gate_f * (1.0 - sigma)))).astype(BF16)
    grad_scanned, sum_up = lax.optimization_barrier((grad_scanned, sum_up))
    later_grad = []
    for part in range(HALVES):
        rate_part = rate2[:, part * width // HALVES : (part + 1) * width // HALVES]
        start = start_grads(step_low, w_step, bias2, st, grad_scanned, rate2, c_wide, part, HALVES)
        start = jnp.concatenate([start, own_sums[part]])
        came = [shifted(start, "expert", -hop) for hop in hops]
        later_grad.append(entering([c[:states] for c in came], [total(c[states:]) for c in came], rate_part))
    grad_input_z = halved(contract(grad_gate_in, norm_own).astype(BF16), devices).reshape(width, model)
    grad_norm_z = product_back(grad_gate_in, w_input[:, width:])
    later_grad, sum_down, grad_output_w, grad_input_z, grad_norm_z = lax.optimization_barrier(
        (jnp.concatenate(later_grad, 1), sum_down, grad_output_w.astype(BF16), grad_input_z, grad_norm_z)
    )
    sum_output = lax.psum_scatter(grad_output_w, "dp", scatter_dimension=0, tiled=True)
    sum_input_z = lax.psum_scatter(grad_input_z, "dp", scatter_dimension=0, tiled=True)
    grad_pre_step, grad_inner, grad_decay_t, grad_skip, grad_step_bias, grad_b, grad_c = backward_scan(
        step_low, w_step, bias2, st, inner_low, grad_scanned, rate2, skip2,
        c_wide, b_block, one_block, history, marks, later_grad,
    )
    grad_pre_step, sum_output, sum_input_z = lax.optimization_barrier((grad_pre_step, sum_output, sum_input_z))
    grad_step_w = contract(step_low, grad_pre_step)
    grad_step_low = product_back(grad_pre_step, w_step).astype(BF16)
    grad_selected = jnp.concatenate(
        [grad_step_low, grad_b[:, :states], grad_c[:, 0].reshape(rows, states).astype(BF16)], 1
    )
    grad_select_w = contract(grad_selected, inner_low)
    summed = stacked(
        [
            grad_select_w, grad_step_w, grad_decay_t, grad_step_bias, grad_skip,
            paired_rows(jnp.concatenate([grad_ffn_gain[None], grad_ffn_gain[None], grad_router], 0), devices),
        ]
    )
    share, norm_share = width // devices, model // devices
    summed_shape = (summed.shape[0], share)
    summed = shares(summed, devices)
    grad_inner, summed = lax.optimization_barrier((grad_inner, summed))
    grad_conv_in, grad_kernel, grad_conv_b = conv_back(
        conv_in, grad_inner, slope_low, grad_selected, w_select, w_conv, ok
    )
    grad_norm_x = product_back(grad_conv_in, w_input[:, :width])
    returned_edge = shifted(grad_norm_x[PAD - taps + 1 : PAD], "expert", -1) * edge_keep
    grad_norm_one = grad_norm_x[PAD:] + grad_norm_z + jnp.pad(returned_edge, ((rows - taps + 1, 0), (0, 0)))
    grad_norm_gain = jnp.sum(grad_norm_one * hidden_in * norm_r, axis=0, keepdims=True)
    grad_input_x = contract(grad_conv_in, norm_low).astype(BF16)
    tiny = jnp.concatenate([shares(jnp.concatenate([grad_kernel, grad_conv_b]), devices), shares(grad_norm_gain, devices)], 1)
    rest = jnp.concatenate([summed, tiny.astype(BF16)], 1)
    more = -(-rest.shape[1] // model)
    more += -(more + share) % (8 * groups)
    rest = jnp.pad(rest, ((0, 0), (0, more * model - rest.shape[1]))).reshape(devices, more, model)
    pieces = []
    for d in range(devices):
        block = d % (devices // 2) * 2 + d // (devices // 2)
        pieces += [grad_input_x[block * share : (block + 1) * share], rest[d]]
    packed = jnp.concatenate(pieces)
    packed, sum_output, sum_input_z = lax.optimization_barrier((packed, sum_output, sum_input_z))
    packed = lax.psum_scatter(packed, "dp", scatter_dimension=0, tiled=True)
    sum_output, sum_input_z = expert_sum(sum_output, sum_input_z)
    scaled_one = norm_f * grad_norm_one
    grad_tokens = (
        grad_hidden
        + norm_r * scaled_one
        - hidden_in * (norm_r * norm_r * norm_r) * jnp.mean(hidden_in * scaled_one, axis=-1, keepdims=True)
    ).astype(BF16)
    packed, sum_output, sum_input_z, grad_tokens = lax.optimization_barrier((packed, sum_output, sum_input_z, grad_tokens))
    (packed,) = expert_sum(packed)
    sum_input_x, tiny = packed[:share], packed[share:].astype(F32).reshape(-1)
    summed = tiny[: summed_shape[0] * share].reshape(summed_shape)
    tiny = tiny[summed_shape[0] * share :]
    half = devices // 2
    low = lax.axis_index("dp") < half
    other = lax.ppermute(
        jnp.where(low, sum_input_z, sum_input_x), "dp", [(i, (i + half) % devices) for i in range(devices)]
    )
    own_half = jnp.where(low, sum_input_x, sum_input_z)
    sum_input = jnp.concatenate([jnp.where(low, own_half, other), jnp.where(low, other, own_half)])
    sum_kernel = tiny[: taps * share].reshape(taps, share)
    sum_conv_b = tiny[taps * share : (taps + 1) * share]
    sum_norm = tiny[(taps + 1) * share : (taps + 1) * share + norm_share]
    sum_select, sum_step, sum_decay, sum_step_b, sum_skip, singles = cut(
        summed, (w_select.shape[0], rank, states, 1, 1, (groups + 2) // 2)
    )
    singles = single_rows(singles, 1)
    sum_input, sum_output = sum_input.astype(F32).T, sum_output.astype(F32)
    return (
        output, grad_tokens, sum_input, sum_kernel, sum_conv_b, sum_select.T, sum_step, sum_step_b[0],
        sum_decay.T, sum_skip[0], sum_output, sum_norm, singles[1], singles[2:].T,
        sum_up.astype(F32).T[None], sum_down.astype(F32)[None],
    )


def solution(mesh):
    placed = (
        P(("dp", "expert"), None),
        P(("dp", "expert"), None),
        P(("dp", "expert"), None),
        P(("dp", "expert")),
        P(None, "dp"),
        P(None, "dp"),
        P("dp"),
        P("dp", None),
        P(None, "dp"),
        P("dp"),
        P("dp", None),
        P("dp"),
        P("dp", None),
        P("dp"),
        P("dp"),
        P("dp", None),
        P("expert", None, "dp"),
        P("expert", "dp", None),
    )
    return jax.shard_map(
        body,
        mesh=mesh,
        in_specs=placed,
        out_specs=(
            P(("dp", "expert"), None),
            P(("dp", "expert"), None),
            P(None, "dp"),
            P(None, "dp"),
            P("dp"),
            P("dp", None),
            P(None, "dp"),
            P("dp"),
            P("dp", None),
            P("dp"),
            P("dp", None),
            P("dp"),
            P("dp"),
            P("dp", None),
            P("expert", None, "dp"),
            P("expert", "dp", None),
        ),
        check_vma=False,
    )
```
